128 devices in a mesh: fsdp: 8 (over y, core), tp: 16 (over z, x).
Axes of the slice: x: 4, y: 4, z: 4, core: 2. Of those that a mesh axis runs over, the one named last changes fastest.
Arguments:
- qkv_weight: bfloat16 [16384, 18432], P('fsdp', 'tp'), may hold values from -5 to 5
- placement: int32 [144], replicated, may hold values from 0 to 15, as said below
Outputs:
- packed_codes: bfloat16 [16, 16, 128, 16384], P('tp', None, None, 'fsdp')
- packed_peaks: float32 [16, 16, 128], P('tp')
The draws below stay inside these ranges and needn't reach their ends.
Inputs may be any that keep to these rules, and one draw needn't show every extreme that they name: `placement`: heads t * 9 to (t + 1) * 9 - 1 form block t. No owner takes more than 1 head of one block, and one owner takes exactly 1 head of every block, so 16 heads in all.
All inputs are finite; a program needn't handle non-finite values. Where the reference program divides by a largest or mean magnitude, that divisor is 1e-20 or more.
Results may differ from the reference program's by a relative error of at most 0.0075.
Values may be sent and summed in bfloat16 or wider, within the bound.
No kernel may reach another device: no remote copies, remote signals or barrier semaphores. Data moves between devices by JAX's collectives and lax.ppermute only.
A program may use at most 192 MiB of HBM per device.

```python
import math
import jax
import jax.numpy as jnp
from jax import lax

D = 16384
HEAD_DIM = 128
HAD = 128
QKV = 18432
HEADS_DEV = 9
SEND = 1
CAP = 16
N_TP = 16


def draw_qkv_weight(key, part):
    key = jax.random.fold_in(key, 5)
    key_base, key_rows, key_cols = jax.random.split(key, 3)
    col_scale = jnp.exp(jax.random.uniform(key_cols, (1, QKV), jnp.float32, 0.0, math.log(10.0)))
    row_scale = jnp.exp(jax.random.uniform(key_rows, (D, 1), jnp.float32, 0.0, math.log(10.0)))
    base_vals = jnp.clip(jax.random.normal(key_base, (D, QKV), jnp.float32), -4.0, 4.0)
    return (base_vals * row_scale * col_scale / HAD).astype(jnp.bfloat16)


def draw_placement(key, part):
    key = jax.random.fold_in(key, 11)
    special = jax.random.randint(jax.random.fold_in(key, 0), (), 0, N_TP)

    def one_block(block_id):
        key_block = jax.random.fold_in(key, block_id + 1)
        key_slots, key_shuffle = jax.random.split(key_block)
        others = jax.random.permutation(key_slots, (N_TP - 1) * SEND)
        other_owner = (special + 1 + others // SEND) % N_TP
        chosen = jnp.concatenate([jnp.full((SEND,), special, jnp.int32), other_owner[:HEADS_DEV - SEND].astype(jnp.int32)])
        shuffle = jax.random.permutation(key_shuffle, HEADS_DEV)
        return chosen[shuffle]
    return jax.vmap(one_block)(jnp.arange(N_TP)).reshape(-1).astype(jnp.int32)


def setup_inputs(seed: int = 0) -> dict:
    seeds = jax.random.split(jax.random.key(seed), 3)
    qkv_weight = draw_qkv_weight(jax.random.fold_in(seeds[2], 71), 0)
    placement = draw_placement(jax.random.fold_in(seeds[2], 71), 0)
    return dict(qkv_weight=qkv_weight, placement=placement)


def hadamard_table(order):
    matrix = jnp.ones((1, 1), jnp.float32)
    while matrix.shape[0] < order:
        upper = jnp.concatenate([matrix, matrix], axis=1)
        lower = jnp.concatenate([matrix, -matrix], axis=1)
        matrix = jnp.concatenate([upper, lower], axis=0)
    return matrix


def rotate_head(columns):
    signs_f = hadamard_table(HAD)
    grid_view = columns.reshape(HAD, HAD, HEAD_DIM)
    half_turn = jnp.einsum('ia,abc->cib', signs_f, grid_view, precision=lax.Precision.HIGHEST)
    second = jnp.einsum('cib,jb->cij', half_turn, signs_f, precision=lax.Precision.HIGHEST)
    rotated = second * (1.0 / HAD)
    peak_vals = jnp.max(jnp.abs(rotated), axis=(1, 2))
    code_rows = (rotated / (peak_vals + 1e-6)[:, None, None]).astype(jnp.bfloat16)
    return code_rows.reshape(HEAD_DIM, D), peak_vals


def reference(qkv_weight, placement):
    head_count = placement.shape[0]
    head_order = jnp.arange(head_count, dtype=jnp.int32)
    same_owner = placement[None, :] == placement[:, None]
    head_rank = jnp.sum((same_owner & (head_order[None, :] < head_order[:, None])).astype(jnp.int32), axis=1)
    slot_ids = jnp.arange(N_TP * CAP, dtype=jnp.int32)
    hits = (placement[None, :] == (slot_ids // CAP)[:, None]) & (head_rank[None, :] == (slot_ids % CAP)[:, None])
    source = jnp.sum(hits.astype(jnp.int32) * head_order[None, :], axis=1).astype(jnp.int32)
    filled = jnp.any(hits, axis=1)
    stacked = qkv_weight.reshape(D, head_count, HEAD_DIM)

    def one_slot(item_pair):
        head_id, is_live = item_pair
        columns = lax.dynamic_index_in_dim(stacked, head_id, 1, keepdims=False).astype(jnp.float32)

        def live_case():
            return rotate_head(columns)

        def empty_case():
            return jnp.zeros((HEAD_DIM, D), jnp.bfloat16), jnp.zeros((HEAD_DIM,), jnp.float32)

        return lax.cond(is_live, live_case, empty_case)

    code_rows, peak_vals = lax.map(one_slot, (source, filled))
    return code_rows.reshape(N_TP, CAP, HEAD_DIM, D), peak_vals.reshape(N_TP, CAP, HEAD_DIM)
```

```python
import functools

import numpy as np
import jax
import jax.numpy as jnp
from jax import lax
from jax.experimental import pallas as pl
from jax.experimental.pallas import tpu as pltpu
from jax.sharding import PartitionSpec as P

HEAD_DIM = 128
HAD = 128
CHUNKS = 2
VMEM_BYTES = 48 * 1024 * 1024


def hadamard_table(order):
    matrix = np.ones((1, 1), np.float32)
    while matrix.shape[0] < order:
        matrix = np.block([[matrix, matrix], [matrix, -matrix]])
    return matrix


def butterfly(values):
    values = list(values)
    half = 1
    while half < len(values):
        for low in range(len(values)):
            if not low & half:
                first, second = values[low], values[low + half]
                values[low], values[low + half] = first + second, first - second
        half *= 2
    return values


def local_turn_kernel(rows_a, groups, weight_ref, signs_ref, *refs):
    out_refs, turned = refs[:-1], refs[-1]
    for a in range(rows_a):
        block = weight_ref[a * HAD : (a + 1) * HAD, :]
        turned[a] = lax.dot_general(
            block, signs_ref[...], (((0,), (0,)), ((), ())), preferred_element_type=jnp.float32
        )
    chans = HEAD_DIM // len(out_refs)
    each = rows_a // groups
    for chunk, out_ref in enumerate(out_refs):
        for low in range(0, chans, 16):
            start = chunk * chans + low
            outs = butterfly([turned[a, start : start + 16, :] for a in range(rows_a)])
            for a in range(rows_a):
                out_ref[a // each, 0, a % each, low : low + 16, :] = (outs[a] * (1.0 / HAD)).astype(jnp.bfloat16)


def cross_turn_kernel(in_ref, out_ref, peak_ref):
    groups, heads, each, chans, _ = in_ref.shape
    for head in range(heads):
        for low in range(0, chans, 16):
            rows = slice(low, low + 16)
            largest = None
            for e in range(each):
                outs = butterfly([in_ref[g, head, e, rows, :].astype(jnp.float32) for g in range(groups)])
                for g in range(groups):
                    out_ref[g, head, e, rows, :] = outs[g].astype(jnp.bfloat16)
                    magnitude = jnp.abs(outs[g])
                    largest = magnitude if largest is None else jnp.maximum(largest, magnitude)
            peak_ref[head, rows, :] = largest


def spread_kernel(head_ref, in_ref, out_ref, sems):
    copies = []
    for owner in range(out_ref.shape[0]):
        copies.append(pltpu.make_async_copy(in_ref.at[:, head_ref[owner]], out_ref.at[owner], sems.at[owner]))
    for copy in copies:
        copy.start()
    for copy in copies:
        copy.wait()


def pack_kernel(source_ref, live_ref, scale_ref, *refs):
    in_refs, out_ref = refs[:-1], refs[-1]
    slot = pl.program_id(0)
    _, groups, each, chans, _ = in_refs[0].shape

    @pl.when(live_ref[slot] != 0)
    def _():
        for chunk, in_ref in enumerate(in_refs):
            rows = slice(chunk * chans, (chunk + 1) * chans)
            scale = scale_ref[0, rows, :]
            for g in range(groups):
                for e in range(each):
                    lane = (g * each + e) * HAD
                    out_ref[0, 0, rows, lane : lane + HAD] = (
                        in_ref[0, g, e].astype(jnp.float32) * scale
                    ).astype(jnp.bfloat16)

    @pl.when(live_ref[slot] == 0)
    def _():
        out_ref[...] = jnp.zeros_like(out_ref)


def per_device(qkv_weight, placement):
    rows_local, cols_local = qkv_weight.shape
    heads = cols_local // HEAD_DIM
    owners = lax.axis_size("tp")
    groups = lax.axis_size("fsdp")
    rows_a = rows_local // HAD
    each = rows_a // groups
    chans = HEAD_DIM // CHUNKS
    params = pltpu.CompilerParams(vmem_limit_bytes=VMEM_BYTES)
    any_spec = pl.BlockSpec(memory_space=pl.ANY)

    me = lax.axis_index("tp")
    table = placement.reshape(owners, heads)
    my_owners = lax.dynamic_slice_in_dim(table, me, 1, axis=0)[0]
    head_ids = jnp.arange(heads, dtype=jnp.int32)
    owner_ids = jnp.arange(owners, dtype=jnp.int32)
    head_for = jnp.sum(jnp.where(my_owners[None, :] == owner_ids[:, None], head_ids[None, :], 0), axis=1)
    mine = table == me
    has = jnp.any(mine, axis=1)
    rank = jnp.cumsum(has.astype(jnp.int32)) - 1
    count = jnp.sum(has.astype(jnp.int32))
    takes = has[None, :] & (rank[None, :] == owner_ids[:, None])
    source = jnp.sum(jnp.where(takes, owner_ids[None, :], 0), axis=1)
    live = (owner_ids < count).astype(jnp.int32)
    picked = (takes[:, :, None] & mine[None]).reshape(owners, owners * heads)

    signs = jnp.asarray(hadamard_table(HAD), jnp.bfloat16)
    piece = (groups, heads, each, chans, HAD)
    sent = pl.pallas_call(
        functools.partial(local_turn_kernel, rows_a, groups),
        grid=(heads,),
        in_specs=[
            pl.BlockSpec((rows_local, HEAD_DIM), lambda h: (0, h)),
            pl.BlockSpec((HAD, HAD), lambda h: (0, 0)),
        ],
        out_specs=[pl.BlockSpec((groups, 1, each, chans, HAD), lambda h: (0, h, 0, 0, 0))] * CHUNKS,
        out_shape=[jax.ShapeDtypeStruct(piece, jnp.bfloat16)] * CHUNKS,
        scratch_shapes=[pltpu.VMEM((rows_a, HEAD_DIM, HAD), jnp.float32)],
        compiler_params=params,
        name="local_turn",
    )(qkv_weight, signs)

    step = 3 if heads % 3 == 0 else 1
    arrived, peaks = [], []
    previous = None
    for chunk in range(CHUNKS):
        block = sent[chunk]
        if previous is not None:
            block, previous = lax.optimization_barrier((block, previous))
        received = lax.all_to_all(block, "fsdp", split_axis=0, concat_axis=0, tiled=True)
        previous = received
        turned, partial_peak = pl.pallas_call(
            cross_turn_kernel,
            grid=(heads // step,),
            in_specs=[pl.BlockSpec((groups, step, each, chans, HAD), lambda h: (0, h, 0, 0, 0))],
            out_specs=[
                pl.BlockSpec((groups, step, each, chans, HAD), lambda h: (0, h, 0, 0, 0)),
                pl.BlockSpec((step, chans, HAD), lambda h: (h, 0, 0)),
            ],
            out_shape=[
                jax.ShapeDtypeStruct(piece, jnp.bfloat16),
                jax.ShapeDtypeStruct((heads, chans, HAD), jnp.float32),
            ],
            compiler_params=params,
            name="cross_turn",
        )(received)
        peaks.append(jnp.max(partial_peak, axis=2))
        returned = lax.all_to_all(turned, "fsdp", split_axis=0, concat_axis=0, tiled=True)
        spread = pl.pallas_call(
            spread_kernel,
            grid_spec=pltpu.PrefetchScalarGridSpec(
                num_scalar_prefetch=1,
                grid=(1,),
                in_specs=[any_spec],
                out_specs=any_spec,
                scratch_shapes=[pltpu.SemaphoreType.DMA((owners,))],
            ),
            out_shape=jax.ShapeDtypeStruct((owners, groups, each, chans, HAD), jnp.bfloat16),
            compiler_params=params,
            name="spread",
        )(head_for, returned)
        arrived.append(lax.all_to_all(spread, "tp", split_axis=0, concat_axis=0, tiled=True))

    local_peak = jnp.concatenate(peaks, axis=1)
    all_peaks = lax.all_gather(local_peak, ("fsdp", "tp"), axis=0, tiled=False)
    all_peaks = jnp.max(all_peaks.reshape(groups, owners * heads, HEAD_DIM), axis=0)
    slot_peaks = jnp.max(jnp.where(picked[:, :, None], all_peaks[None], 0.0), axis=1)
    scale = jnp.broadcast_to((1.0 / (slot_peaks + 1e-06))[:, :, None], (owners, HEAD_DIM, HAD))

    packed = pl.pallas_call(
        pack_kernel,
        grid_spec=pltpu.PrefetchScalarGridSpec(
            num_scalar_prefetch=2,
            grid=(owners,),
            in_specs=[pl.BlockSpec((1, HEAD_DIM, HAD), lambda k, source, live: (k, 0, 0))]
            + [
                pl.BlockSpec((1, groups, each, chans, HAD), lambda k, source, live: (source[k], 0, 0, 0, 0))
            ]
            * CHUNKS,
            out_specs=pl.BlockSpec((1, 1, HEAD_DIM, rows_local), lambda k, source, live: (0, k, 0, 0)),
        ),
        out_shape=jax.ShapeDtypeStruct((1, owners, HEAD_DIM, rows_local), jnp.bfloat16),
        compiler_params=params,
        name="pack",
    )(source, live, scale, *arrived)
    return packed, slot_peaks[None]


def solution(mesh):
    in_specs = (P("fsdp", "tp"), P())
    out_specs = (P("tp", None, None, "fsdp"), P("tp", None, None))
    return jax.shard_map(
        per_device, mesh=mesh, in_specs=in_specs, out_specs=out_specs, check_vma=False
    )
```

```python
import functools

import numpy as np
import jax
import jax.numpy as jnp
from jax import lax
from jax.experimental import pallas as pl
from jax.experimental.pallas import tpu as pltpu
from jax.sharding import PartitionSpec as P

HEAD_DIM = 128
HAD = 128
CHUNKS = ((0, 32), (32, 48), (80, 48))
ORDER = (
    ("start", 0),
    ("start", 1),
    ("y_turn", 0),
    ("core_turn", 0),
    ("y_turn", 1),
    ("start", 2),
    ("core_turn", 1),
    ("spread", 0),
    ("regroup", 0),
    ("y_turn", 2),
    ("spread", 1),
    ("core_turn", 2),
    ("pack", 0),
    ("regroup", 1),
    ("spread", 2),
    ("pack", 1),
    ("regroup", 2),
    ("pack", 2),
)
TAIL = 16
VMEM_BYTES = 24 * 1024 * 1024
BOTH = ("fsdp", "tp")


def hadamard_table(order):
    matrix = np.ones((1, 1), np.float32)
    while matrix.shape[0] < order:
        matrix = np.block([[matrix, matrix], [matrix, -matrix]])
    return matrix


def butterfly(values):
    values = list(values)
    half = 1
    while half < len(values):
        for low in range(len(values)):
            if not low & half:
                first, second = values[low], values[low + half]
                values[low], values[low + half] = first + second, first - second
        half *= 2
    return values


def hop(array, flip):
    size = lax.axis_size("fsdp")
    return lax.ppermute(array, "fsdp", [(i, i ^ flip) for i in range(size)])


def ring_exchange(blocks):
    own, one, three, two_a, two_b = blocks
    two_a, two_b = hop(two_a, 2), hop(two_b, 6)
    one, three = hop(one, 2), hop(three, 6)
    return own, one, three, hop(two_a, 6), hop(two_b, 2)


def owner_table(core):
    one, two = ((1, 3), (3, 1))[core]
    table = np.zeros((4, 4), np.int32)
    for i in range(4):
        for j in range(4):
            x = (i & 1) * one ^ (j & 1) * two
            z = (i >> 1) * one ^ (j >> 1) * two
            table[i, j] = 4 * z + x
    return table


def pair_exchange(array, second):
    groups, owners = lax.axis_size("fsdp"), lax.axis_size("tp")
    members = []
    for f in range(groups):
        table = owner_table(f & 1)
        table = table if second else table.T
        members += [[f * owners + int(t) for t in row] for row in table]
    return lax.all_to_all(array, BOTH, split_axis=0, concat_axis=0, tiled=True, axis_index_groups=members)


def local_turn_kernel(rows_a, flip_ref, weight_ref, signs_ref, *refs):
    out_refs, turned = refs[:-1], refs[-1]
    columns = jnp.concatenate([weight_ref[a * HAD : (a + 1) * HAD, :].T for a in range(rows_a)], axis=0)
    turned[...] = jnp.dot(columns, signs_ref[...], preferred_element_type=jnp.float32)
    for index, (first, chans) in enumerate(CHUNKS):
        own, one, three, two_a, two_b = out_refs[5 * index : 5 * index + 5]
        for low in range(0, chans, 16):
            outs = []
            for a in range(rows_a):
                start = a * HEAD_DIM + first + low
                outs.append(turned[start : start + 16, :] * (flip_ref[a] * (1.0 / HAD)))
            outs = butterfly(outs)
            for a in range(rows_a):
                offset, e = a // 4, a % 4
                if offset == 2:
                    out_ref, e = (two_a, two_b)[e // 2], e % 2
                else:
                    out_ref = {0: own, 1: one, 3: three}[offset]
                out_ref[e * chans + low : e * chans + low + 16, :] = outs[a].astype(jnp.bfloat16)


def pieces(head, e, chans, low):
    whole = (head * 4 + e) * chans + low
    half = (head * 2 + e % 2) * chans + low
    return (0, whole), (1, whole), (3 + e // 2, half), (2, whole)


def y_turn_kernel(heads, chans, flip_in_ref, flip_out_ref, *refs):
    in_refs, out_ref = refs[:-1], refs[-1]
    for head in range(heads):
        for e in range(4):
            for low in range(0, chans, 16):
                parts = [
                    in_refs[array][row : row + 16, :].astype(jnp.float32) * flip_in_ref[o]
                    for o, (array, row) in enumerate(pieces(head, e, chans, low))
                ]
                row = (head * 4 + e) * chans + low
                for o, value in enumerate(butterfly(parts)):
                    out_ref[o, row : row + 16, :] = (value * flip_out_ref[o]).astype(jnp.bfloat16)


def join_parts(value, chans):
    return value + pltpu.roll(value, HAD - chans, 1)


def split_parts(value, chans):
    high = value.astype(jnp.bfloat16).astype(jnp.float32)
    lane = lax.broadcasted_iota(jnp.int32, value.shape, 1)
    both = jnp.where(lane < chans, high, pltpu.roll(value - high, chans, 1))
    return jnp.where(lane < 2 * chans, both, 0.0).astype(jnp.bfloat16)


def core_turn_kernel(heads, chans, sign_ref, mine_ref, other_ref, *out_refs):
    row_id = lax.broadcasted_iota(jnp.int32, (TAIL, HAD), 0)
    tail = jnp.zeros((TAIL, HAD), jnp.float32)
    sign = sign_ref[0]
    for head in range(heads):
        columns = []
        for low in range(0, chans, 16):
            largest = None
            for e in range(4):
                row = (head * 4 + e) * chans + low
                for o, (array, out_row) in enumerate(pieces(head, e, chans, low)):
                    mine = mine_ref[o, row : row + 16, :].astype(jnp.float32)
                    other = other_ref[o, row : row + 16, :].astype(jnp.float32)
                    out_refs[array][out_row : out_row + 16, :] = (other + mine * sign).astype(jnp.bfloat16)
                    magnitude = jnp.abs(mine) + jnp.abs(other)
                    largest = magnitude if largest is None else jnp.maximum(largest, magnitude)
            columns.append(largest)
        columns.append(jnp.zeros((HAD - chans, HAD), jnp.float32))
        peak = jnp.max(jnp.concatenate(columns, axis=0).T, axis=0, keepdims=True)
        tail = jnp.where(row_id == head, peak, tail)
    tail = split_parts(tail, chans)
    for out_ref in out_refs[:4]:
        out_ref[out_ref.shape[0] - TAIL :, :] = tail


def spread_kernel(heads, chans, head_ref, *refs):
    in_refs, out_ref = refs[:-1], refs[-1]
    peaks = None
    for in_ref in in_refs[:4]:
        part = join_parts(in_ref[in_ref.shape[0] - TAIL :, :].astype(jnp.float32), chans)
        peaks = part if peaks is None else jnp.maximum(peaks, part)
    row_id = lax.broadcasted_iota(jnp.int32, (TAIL, HAD), 0)
    span = 4 * chans
    half = 2 * chans
    own, one, three, two_a, two_b = in_refs
    for slot in range(16):
        head = head_ref[slot]
        whole = pl.ds(pl.multiple_of(head * span, 16), span)
        part = pl.ds(pl.multiple_of(head * half, 16), half)
        i, j = slot // 4, slot % 4
        out_ref[i, j, 0:span, :] = own[whole, :]
        out_ref[i, j, span : 2 * span, :] = one[whole, :]
        out_ref[i, j, 2 * span : 2 * span + half, :] = two_a[part, :]
        out_ref[i, j, 2 * span + half : 3 * span, :] = two_b[part, :]
        out_ref[i, j, 3 * span : 4 * span, :] = three[whole, :]
        peak = jnp.sum(jnp.where(row_id == head, peaks, 0.0), axis=0, keepdims=True)
        out_ref[i, j, 4 * span :, :] = split_parts(jnp.broadcast_to(peak, (TAIL, HAD)), chans)


def regroup_kernel(in_ref, out_ref):
    for i in range(4):
        for j in range(4):
            out_ref[j, i] = in_ref[i, j]


def pack_kernel(owners, chunk, has_past, from_ref, live_ref, place_ref, in_ref, *refs):
    first, chans = chunk
    past_ref = refs[0] if has_past else None
    peak_ref, out_ref, buffer, sems = refs[-4:]
    lane = lax.broadcasted_iota(jnp.int32, (TAIL, HAD), 1)
    depth = buffer.shape[0]
    copies = [None] * depth
    for slot in range(owners):
        part = slot % depth
        if copies[part] is not None:
            copies[part].wait()
        live = live_ref[slot] != 0
        origin = from_ref[slot]
        i, j = origin // 4, origin % 4
        tail = in_ref[i, j, 16 * chans :, :].astype(jnp.float32)
        row = jnp.where((lane < chans) & live, join_parts(tail, chans), 0.0)[:1, :]
        scale = jnp.where(live, 1.0 / (row + 1e-06), 0.0)
        scale = jnp.broadcast_to(scale, (HEAD_DIM, HAD)).T[:chans, :]
        row = pltpu.roll(jnp.broadcast_to(row, (8, HAD)), first, 1)[:1, :] if first else row
        if has_past:
            row = row + past_ref[slot : slot + 1, :]
        peak_ref[slot : slot + 1, :] = row
        for o in range(4):
            for e in range(4):
                start = (o * 4 + e) * chans
                lanes = pl.ds(pl.multiple_of(place_ref[o] + e * HAD, HAD), HAD)
                block = in_ref[i, j, start : start + chans, :]
                buffer[part, :, lanes] = (block.astype(jnp.float32) * scale).astype(jnp.bfloat16)
        copies[part] = pltpu.make_async_copy(
            buffer.at[part], out_ref.at[0, slot, first : first + chans, :], sems.at[part]
        )
        copies[part].start()
    for copy in copies:
        copy.wait()


def per_device(qkv_weight, placement):
    rows_local, cols_local = qkv_weight.shape
    heads = cols_local // HEAD_DIM
    owners = lax.axis_size("tp")
    rows_a = rows_local // HAD
    params = pltpu.CompilerParams(vmem_limit_bytes=VMEM_BYTES)
    any_spec = pl.BlockSpec(memory_space=pl.ANY)
    smem_spec = pl.BlockSpec(memory_space=pltpu.SMEM)
    vmem_spec = pl.BlockSpec(memory_space=pltpu.VMEM)

    def block_of(rows):
        return jax.ShapeDtypeStruct((rows, HAD), jnp.bfloat16)

    def blocks_of(chans, tail):
        whole, half = heads * 4 * chans, heads * 2 * chans
        return [block_of(rows) for rows in (whole + tail, whole + tail, whole + tail, half + tail, half)]

    me = lax.axis_index("tp")
    group = lax.axis_index("fsdp")
    y, core = group // 2, group % 2
    table_y = jnp.asarray(hadamard_table(4))
    flip_a = jnp.asarray(hadamard_table(rows_a))[4 * y]
    flip_in = table_y[y]
    flip_out = flip_in * flip_in[y]
    sign = (1 - 2 * core).astype(jnp.float32).reshape(1)
    place = (jnp.arange(4, dtype=jnp.int32) ^ y) * (4 * HAD)

    blocks = placement.reshape(owners, heads)
    head_ids = jnp.arange(heads, dtype=jnp.int32)
    owner_ids = jnp.arange(owners, dtype=jnp.int32)
    by_core = [owner_table(c) for c in range(2)]
    send_to = jnp.where(core == 0, jnp.asarray(by_core[0].reshape(-1)), jnp.asarray(by_core[1].reshape(-1)))
    source = jnp.where(core == 0, jnp.asarray(by_core[0].T.reshape(-1)), jnp.asarray(by_core[1].T.reshape(-1)))
    my_owners = lax.dynamic_slice_in_dim(blocks, me, 1, axis=0)
    head_for = jnp.sum(jnp.where(my_owners == send_to[:, None], head_ids[None, :], 0), axis=1)
    has = jnp.any(blocks == me, axis=1)
    present = jnp.any(has[None, :] & (source[:, None] == owner_ids[None, :]), axis=1)
    rank = jnp.sum(((source[None, :] < source[:, None]) & present[None, :]).astype(jnp.int32), axis=1)
    taken = present[None, :] & (rank[None, :] == owner_ids[:, None])
    come_from = jnp.sum(jnp.where(taken, owner_ids[None, :], 0), axis=1)
    live = jnp.any(taken, axis=1).astype(jnp.int32)

    signs = jnp.asarray(hadamard_table(HAD), jnp.bfloat16)
    first_blocks = [shape for _, chans in CHUNKS for shape in blocks_of(chans, 0)]
    turned = pl.pallas_call(
        functools.partial(local_turn_kernel, rows_a),
        grid=(heads,),
        in_specs=[
            smem_spec,
            pl.BlockSpec((rows_local, HEAD_DIM), lambda h: (0, h)),
            pl.BlockSpec((HAD, HAD), lambda h: (0, 0)),
        ],
        out_specs=[pl.BlockSpec((shape.shape[0] // heads, HAD), lambda h: (h, 0)) for shape in first_blocks],
        out_shape=first_blocks,
        scratch_shapes=[pltpu.VMEM((rows_local, HAD), jnp.float32)],
        compiler_params=params,
        name="local_turn",
    )(flip_a, qkv_weight, signs)

    state = [turned[5 * index : 5 * index + 5] for index in range(len(CHUNKS))]
    token = None
    past = []

    def tie(arrays):
        if token is None:
            return list(arrays)
        return list(lax.optimization_barrier((list(arrays), token))[0])

    for stage, index in ORDER:
        first, chans = chunk = CHUNKS[index]
        arrays = tie(state[index])
        if stage == "start":
            state[index] = ring_exchange(arrays)
        elif stage == "y_turn":
            token = pl.pallas_call(
                functools.partial(y_turn_kernel, heads, chans),
                in_specs=[smem_spec] * 2 + [vmem_spec] * 5,
                out_specs=vmem_spec,
                out_shape=jax.ShapeDtypeStruct((4, heads * 4 * chans, HAD), jnp.bfloat16),
                compiler_params=params,
                name="y_turn",
            )(flip_in, flip_out, *arrays)
            state[index] = [token, hop(token, 1)]
        elif stage == "core_turn":
            outs = pl.pallas_call(
                functools.partial(core_turn_kernel, heads, chans),
                in_specs=[smem_spec] + [vmem_spec] * 2,
                out_specs=[vmem_spec] * 5,
                out_shape=blocks_of(chans, TAIL)[:4] + blocks_of(chans, 0)[4:],
                compiler_params=params,
                name="core_turn",
            )(sign, *arrays)
            token = outs[0]
            state[index] = ring_exchange(outs)
        elif stage == "spread":
            token = pl.pallas_call(
                functools.partial(spread_kernel, heads, chans),
                in_specs=[smem_spec] + [vmem_spec] * 5,
                out_specs=vmem_spec,
                out_shape=jax.ShapeDtypeStruct((4, 4, 16 * chans + TAIL, HAD), jnp.bfloat16),
                compiler_params=params,
                name="spread",
            )(head_for, *arrays)
            state[index] = [pair_exchange(token, False)]
        elif stage == "regroup":
            token = pl.pallas_call(
                regroup_kernel,
                in_specs=[vmem_spec],
                out_specs=vmem_spec,
                out_shape=jax.ShapeDtypeStruct(arrays[0].shape, jnp.bfloat16),
                compiler_params=params,
                name="regroup",
            )(*arrays)
            state[index] = [pair_exchange(token, True)]
        else:
            past = pl.pallas_call(
                functools.partial(pack_kernel, owners, chunk, bool(past)),
                in_specs=[smem_spec] * 3 + [vmem_spec] + ([vmem_spec, any_spec] if past else []),
                out_specs=[vmem_spec, any_spec],
                out_shape=[
                    jax.ShapeDtypeStruct((owners, HEAD_DIM), jnp.float32),
                    jax.ShapeDtypeStruct((1, owners, HEAD_DIM, rows_local), jnp.bfloat16),
                ],
                scratch_shapes=[pltpu.VMEM((3, chans, rows_local), jnp.bfloat16), pltpu.SemaphoreType.DMA((3,))],
                input_output_aliases={5: 1} if past else {},
                compiler_params=params,
                name="pack",
            )(come_from, live, place, *arrays, *past)
            token = past[0]
    peaks, packed = past
    return packed, peaks[None]


def solution(mesh):
    in_specs = (P("fsdp", "tp"), P())
    out_specs = (P("tp", None, None, "fsdp"), P("tp", None, None))
    return jax.shard_map(
        per_device, mesh=mesh, in_specs=in_specs, out_specs=out_specs, check_vma=False
    )
```

```python
import functools

import numpy as np
import jax
import jax.numpy as jnp
from jax import lax
from jax.experimental import pallas as pl
from jax.experimental.pallas import tpu as pltpu
from jax.sharding import PartitionSpec as P

HEAD_DIM = 128
HAD = 128
CHUNKS = ((0, 48), (48, 48), (96, 32))
DIRECT = 2
ORDER = (
    ("start", 0),
    ("start", 1),
    ("y_turn", 0),
    ("core_turn", 0),
    ("y_turn", 1),
    ("spread", 0),
    ("start", 2),
    ("core_turn", 1),
    ("y_turn", 2),
    ("core_turn", 2),
    ("spread", 1),
    ("spread", 2),
    ("pack", 0),
    ("pack", 1),
    ("pack", 2),
)
TAIL = 16
VMEM_BYTES = 12 * 1024 * 1024
BOTH = ("fsdp", "tp")


def hadamard_table(order):
    matrix = np.ones((1, 1), np.float32)
    while matrix.shape[0] < order:
        matrix = np.block([[matrix, matrix], [matrix, -matrix]])
    return matrix


def butterfly(values):
    values = list(values)
    half = 1
    while half < len(values):
        for low in range(len(values)):
            if not low & half:
                first, second = values[low], values[low + half]
                values[low], values[low + half] = first + second, first - second
        half *= 2
    return values


def hop(array, flip):
    size = lax.axis_size("fsdp")
    return lax.ppermute(array, "fsdp", [(i, i ^ flip) for i in range(size)])


def ring_exchange(blocks):
    own, one, three, two_a, two_b = blocks
    two_a, two_b = hop(two_a, 2), hop(two_b, 6)
    one, three = hop(one, 2), hop(three, 6)
    return own, one, three, hop(two_a, 6), hop(two_b, 2)


PAIRINGS = ((1, 3), (3, 1))
BITS_A = ((1, 0), (4, 0), (1, 1), (4, 1))
BITS_B = ((4, 0), (1, 0), (4, 1), (1, 1))


def owner_offsets(core, bits):
    table = np.zeros(1 << len(bits), np.int32)
    for index in range(len(table)):
        for bit, (factor, which) in enumerate(bits):
            if index >> bit & 1:
                table[index] ^= factor * PAIRINGS[core][which]
    return table


def owner_hop(array, factor, which):
    groups, owners = lax.axis_size("fsdp"), lax.axis_size("tp")
    pairs = []
    for f in range(groups):
        flip = factor * PAIRINGS[f & 1][which]
        pairs += [(f * owners + t, f * owners + (t ^ flip)) for t in range(owners)]
    return lax.ppermute(array, BOTH, pairs)


def regroup_kernel(plan, *refs):
    out_ref = refs[-1]
    for row, (array, index) in enumerate(plan):
        out_ref[row] = refs[array][index]


def hypercube(keep, send, bits):
    held = [keep, owner_hop(send, *bits[0])]
    for step in range(1, len(bits)):
        plan = []
        for array in range(len(held)):
            origins = 1 << max(array - 1, 0)
            size = keep.shape[0] // origins
            for origin in range(origins):
                width = keep.shape[0] >> step
                plan += [(array, origin * size + width + i) for i in range(width)]
        vmem_spec = pl.BlockSpec(memory_space=pltpu.VMEM)
        payload = pl.pallas_call(
            functools.partial(regroup_kernel, tuple(plan)),
            in_specs=[vmem_spec] * len(held),
            out_specs=vmem_spec,
            out_shape=jax.ShapeDtypeStruct(keep.shape, keep.dtype),
            compiler_params=pltpu.CompilerParams(vmem_limit_bytes=VMEM_BYTES),
            name="regroup",
        )(*held)
        held.append(owner_hop(payload, *bits[step]))
    return held


def first_slots(bits):
    slots = [(0, 0)]
    for array in range(1, bits + 1):
        origins = 1 << (array - 1)
        size = (1 << (bits - 1)) // origins
        slots += [(array, origin * size) for origin in range(origins)]
    return slots


def local_turn_kernel(rows_a, flip_ref, weight_ref, signs_ref, *refs):
    out_refs, turned = refs[:-1], refs[-1]
    columns = jnp.concatenate([weight_ref[a * HAD : (a + 1) * HAD, :].T for a in range(rows_a)], axis=0)
    turned[...] = jnp.dot(columns, signs_ref[...], preferred_element_type=jnp.float32)
    for index, (first, chans) in enumerate(CHUNKS):
        own, one, three, two_a, two_b = out_refs[5 * index : 5 * index + 5]
        for low in range(0, chans, 16):
            outs = []
            for a in range(rows_a):
                start = a * HEAD_DIM + first + low
                outs.append(turned[start : start + 16, :] * (flip_ref[a] * (1.0 / HAD)))
            outs = butterfly(outs)
            for a in range(rows_a):
                offset, e = a // 4, a % 4
                if offset == 2:
                    out_ref, e = (two_a, two_b)[e // 2], e % 2
                else:
                    out_ref = {0: own, 1: one, 3: three}[offset]
                out_ref[e * chans + low : e * chans + low + 16, :] = outs[a].astype(jnp.bfloat16)


def pieces(head, e, chans, low):
    whole = (head * 4 + e) * chans + low
    half = (head * 2 + e % 2) * chans + low
    return (0, whole), (1, whole), (3 + e // 2, half), (2, whole)


def y_turn_kernel(heads, chans, flip_in_ref, flip_out_ref, *refs):
    in_refs, out_ref = refs[:-1], refs[-1]
    for head in range(heads):
        for e in range(4):
            for low in range(0, chans, 16):
                parts = [
                    in_refs[array][row : row + 16, :].astype(jnp.float32) * flip_in_ref[o]
                    for o, (array, row) in enumerate(pieces(head, e, chans, low))
                ]
                row = (head * 4 + e) * chans + low
                for o, value in enumerate(butterfly(parts)):
                    out_ref[o, row : row + 16, :] = (value * flip_out_ref[o]).astype(jnp.bfloat16)


def join_parts(value, chans):
    return value + pltpu.roll(value, HAD - chans, 1)


def split_parts(value, chans):
    high = value.astype(jnp.bfloat16).astype(jnp.float32)
    lane = lax.broadcasted_iota(jnp.int32, value.shape, 1)
    both = jnp.where(lane < chans, high, pltpu.roll(value - high, chans, 1))
    return jnp.where(lane < 2 * chans, both, 0.0).astype(jnp.bfloat16)


def core_turn_kernel(heads, chans, sign_ref, mine_ref, other_ref, *out_refs):
    row_id = lax.broadcasted_iota(jnp.int32, (TAIL, HAD), 0)
    tail = jnp.zeros((TAIL, HAD), jnp.float32)
    sign = sign_ref[0]
    for head in range(heads):
        columns = []
        for low in range(0, chans, 16):
            largest = None
            for e in range(4):
                row = (head * 4 + e) * chans + low
                for o, (array, out_row) in enumerate(pieces(head, e, chans, low)):
                    mine = mine_ref[o, row : row + 16, :].astype(jnp.float32)
                    other = other_ref[o, row : row + 16, :].astype(jnp.float32)
                    out_refs[array][out_row : out_row + 16, :] = (other + mine * sign).astype(jnp.bfloat16)
                    magnitude = jnp.abs(mine) + jnp.abs(other)
                    largest = magnitude if largest is None else jnp.maximum(largest, magnitude)
            columns.append(largest)
        columns.append(jnp.zeros((HAD - chans, HAD), jnp.float32))
        peak = jnp.max(jnp.concatenate(columns, axis=0).T, axis=0, keepdims=True)
        tail = jnp.where(row_id == head, peak, tail)
    tail = split_parts(tail, chans)
    for out_ref in out_refs[:4]:
        out_ref[out_ref.shape[0] - TAIL :, :] = tail


def spread_kernel(heads, chans, head_ref, *refs):
    in_refs, out_refs = refs[:5], refs[5:]
    peaks = None
    for in_ref in in_refs[:4]:
        part = join_parts(in_ref[in_ref.shape[0] - TAIL :, :].astype(jnp.float32), chans)
        peaks = part if peaks is None else jnp.maximum(peaks, part)
    row_id = lax.broadcasted_iota(jnp.int32, (TAIL, HAD), 0)
    span, half = 4 * chans, 2 * chans
    sizes = ((0, span), (1, span), (3, half), (4, half), (2, span))
    for slot in range(16):
        if len(out_refs) == 1:
            parts = ((out_refs[0], slot, head_ref[slot], sizes, True),)
        else:
            parts = (
                (out_refs[slot // 8], slot % 8, head_ref[slot], sizes[:2], False),
                (out_refs[2 + slot // 8], slot % 8, head_ref[16 + slot], sizes[2:], True),
            )
        for out_ref, index, head, arrays, with_tail in parts:
            start = 0
            for array, size in arrays:
                rows = pl.ds(pl.multiple_of(head * size, 16), size)
                out_ref[index, start : start + size, :] = in_refs[array][rows, :]
                start += size
            if with_tail:
                peak = jnp.sum(jnp.where(row_id == head, peaks, 0.0), axis=0, keepdims=True)
                out_ref[index, start:, :] = split_parts(jnp.broadcast_to(peak, (TAIL, HAD)), chans)


def pack_kernel(owners, chunk, has_past, slot_ref, live_ref, place_ref, *refs):
    first, chans = chunk
    peak_ref, out_ref, buffer, sems = refs[-4:]
    past_ref = refs[-6] if has_past else None
    in_refs = refs[: -6 if has_past else -4]
    lane = lax.broadcasted_iota(jnp.int32, (TAIL, HAD), 1)
    depth = buffer.shape[0]
    copies = [None] * depth
    slots = first_slots(4)
    for origin in range(owners):
        if len(in_refs) == 1:
            halves = ((in_refs[0], origin, 0), (in_refs[0], origin, 8 * chans))
        else:
            a_array, a_index = slots[origin]
            b_array, b_index = slots[((origin & 5) << 1) | ((origin & 10) >> 1)]
            halves = ((in_refs[a_array], a_index, 0), (in_refs[5 + b_array], b_index, 0))
        part = origin % depth
        if copies[part] is not None:
            copies[part].wait()
        live = live_ref[origin] != 0
        slot = slot_ref[origin]
        last_ref, last_index, last_start = halves[1]
        tail = last_ref[last_index, last_start + 8 * chans :, :].astype(jnp.float32)
        row = jnp.where((lane < chans) & live, join_parts(tail, chans), 0.0)[:1, :]
        scale = jnp.where(live, 1.0 / (row + 1e-06), 0.0)
        scale = jnp.broadcast_to(scale, (HEAD_DIM, HAD)).T[:chans, :]
        row = pltpu.roll(jnp.broadcast_to(row, (8, HAD)), first, 1)[:1, :] if first else row
        if has_past:
            row = row + past_ref[pl.ds(slot, 1), :]
        peak_ref[pl.ds(slot, 1), :] = row
        for o in range(4):
            in_ref, index, offset = halves[o // 2]
            for e in range(4):
                start = offset + (o % 2 * 4 + e) * chans
                lanes = pl.ds(pl.multiple_of(place_ref[o] + e * HAD, HAD), HAD)
                block = in_ref[index, start : start + chans, :]
                buffer[part, :, lanes] = (block.astype(jnp.float32) * scale).astype(jnp.bfloat16)
        copies[part] = pltpu.make_async_copy(
            buffer.at[part], out_ref.at[0, slot, first : first + chans, :], sems.at[part]
        )
        copies[part].start()
    for copy in copies:
        copy.wait()


def per_device(qkv_weight, placement):
    rows_local, cols_local = qkv_weight.shape
    heads = cols_local // HEAD_DIM
    owners = lax.axis_size("tp")
    rows_a = rows_local // HAD
    params = pltpu.CompilerParams(vmem_limit_bytes=VMEM_BYTES)
    any_spec = pl.BlockSpec(memory_space=pl.ANY)
    smem_spec = pl.BlockSpec(memory_space=pltpu.SMEM)
    vmem_spec = pl.BlockSpec(memory_space=pltpu.VMEM)

    def block_of(rows):
        return jax.ShapeDtypeStruct((rows, HAD), jnp.bfloat16)

    def blocks_of(chans, tail):
        whole, half = heads * 4 * chans, heads * 2 * chans
        return [block_of(rows) for rows in (whole + tail, whole + tail, whole + tail, half + tail, half)]

    me = lax.axis_index("tp")
    group = lax.axis_index("fsdp")
    y, core = group // 2, group % 2
    table_y = jnp.asarray(hadamard_table(4))
    flip_a = jnp.asarray(hadamard_table(rows_a))[4 * y]
    flip_in = table_y[y]
    flip_out = flip_in * flip_in[y]
    sign = (1 - 2 * core).astype(jnp.float32).reshape(1)
    place = (jnp.arange(4, dtype=jnp.int32) ^ y) * (4 * HAD)

    blocks = placement.reshape(owners, heads)
    head_ids = jnp.arange(heads, dtype=jnp.int32)
    owner_ids = jnp.arange(owners, dtype=jnp.int32)
    my_owners = lax.dynamic_slice_in_dim(blocks, me, 1, axis=0)
    has = jnp.any(blocks == me, axis=1)

    def pick(bits):
        return jnp.where(core == 0, *(jnp.asarray(owner_offsets(c, bits)) for c in range(2))) ^ me

    def heads_for(to):
        return jnp.sum(jnp.where(my_owners == to[:, None], head_ids[None, :], 0), axis=1)

    def slots_of(source):
        live = jnp.any(has[None, :] & (source[:, None] == owner_ids[None, :]), axis=1)
        before = source[None, :] < source[:, None]
        rank = jnp.sum((before & live[None, :]).astype(jnp.int32), axis=1)
        spare = jnp.sum((before & ~live[None, :]).astype(jnp.int32), axis=1) + jnp.sum(live.astype(jnp.int32))
        return jnp.where(live, rank, spare), live.astype(jnp.int32)

    direct_heads = heads_for(owner_ids)
    direct_slots = slots_of(owner_ids)
    cube_heads = jnp.concatenate([heads_for(pick(bits[::-1])) for bits in (BITS_A, BITS_B)])
    cube_slots = slots_of(pick(BITS_A))

    signs = jnp.asarray(hadamard_table(HAD), jnp.bfloat16)
    tables = (flip_a, flip_in, flip_out, sign, place, direct_heads, direct_slots, cube_heads, cube_slots)
    tables, qkv_weight = lax.optimization_barrier((tables, qkv_weight))
    flip_a, flip_in, flip_out, sign, place, direct_heads, direct_slots, cube_heads, cube_slots = tables
    first_blocks = [shape for _, chans in CHUNKS for shape in blocks_of(chans, 0)]
    turned = pl.pallas_call(
        functools.partial(local_turn_kernel, rows_a),
        grid=(heads,),
        in_specs=[
            smem_spec,
            pl.BlockSpec((rows_local, HEAD_DIM), lambda h: (0, h)),
            pl.BlockSpec((HAD, HAD), lambda h: (0, 0)),
        ],
        out_specs=[pl.BlockSpec((shape.shape[0] // heads, HAD), lambda h: (h, 0)) for shape in first_blocks],
        out_shape=first_blocks,
        scratch_shapes=[pltpu.VMEM((rows_local, HAD), jnp.float32)],
        compiler_params=params,
        name="local_turn",
    )(flip_a, qkv_weight, signs)

    state = [turned[5 * index : 5 * index + 5] for index in range(len(CHUNKS))]
    token = None
    past = []

    def tie(arrays):
        if token is None:
            return list(arrays)
        return list(lax.optimization_barrier((list(arrays), token))[0])

    for stage, index in ORDER:
        first, chans = chunk = CHUNKS[index]
        arrays = tie(state[index])
        if stage == "start":
            state[index] = ring_exchange(arrays)
        elif stage == "y_turn":
            token = pl.pallas_call(
                functools.partial(y_turn_kernel, heads, chans),
                in_specs=[smem_spec] * 2 + [vmem_spec] * 5,
                out_specs=vmem_spec,
                out_shape=jax.ShapeDtypeStruct((4, heads * 4 * chans, HAD), jnp.bfloat16),
                compiler_params=params,
                name="y_turn",
            )(flip_in, flip_out, *arrays)
            state[index] = [token, hop(token, 1)]
        elif stage == "core_turn":
            outs = pl.pallas_call(
                functools.partial(core_turn_kernel, heads, chans),
                in_specs=[smem_spec] + [vmem_spec] * 2,
                out_specs=[vmem_spec] * 5,
                out_shape=blocks_of(chans, TAIL)[:4] + blocks_of(chans, 0)[4:],
                compiler_params=params,
                name="core_turn",
            )(sign, *arrays)
            token = outs[0]
            state[index] = ring_exchange(outs)
        elif stage == "spread":
            direct = index < DIRECT
            if direct:
                shapes = [(owners, 16 * chans + TAIL)]
            else:
                shapes = [(owners // 2, 8 * chans)] * 2 + [(owners // 2, 8 * chans + TAIL)] * 2
            outs = pl.pallas_call(
                functools.partial(spread_kernel, heads, chans),
                in_specs=[smem_spec] + [vmem_spec] * 5,
                out_specs=[vmem_spec] * len(shapes),
                out_shape=[jax.ShapeDtypeStruct(shape + (HAD,), jnp.bfloat16) for shape in shapes],
                compiler_params=params,
                name="spread",
            )(direct_heads if direct else cube_heads, *arrays)
            token = outs[0]
            if direct:
                state[index] = [lax.all_to_all(outs[0], "tp", split_axis=0, concat_axis=0, tiled=True)]
            else:
                state[index] = hypercube(*outs[:2], BITS_A) + hypercube(*outs[2:], BITS_B)
        else:
            slot, live = direct_slots if index < DIRECT else cube_slots
            past = pl.pallas_call(
                functools.partial(pack_kernel, owners, chunk, bool(past)),
                in_specs=[smem_spec] * 3 + [vmem_spec] * len(arrays) + ([vmem_spec, any_spec] if past else []),
                out_specs=[vmem_spec, any_spec],
                out_shape=[
                    jax.ShapeDtypeStruct((owners, HEAD_DIM), jnp.float32),
                    jax.ShapeDtypeStruct((1, owners, HEAD_DIM, rows_local), jnp.bfloat16),
                ],
                scratch_shapes=[pltpu.VMEM((3, chans, rows_local), jnp.bfloat16), pltpu.SemaphoreType.DMA((3,))],
                input_output_aliases={4 + len(arrays): 1} if past else {},
                compiler_params=params,
                name="pack",
            )(slot, live, place, *arrays, *past)
            token = past[0]
    peaks, packed = past
    return packed, peaks[None]


def solution(mesh):
    in_specs = (P("fsdp", "tp"), P())
    out_specs = (P("tp", None, None, "fsdp"), P("tp", None, None))
    return jax.shard_map(
        per_device, mesh=mesh, in_specs=in_specs, out_specs=out_specs, check_vma=False
    )
```

```python
import functools

import numpy as np
import jax
import jax.numpy as jnp
from jax import lax
from jax.experimental import pallas as pl
from jax.experimental.pallas import tpu as pltpu
from jax.sharding import PartitionSpec as P

HEAD_DIM = 128
HAD = 128
CHUNKS = ((0, 48), (48, 48), (96, 32))
DIRECT = 2
ORDER = (
    ("start", 0),
    ("cross", 0),
    ("start", 1),
    ("spread", 0),
    ("cross", 1),
    ("start", 2),
    ("spread", 1),
    ("cross", 2),
    ("pack", 0),
    ("spread", 2),
    ("pack", 1),
    ("pack", 2),
)
TAIL = 16
VMEM_BYTES = 12 * 1024 * 1024
BOTH = ("fsdp", "tp")


def hadamard_table(order):
    matrix = np.ones((1, 1), np.float32)
    while matrix.shape[0] < order:
        matrix = np.block([[matrix, matrix], [matrix, -matrix]])
    return matrix


def butterfly(values):
    values = list(values)
    half = 1
    while half < len(values):
        for low in range(len(values)):
            if not low & half:
                first, second = values[low], values[low + half]
                values[low], values[low + half] = first + second, first - second
        half *= 2
    return values


PATHS = {4: (2, 6), 5: (6, 3), 2: (2,), 6: (6,), 3: (3,), 7: (7,), 1: (1,)}


def ring_exchange(blocks):
    size = lax.axis_size("fsdp")
    out = list(blocks)
    for offset, hops in PATHS.items():
        for flip in hops:
            out[offset] = lax.ppermute(out[offset], "fsdp", [(i, i ^ flip) for i in range(size)])
    return out


PAIRINGS = ((1, 3), (3, 1))
BITS_A = ((1, 0), (4, 0), (1, 1), (4, 1))
BITS_B = ((4, 0), (1, 0), (4, 1), (1, 1))


def owner_offsets(core, bits):
    table = np.zeros(1 << len(bits), np.int32)
    for index in range(len(table)):
        for bit, (factor, which) in enumerate(bits):
            if index >> bit & 1:
                table[index] ^= factor * PAIRINGS[core][which]
    return table


def owner_hop(array, factor, which):
    groups, owners = lax.axis_size("fsdp"), lax.axis_size("tp")
    pairs = []
    for f in range(groups):
        flip = factor * PAIRINGS[f & 1][which]
        pairs += [(f * owners + t, f * owners + (t ^ flip)) for t in range(owners)]
    return lax.ppermute(array, BOTH, pairs)


def regroup_kernel(plan, *refs):
    out_ref = refs[-1]
    for row, (array, index) in enumerate(plan):
        out_ref[row] = refs[array][index]


def hypercube(keep, send, bits):
    held = [keep, owner_hop(send, *bits[0])]
    for step in range(1, len(bits)):
        plan = []
        for array in range(len(held)):
            origins = 1 << max(array - 1, 0)
            size = keep.shape[0] // origins
            for origin in range(origins):
                width = keep.shape[0] >> step
                plan += [(array, origin * size + width + i) for i in range(width)]
        vmem_spec = pl.BlockSpec(memory_space=pltpu.VMEM)
        payload = pl.pallas_call(
            functools.partial(regroup_kernel, tuple(plan)),
            in_specs=[vmem_spec] * len(held),
            out_specs=vmem_spec,
            out_shape=jax.ShapeDtypeStruct(keep.shape, keep.dtype),
            compiler_params=pltpu.CompilerParams(vmem_limit_bytes=VMEM_BYTES),
            name="regroup",
        )(*held)
        held.append(owner_hop(payload, *bits[step]))
    return held


def first_slots(bits):
    slots = [(0, 0)]
    for array in range(1, bits + 1):
        origins = 1 << (array - 1)
        size = (1 << (bits - 1)) // origins
        slots += [(array, origin * size) for origin in range(origins)]
    return slots


def sign_of(value, bits):
    both = value & bits
    both = both ^ (both >> 2)
    both = both ^ (both >> 1)
    return (1 - 2 * (both & 1)).astype(jnp.float32)


def local_turn_kernel(rows_a, weight_ref, signs_ref, *refs):
    out_refs, turned = refs[:-1], refs[-1]
    group = lax.axis_index("fsdp")
    flips = [sign_of(group, a >> 1) * (1.0 / HAD) for a in range(rows_a)]
    columns = jnp.concatenate([weight_ref[a * HAD : (a + 1) * HAD, :].T for a in range(rows_a)], axis=0)
    turned[...] = jnp.dot(columns, signs_ref[...], preferred_element_type=jnp.float32)
    for index, (first, chans) in enumerate(CHUNKS):
        for low in range(0, chans, 16):
            outs = []
            for a in range(rows_a):
                start = a * HEAD_DIM + first + low
                outs.append(turned[start : start + 16, :] * flips[a])
            outs = butterfly(outs)
            for a in range(rows_a):
                row = a % 2 * chans + low
                out_refs[8 * index + a // 2][row : row + 16, :] = outs[a].astype(jnp.bfloat16)


def join_parts(value, chans):
    return value + pltpu.roll(value, HAD - chans, 1)


def split_parts(value, chans):
    high = value.astype(jnp.bfloat16).astype(jnp.float32)
    lane = lax.broadcasted_iota(jnp.int32, value.shape, 1)
    both = jnp.where(lane < chans, high, pltpu.roll(value - high, chans, 1))
    return jnp.where(lane < 2 * chans, both, 0.0).astype(jnp.bfloat16)


def cross_turn_kernel(heads, chans, *refs):
    in_refs, out_refs = refs[:8], refs[8:]
    group = lax.axis_index("fsdp")
    flips_in = [sign_of(group, s) for s in range(8)]
    flips_out = [flip * sign_of(group, group) for flip in flips_in]
    row_id = lax.broadcasted_iota(jnp.int32, (TAIL, HAD), 0)
    tail = jnp.zeros((TAIL, HAD), jnp.float32)
    for head in range(heads):
        columns = []
        for low in range(0, chans, 16):
            largest = None
            for e in range(2):
                row = (head * 2 + e) * chans + low
                outs = butterfly([in_refs[s][row : row + 16, :].astype(jnp.float32) * flips_in[s] for s in range(8)])
                for s in range(8):
                    out_refs[s][row : row + 16, :] = (outs[s] * flips_out[s]).astype(jnp.bfloat16)
                    magnitude = jnp.abs(outs[s])
                    largest = magnitude if largest is None else jnp.maximum(largest, magnitude)
            columns.append(largest)
        columns.append(jnp.zeros((HAD - chans, HAD), jnp.float32))
        peak = jnp.max(jnp.concatenate(columns, axis=0).T, axis=0, keepdims=True)
        tail = jnp.where(row_id == head, peak, tail)
    tail = split_parts(tail, chans)
    for out_ref in out_refs:
        out_ref[heads * 2 * chans :, :] = tail


def cube_offset(core, bits, index):
    offsets = [int(owner_offsets(c, bits)[index]) for c in range(2)]
    return jnp.where(core == 0, offsets[0], offsets[1])


def spread_kernel(heads, chans, placement_ref, *refs):
    in_refs, out_refs = refs[:8], refs[8:]
    me, core = lax.axis_index("tp"), lax.axis_index("fsdp") & 1
    mine = [placement_ref[me * heads + head] for head in range(heads)]

    def head_for(owner):
        head = 0
        for index in range(1, heads):
            head = jnp.where(mine[index] == owner, index, head)
        return head

    peaks = None
    for in_ref in in_refs:
        part = join_parts(in_ref[heads * 2 * chans :, :].astype(jnp.float32), chans)
        peaks = part if peaks is None else jnp.maximum(peaks, part)
    row_id = lax.broadcasted_iota(jnp.int32, (TAIL, HAD), 0)
    span = 2 * chans
    for slot in range(16):
        if len(out_refs) == 1:
            parts = ((out_refs[0], slot, head_for(slot), in_refs, True),)
        else:
            to_a, to_b = (me ^ cube_offset(core, bits[::-1], slot) for bits in (BITS_A, BITS_B))
            parts = (
                (out_refs[slot // 8], slot % 8, head_for(to_a), in_refs[:4], False),
                (out_refs[2 + slot // 8], slot % 8, head_for(to_b), in_refs[4:], True),
            )
        for out_ref, index, head, arrays, with_tail in parts:
            rows = pl.ds(pl.multiple_of(head * span, 16), span)
            for s, array in enumerate(arrays):
                out_ref[index, s * span : (s + 1) * span, :] = array[rows, :]
            if with_tail:
                peak = jnp.sum(jnp.where(row_id == head, peaks, 0.0), axis=0, keepdims=True)
                out_ref[index, len(arrays) * span :, :] = split_parts(jnp.broadcast_to(peak, (TAIL, HAD)), chans)


def pack_kernel(owners, heads, chunk, has_past, placement_ref, *refs):
    first, chans = chunk
    peak_ref, out_ref, buffer, sems, live_ref, slot_ref = refs[-6:]
    past_ref = refs[-8] if has_past else None
    in_refs = refs[: -8 if has_past else -6]
    me, group = lax.axis_index("tp"), lax.axis_index("fsdp")
    count = 0
    for source in range(owners):
        live = 0
        for head in range(heads):
            live = jnp.where(placement_ref[source * heads + head] == me, 1, live)
        live_ref[source] = live
        slot_ref[source] = count
        count = count + live
    lane = lax.broadcasted_iota(jnp.int32, (TAIL, HAD), 1)
    depth = buffer.shape[0]
    copies = [None] * depth
    slots = first_slots(4)
    for origin in range(owners):
        if len(in_refs) == 1:
            source = origin
            halves = ((in_refs[0], origin, 0), (in_refs[0], origin, 8 * chans))
        else:
            source = me ^ cube_offset(group & 1, BITS_A, origin)
            a_array, a_index = slots[origin]
            b_array, b_index = slots[((origin & 5) << 1) | ((origin & 10) >> 1)]
            halves = ((in_refs[a_array], a_index, 0), (in_refs[5 + b_array], b_index, 0))
        part = origin % depth
        if copies[part] is not None:
            copies[part].wait()
        live = live_ref[source] != 0
        slot = jnp.where(live, slot_ref[source], count + source - slot_ref[source])
        last_ref, last_index, last_start = halves[1]
        tail = last_ref[last_index, last_start + 8 * chans :, :].astype(jnp.float32)
        row = jnp.where((lane < chans) & live, join_parts(tail, chans), 0.0)[:1, :]
        scale = jnp.where(live, 1.0 / (row + 1e-06), 0.0)
        scale = jnp.broadcast_to(scale, (HEAD_DIM, HAD)).T[:chans, :]
        row = pltpu.roll(jnp.broadcast_to(row, (8, HAD)), first, 1)[:1, :] if first else row
        if has_past:
            row = row + past_ref[pl.ds(slot, 1), :]
        peak_ref[pl.ds(slot, 1), :] = row
        for s in range(8):
            in_ref, index, offset = halves[s // 4]
            for e in range(2):
                start = offset + (s % 4 * 2 + e) * chans
                lanes = pl.ds(pl.multiple_of(((group ^ s) * 2 + e) * HAD, HAD), HAD)
                block = in_ref[index, start : start + chans, :]
                buffer[part, :, lanes] = (block.astype(jnp.float32) * scale).astype(jnp.bfloat16)
        copies[part] = pltpu.make_async_copy(
            buffer.at[part], out_ref.at[0, slot, first : first + chans, :], sems.at[part]
        )
        copies[part].start()
    for copy in copies:
        copy.wait()


def per_device(qkv_weight, placement):
    rows_local, cols_local = qkv_weight.shape
    heads = cols_local // HEAD_DIM
    owners = lax.axis_size("tp")
    rows_a = rows_local // HAD
    params = pltpu.CompilerParams(vmem_limit_bytes=VMEM_BYTES)
    any_spec = pl.BlockSpec(memory_space=pl.ANY)
    smem_spec = pl.BlockSpec(memory_space=pltpu.SMEM)
    vmem_spec = pl.BlockSpec(memory_space=pltpu.VMEM)

    def blocks_of(chans, tail):
        return [jax.ShapeDtypeStruct((heads * 2 * chans + tail, HAD), jnp.bfloat16)] * 8

    signs = jnp.asarray(hadamard_table(HAD), jnp.bfloat16)
    first_blocks = [shape for _, chans in CHUNKS for shape in blocks_of(chans, 0)]
    turned = pl.pallas_call(
        functools.partial(local_turn_kernel, rows_a),
        grid=(heads,),
        in_specs=[
            pl.BlockSpec((rows_local, HEAD_DIM), lambda h: (0, h)),
            pl.BlockSpec((HAD, HAD), lambda h: (0, 0)),
        ],
        out_specs=[pl.BlockSpec((shape.shape[0] // heads, HAD), lambda h: (h, 0)) for shape in first_blocks],
        out_shape=first_blocks,
        scratch_shapes=[pltpu.VMEM((rows_local, HAD), jnp.float32)],
        compiler_params=params,
        name="local_turn",
    )(qkv_weight, signs)

    state = [turned[8 * index : 8 * index + 8] for index in range(len(CHUNKS))]
    token = None
    past = []

    def tie(arrays):
        if token is None:
            return list(arrays)
        return list(lax.optimization_barrier((list(arrays), token))[0])

    for stage, index in ORDER:
        first, chans = chunk = CHUNKS[index]
        arrays = tie(state[index])
        if stage == "start":
            state[index] = ring_exchange(arrays)
        elif stage == "cross":
            outs = pl.pallas_call(
                functools.partial(cross_turn_kernel, heads, chans),
                in_specs=[vmem_spec] * 8,
                out_specs=[vmem_spec] * 8,
                out_shape=blocks_of(chans, TAIL),
                compiler_params=params,
                name="cross_turn",
            )(*arrays)
            token = outs[0]
            state[index] = ring_exchange(outs)
        elif stage == "spread":
            direct = index < DIRECT
            if direct:
                shapes = [(owners, 16 * chans + TAIL)]
            else:
                shapes = [(owners // 2, 8 * chans)] * 2 + [(owners // 2, 8 * chans + TAIL)] * 2
            outs = pl.pallas_call(
                functools.partial(spread_kernel, heads, chans),
                in_specs=[smem_spec] + [vmem_spec] * 8,
                out_specs=[vmem_spec] * len(shapes),
                out_shape=[jax.ShapeDtypeStruct(shape + (HAD,), jnp.bfloat16) for shape in shapes],
                compiler_params=params,
                name="spread",
            )(placement, *arrays)
            token = outs[0]
            if direct:
                state[index] = [lax.all_to_all(outs[0], "tp", split_axis=0, concat_axis=0, tiled=True)]
            else:
                state[index] = hypercube(*outs[:2], BITS_A) + hypercube(*outs[2:], BITS_B)
        else:
            past = pl.pallas_call(
                functools.partial(pack_kernel, owners, heads, chunk, bool(past)),
                in_specs=[smem_spec] + [vmem_spec] * len(arrays) + ([vmem_spec, any_spec] if past else []),
                out_specs=[vmem_spec, any_spec],
                out_shape=[
                    jax.ShapeDtypeStruct((owners, HEAD_DIM), jnp.float32),
                    jax.ShapeDtypeStruct((1, owners, HEAD_DIM, rows_local), jnp.bfloat16),
                ],
                scratch_shapes=[
                    pltpu.VMEM((3, chans, rows_local), jnp.bfloat16),
                    pltpu.SemaphoreType.DMA((3,)),
                    pltpu.SMEM((owners,), jnp.int32),
                    pltpu.SMEM((owners,), jnp.int32),
                ],
                input_output_aliases={2 + len(arrays): 1} if past else {},
                compiler_params=params,
                name="pack",
            )(placement, *arrays, *past)
            token = past[0]
    peaks, packed = past
    return packed, peaks[None]


def solution(mesh):
    in_specs = (P("fsdp", "tp"), P())
    out_specs = (P("tp", None, None, "fsdp"), P("tp", None, None))
    return jax.shard_map(
        per_device, mesh=mesh, in_specs=in_specs, out_specs=out_specs, check_vma=False
    )
```

```python
import functools

import numpy as np
import jax
import jax.numpy as jnp
from jax import lax
from jax.experimental import pallas as pl
from jax.experimental.pallas import tpu as pltpu
from jax.sharding import PartitionSpec as P

HEAD_DIM = 128
HAD = 128
CHUNKS = ((0, 32), (32, 48), (80, 48))
ORDER = (
    ("start", 0),
    ("start", 1),
    ("y_regroup", 0),
    ("y_regroup", 1),
    ("cross", 0),
    ("start", 2),
    ("y_regroup", 0),
    ("cross", 1),
    ("spread", 0),
    ("y_regroup", 2),
    ("y_regroup", 1),
    ("regroup", 0),
    ("cross", 2),
    ("spread", 1),
    ("pack", 0),
    ("y_regroup", 2),
    ("regroup", 1),
    ("spread", 2),
    ("pack", 1),
    ("regroup", 2),
    ("pack", 2),
)
TAIL = 16
VMEM_BYTES = 12 * 1024 * 1024
BOTH = ("fsdp", "tp")


def hadamard_table(order):
    matrix = np.ones((1, 1), np.float32)
    while matrix.shape[0] < order:
        matrix = np.block([[matrix, matrix], [matrix, -matrix]])
    return matrix


def butterfly(values):
    values = list(values)
    half = 1
    while half < len(values):
        for low in range(len(values)):
            if not low & half:
                first, second = values[low], values[low + half]
                values[low], values[low + half] = first + second, first - second
        half *= 2
    return values


PAIRINGS = ((1, 3), (3, 1))


def hop(array, rule):
    groups, owners = lax.axis_size("fsdp"), lax.axis_size("tp")
    pairs = []
    for f in range(groups):
        for t in range(owners):
            to_f, to_t = rule(f, t)
            pairs.append((f * owners + t, to_f * owners + to_t))
    return lax.ppermute(array, BOTH, pairs)


def y_first(blocks):
    own, core, pair, both = blocks
    pair = hop(pair, lambda f, t: (f ^ 2 * PAIRINGS[f & 1][0], t))
    both = hop(both, lambda f, t: (f ^ 1 ^ 2 * PAIRINGS[1 - (f & 1)][0], t))
    core = hop(core, lambda f, t: (f ^ 1, t))
    return [own, core, pair, both]


def y_second(payload):
    return hop(payload, lambda f, t: (f ^ 2 * PAIRINGS[f & 1][1], t))


def owner_hops(blocks, which):
    out = [None] * 3
    for place in (2, 0, 1):
        factor = (1, 4, 5)[place]
        out[place] = hop(blocks[place], lambda f, t: (f, t ^ factor * PAIRINGS[f & 1][which]))
    return out


def to_slots(values, swap):
    return (
        (values[0], jnp.where(swap, values[2], values[6])),
        (values[1], jnp.where(swap, values[7], values[3])),
        (jnp.where(swap, values[6], values[2]), values[4]),
        (jnp.where(swap, values[3], values[7]), values[5]),
    )


def from_origins(values, swap):
    return (
        values[0],
        values[1],
        jnp.where(swap, values[4], values[2]),
        jnp.where(swap, values[5], values[3]),
        values[6],
        values[7],
        jnp.where(swap, values[2], values[4]),
        jnp.where(swap, values[3], values[5]),
    )


def y_regroup_kernel(*refs):
    for index, in_ref in enumerate(refs[:4]):
        refs[4][index] = in_ref[1]


def regroup_kernel(*refs):
    in_refs, out_refs = refs[:4], refs[4:]
    for slot, out_ref in enumerate(out_refs):
        for index, in_ref in enumerate(in_refs):
            out_ref[index] = in_ref[slot + 1]


def sign_of(value, bits):
    both = value & bits
    both = both ^ (both >> 2)
    both = both ^ (both >> 1)
    return (1 - 2 * (both & 1)).astype(jnp.float32)


def local_turn_kernel(rows_a, weight_ref, signs_ref, *refs):
    out_refs, turned = refs[:-1], refs[-1]
    group = lax.axis_index("fsdp")
    swap = group & 1 != 0
    flips = [sign_of(group, a >> 1) * (1.0 / HAD) for a in range(rows_a)]
    columns = jnp.concatenate([weight_ref[a * HAD : (a + 1) * HAD, :].T for a in range(rows_a)], axis=0)
    turned[...] = jnp.dot(columns, signs_ref[...], preferred_element_type=jnp.float32)
    for index, (first, chans) in enumerate(CHUNKS):
        for low in range(0, chans, 16):
            outs = []
            for a in range(rows_a):
                start = a * HEAD_DIM + first + low
                outs.append(turned[start : start + 16, :] * flips[a])
            outs = butterfly(outs)
            for e in range(2):
                row = e * chans + low
                for array, values in enumerate(to_slots(outs[e::2], swap)):
                    for slot, value in enumerate(values):
                        out_refs[4 * index + array][slot, row : row + 16, :] = value.astype(jnp.bfloat16)


def join_parts(value, chans):
    return value + pltpu.roll(value, HAD - chans, 1)


def split_parts(value, chans):
    high = value.astype(jnp.bfloat16).astype(jnp.float32)
    lane = lax.broadcasted_iota(jnp.int32, value.shape, 1)
    both = jnp.where(lane < chans, high, pltpu.roll(value - high, chans, 1))
    return jnp.where(lane < 2 * chans, both, 0.0).astype(jnp.bfloat16)


def cross_turn_kernel(heads, chans, *refs):
    in_refs, out_refs = refs[:5], refs[5:]
    group = lax.axis_index("fsdp")
    swap = group & 1 != 0
    flips_in = [sign_of(group, s) for s in range(8)]
    flips_out = [flip * sign_of(group, group) for flip in flips_in]
    row_id = lax.broadcasted_iota(jnp.int32, (TAIL, HAD), 0)
    tail = jnp.zeros((TAIL, HAD), jnp.float32)
    for head in range(heads):
        columns = []
        for low in range(0, chans, 16):
            largest = None
            for e in range(2):
                rows = slice((head * 2 + e) * chans + low, (head * 2 + e) * chans + low + 16)
                got = [in_ref[0, rows, :] for in_ref in in_refs[:4]] + [in_refs[4][i, rows, :] for i in range(4)]
                got = from_origins([value.astype(jnp.float32) for value in got], swap)
                outs = butterfly([got[s] * flips_in[s] for s in range(8)])
                for s in range(8):
                    magnitude = jnp.abs(outs[s])
                    largest = magnitude if largest is None else jnp.maximum(largest, magnitude)
                outs = [outs[s] * flips_out[s] for s in range(8)]
                for array, values in enumerate(to_slots(outs, swap)):
                    for slot, value in enumerate(values):
                        out_refs[array][slot, rows, :] = value.astype(jnp.bfloat16)
            columns.append(largest)
        columns.append(jnp.zeros((HAD - chans, HAD), jnp.float32))
        peak = jnp.max(jnp.concatenate(columns, axis=0).T, axis=0, keepdims=True)
        tail = jnp.where(row_id == head, peak, tail)
    tail = split_parts(tail, chans)
    for out_ref in out_refs:
        for slot in range(2):
            out_ref[slot, heads * 2 * chans :, :] = tail


def pairing_offset(core, which, index):
    factor = (index & 1) + 4 * (index >> 1)
    return factor * jnp.where(core == 0, PAIRINGS[0][which], PAIRINGS[1][which])


def spread_kernel(heads, chans, placement_ref, *refs):
    in_refs, out_refs = refs[:5], refs[5:]
    me, core = lax.axis_index("tp"), lax.axis_index("fsdp") & 1
    mine = [placement_ref[me * heads + head] for head in range(heads)]
    blocks = [(in_ref, 0) for in_ref in in_refs[:4]] + [(in_refs[4], index) for index in range(4)]
    peaks = None
    for in_ref, index in blocks:
        part = join_parts(in_ref[index, heads * 2 * chans :, :].astype(jnp.float32), chans)
        peaks = part if peaks is None else jnp.maximum(peaks, part)
    row_id = lax.broadcasted_iota(jnp.int32, (TAIL, HAD), 0)
    span = 2 * chans
    for i, out_ref in enumerate(out_refs):
        for j in range(4):
            owner = me ^ pairing_offset(core, 0, i) ^ pairing_offset(core, 1, j)
            head = 0
            for index in range(1, heads):
                head = jnp.where(mine[index] == owner, index, head)
            rows = pl.ds(pl.multiple_of(head * span, 16), span)
            for s, (in_ref, index) in enumerate(blocks):
                out_ref[j, s * span : (s + 1) * span, :] = in_ref[index, rows, :]
            peak = jnp.sum(jnp.where(row_id == head, peaks, 0.0), axis=0, keepdims=True)
            out_ref[j, 8 * span :, :] = split_parts(jnp.broadcast_to(peak, (TAIL, HAD)), chans)


def pack_kernel(owners, heads, chunk, has_past, placement_ref, *refs):
    first, chans = chunk
    peak_ref, out_ref, buffer, sems, live_ref, slot_ref = refs[-6:]
    past_ref = refs[-8] if has_past else None
    in_refs = refs[: -8 if has_past else -6]
    me, group = lax.axis_index("tp"), lax.axis_index("fsdp")
    count = 0
    for source in range(owners):
        live = 0
        for head in range(heads):
            live = jnp.where(placement_ref[source * heads + head] == me, 1, live)
        live_ref[source] = live
        slot_ref[source] = count
        count = count + live
    lane = lax.broadcasted_iota(jnp.int32, (TAIL, HAD), 1)
    depth = buffer.shape[0]
    copies = [None] * depth
    core = group & 1
    pair = jnp.where(core == 0, 2, 6)
    offsets = (0, 1, pair, pair ^ 1, pair ^ 4, pair ^ 5, 4, 5)
    for origin in range(owners):
        i, j = origin % 4, origin // 4
        in_ref, index = (in_refs[3 + j], i) if j else (in_refs[i], 0)
        source = me ^ pairing_offset(core, 0, i) ^ pairing_offset(core, 1, j)
        part = origin % depth
        if copies[part] is not None:
            copies[part].wait()
        live = live_ref[source] != 0
        slot = jnp.where(live, slot_ref[source], count + source - slot_ref[source])
        tail = in_ref[index, 16 * chans :, :].astype(jnp.float32)
        row = jnp.where((lane < chans) & live, join_parts(tail, chans), 0.0)[:1, :]
        scale = jnp.where(live, 1.0 / (row + 1e-06), 0.0)
        scale = jnp.broadcast_to(scale, (HEAD_DIM, HAD)).T[:chans, :]
        row = pltpu.roll(jnp.broadcast_to(row, (8, HAD)), first, 1)[:1, :] if first else row
        if has_past:
            row = row + past_ref[pl.ds(slot, 1), :]
        peak_ref[pl.ds(slot, 1), :] = row
        for s in range(8):
            for e in range(2):
                start = (s * 2 + e) * chans
                lanes = pl.ds(pl.multiple_of(((group ^ offsets[s]) * 2 + e) * HAD, HAD), HAD)
                block = in_ref[index, start : start + chans, :]
                buffer[part, :, lanes] = (block.astype(jnp.float32) * scale).astype(jnp.bfloat16)
        copies[part] = pltpu.make_async_copy(
            buffer.at[part], out_ref.at[0, slot, first : first + chans, :], sems.at[part]
        )
        copies[part].start()
    for copy in copies:
        copy.wait()


def per_device(qkv_weight, placement):
    rows_local, cols_local = qkv_weight.shape
    heads = cols_local // HEAD_DIM
    owners = lax.axis_size("tp")
    rows_a = rows_local // HAD
    params = pltpu.CompilerParams(vmem_limit_bytes=VMEM_BYTES)
    any_spec = pl.BlockSpec(memory_space=pl.ANY)
    smem_spec = pl.BlockSpec(memory_space=pltpu.SMEM)
    vmem_spec = pl.BlockSpec(memory_space=pltpu.VMEM)

    def call(kernel, name, shapes, *arrays, table=False):
        return pl.pallas_call(
            kernel,
            in_specs=[smem_spec] * table + [vmem_spec] * (len(arrays) - table),
            out_specs=[vmem_spec] * len(shapes),
            out_shape=[jax.ShapeDtypeStruct(shape + (HAD,), jnp.bfloat16) for shape in shapes],
            compiler_params=params,
            name=name,
        )(*arrays)

    signs = jnp.asarray(hadamard_table(HAD), jnp.bfloat16)
    widths = [2 * chans for _, chans in CHUNKS for _ in range(4)]
    turned = pl.pallas_call(
        functools.partial(local_turn_kernel, rows_a),
        grid=(heads,),
        in_specs=[
            pl.BlockSpec((rows_local, HEAD_DIM), lambda h: (0, h)),
            pl.BlockSpec((HAD, HAD), lambda h: (0, 0)),
        ],
        out_specs=[pl.BlockSpec((2, width, HAD), lambda h: (0, h, 0)) for width in widths],
        out_shape=[jax.ShapeDtypeStruct((2, heads * width, HAD), jnp.bfloat16) for width in widths],
        scratch_shapes=[pltpu.VMEM((rows_local, HAD), jnp.float32)],
        compiler_params=params,
        name="local_turn",
    )(qkv_weight, signs)

    state = [turned[4 * index : 4 * index + 4] for index in range(len(CHUNKS))]
    token = None
    past = []

    def tie(arrays):
        if token is None:
            return list(arrays)
        return list(lax.optimization_barrier((list(arrays), token))[0])

    for stage, index in ORDER:
        first, chans = chunk = CHUNKS[index]
        arrays = tie(state[index])
        if stage == "start":
            state[index] = y_first(arrays)
        elif stage == "y_regroup":
            (token,) = call(y_regroup_kernel, stage, [(4,) + arrays[0].shape[1:2]], *arrays)
            state[index] = arrays + [y_second(token)]
        elif stage == "cross":
            shapes = [(2, heads * 2 * chans + TAIL)] * 4
            outs = call(functools.partial(cross_turn_kernel, heads, chans), stage, shapes, *arrays)
            token = outs[0]
            state[index] = y_first(outs)
        elif stage == "spread":
            shapes = [(4, 16 * chans + TAIL)] * 4
            kernel = functools.partial(spread_kernel, heads, chans)
            outs = call(kernel, stage, shapes, placement, *arrays, table=True)
            token = outs[0]
            state[index] = [outs[0]] + owner_hops(outs[1:], 0)
        elif stage == "regroup":
            outs = call(regroup_kernel, stage, [arrays[0].shape[:2]] * 3, *arrays)
            token = outs[0]
            state[index] = arrays + owner_hops(outs, 1)
        else:
            past = pl.pallas_call(
                functools.partial(pack_kernel, owners, heads, chunk, bool(past)),
                in_specs=[smem_spec] + [vmem_spec] * len(arrays) + ([vmem_spec, any_spec] if past else []),
                out_specs=[vmem_spec, any_spec],
                out_shape=[
                    jax.ShapeDtypeStruct((owners, HEAD_DIM), jnp.float32),
                    jax.ShapeDtypeStruct((1, owners, HEAD_DIM, rows_local), jnp.bfloat16),
                ],
                scratch_shapes=[
                    pltpu.VMEM((3, chans, rows_local), jnp.bfloat16),
                    pltpu.SemaphoreType.DMA((3,)),
                    pltpu.SMEM((owners,), jnp.int32),
                    pltpu.SMEM((owners,), jnp.int32),
                ],
                input_output_aliases={2 + len(arrays): 1} if past else {},
                compiler_params=params,
                name="pack",
            )(placement, *arrays, *past)
            token = past[0]
    peaks, packed = past
    return packed, peaks[None]


def solution(mesh):
    in_specs = (P("fsdp", "tp"), P())
    out_specs = (P("tp", None, None, "fsdp"), P("tp", None, None))
    return jax.shard_map(
        per_device, mesh=mesh, in_specs=in_specs, out_specs=out_specs, check_vma=False
    )
```

```python
import functools

import numpy as np
import jax
import jax.numpy as jnp
from jax import lax
from jax.experimental import pallas as pl
from jax.experimental.pallas import tpu as pltpu
from jax.sharding import PartitionSpec as P

HEAD_DIM = 128
HAD = 128
CHUNKS = ((0, 32), (32, 32), (64, 32), (96, 32))
ORDER = (
    ("start", 0),
    ("start", 1),
    ("start", 2),
    ("y_regroup", 0),
    ("start", 3),
    ("cross", 0),
    ("y_regroup", 1),
    ("y_regroup", 0),
    ("cross", 1),
    ("spread", 0),
    ("y_regroup", 1),
    ("y_regroup", 2),
    ("regroup", 0),
    ("spread", 1),
    ("y_regroup", 3),
    ("cross", 2),
    ("cross", 3),
    ("y_regroup", 2),
    ("pack", 0),
    ("regroup", 1),
    ("y_regroup", 3),
    ("spread", 2),
    ("spread", 3),
    ("pack", 1),
    ("regroup", 2),
    ("regroup", 3),
    ("pack", 2),
    ("pack", 3),
)
TAIL = 16
VMEM_BYTES = 12 * 1024 * 1024
BOTH = ("fsdp", "tp")


def hadamard_table(order):
    matrix = np.ones((1, 1), np.float32)
    while matrix.shape[0] < order:
        matrix = np.block([[matrix, matrix], [matrix, -matrix]])
    return matrix


def butterfly(values):
    values = list(values)
    half = 1
    while half < len(values):
        for low in range(len(values)):
            if not low & half:
                first, second = values[low], values[low + half]
                values[low], values[low + half] = first + second, first - second
        half *= 2
    return values


PAIRINGS = ((1, 3), (3, 1))


def hop(array, rule):
    groups, owners = lax.axis_size("fsdp"), lax.axis_size("tp")
    pairs = []
    for f in range(groups):
        for t in range(owners):
            to_f, to_t = rule(f, t)
            pairs.append((f * owners + t, to_f * owners + to_t))
    return lax.ppermute(array, BOTH, pairs)


def y_first(blocks):
    own, core, pair, both = blocks
    pair = hop(pair, lambda f, t: (f ^ 2 * PAIRINGS[f & 1][0], t))
    both = hop(both, lambda f, t: (f ^ 1 ^ 2 * PAIRINGS[1 - (f & 1)][0], t))
    core = hop(core, lambda f, t: (f ^ 1, t))
    return [own, core, pair, both]


def y_second(payload):
    return hop(payload, lambda f, t: (f ^ 2 * PAIRINGS[f & 1][1], t))


def owner_hops(blocks, which):
    out = [None] * 3
    for place in (2, 0, 1):
        factor = (1, 4, 5)[place]
        out[place] = hop(blocks[place], lambda f, t: (f, t ^ factor * PAIRINGS[f & 1][which]))
    return out


def to_slots(values, swap):
    return (
        (values[0], jnp.where(swap, values[2], values[6])),
        (values[1], jnp.where(swap, values[7], values[3])),
        (jnp.where(swap, values[6], values[2]), values[4]),
        (jnp.where(swap, values[3], values[7]), values[5]),
    )


def from_origins(values, swap):
    return (
        values[0],
        values[1],
        jnp.where(swap, values[4], values[2]),
        jnp.where(swap, values[5], values[3]),
        values[6],
        values[7],
        jnp.where(swap, values[2], values[4]),
        jnp.where(swap, values[3], values[5]),
    )


def y_regroup_kernel(*refs):
    for index, in_ref in enumerate(refs[:4]):
        refs[4][index] = in_ref[1]


def regroup_kernel(*refs):
    in_refs, out_refs = refs[:4], refs[4:]
    for slot, out_ref in enumerate(out_refs):
        for index, in_ref in enumerate(in_refs):
            out_ref[index] = in_ref[slot + 1]


def sign_of(value, bits):
    both = value & bits
    both = both ^ (both >> 2)
    both = both ^ (both >> 1)
    return (1 - 2 * (both & 1)).astype(jnp.float32)


def local_turn_kernel(rows_a, weight_ref, signs_ref, *refs):
    out_refs, turned = refs[:-1], refs[-1]
    group = lax.axis_index("fsdp")
    swap = group & 1 != 0
    flips = [sign_of(group, a >> 1) * (1.0 / HAD) for a in range(rows_a)]
    columns = jnp.concatenate([weight_ref[a * HAD : (a + 1) * HAD, :].T for a in range(rows_a)], axis=0)
    turned[...] = jnp.dot(columns, signs_ref[...], preferred_element_type=jnp.float32)
    for index, (first, chans) in enumerate(CHUNKS):
        for low in range(0, chans, 16):
            outs = []
            for a in range(rows_a):
                start = a * HEAD_DIM + first + low
                outs.append(turned[start : start + 16, :] * flips[a])
            outs = butterfly(outs)
            for e in range(2):
                row = e * chans + low
                for array, values in enumerate(to_slots(outs[e::2], swap)):
                    for slot, value in enumerate(values):
                        out_refs[4 * index + array][slot, row : row + 16, :] = value.astype(jnp.bfloat16)


def join_parts(value, chans):
    return value + pltpu.roll(value, HAD - chans, 1)


def split_parts(value, chans):
    high = value.astype(jnp.bfloat16).astype(jnp.float32)
    lane = lax.broadcasted_iota(jnp.int32, value.shape, 1)
    both = jnp.where(lane < chans, high, pltpu.roll(value - high, chans, 1))
    return jnp.where(lane < 2 * chans, both, 0.0).astype(jnp.bfloat16)


def cross_turn_kernel(heads, chans, *refs):
    in_refs, out_refs = refs[:5], refs[5:]
    group = lax.axis_index("fsdp")
    swap = group & 1 != 0
    flips_in = [sign_of(group, s) for s in range(8)]
    flips_out = [flip * sign_of(group, group) for flip in flips_in]
    row_id = lax.broadcasted_iota(jnp.int32, (TAIL, HAD), 0)
    tail = jnp.zeros((TAIL, HAD), jnp.float32)
    for head in range(heads):
        columns = []
        for low in range(0, chans, 16):
            largest = None
            for e in range(2):
                rows = slice((head * 2 + e) * chans + low, (head * 2 + e) * chans + low + 16)
                got = [in_ref[0, rows, :] for in_ref in in_refs[:4]] + [in_refs[4][i, rows, :] for i in range(4)]
                got = from_origins([value.astype(jnp.float32) for value in got], swap)
                outs = butterfly([got[s] * flips_in[s] for s in range(8)])
                for s in range(8):
                    magnitude = jnp.abs(outs[s])
                    largest = magnitude if largest is None else jnp.maximum(largest, magnitude)
                outs = [outs[s] * flips_out[s] for s in range(8)]
                for array, values in enumerate(to_slots(outs, swap)):
                    for slot, value in enumerate(values):
                        out_refs[array][slot, rows, :] = value.astype(jnp.bfloat16)
            columns.append(largest)
        columns.append(jnp.zeros((HAD - chans, HAD), jnp.float32))
        peak = jnp.max(jnp.concatenate(columns, axis=0).T, axis=0, keepdims=True)
        tail = jnp.where(row_id == head, peak, tail)
    tail = split_parts(tail, chans)
    for out_ref in out_refs:
        for slot in range(2):
            out_ref[slot, heads * 2 * chans :, :] = tail


def pairing_offset(core, which, index):
    factor = (index & 1) + 4 * (index >> 1)
    return factor * jnp.where(core == 0, PAIRINGS[0][which], PAIRINGS[1][which])


def spread_kernel(heads, chans, placement_ref, *refs):
    in_refs, out_refs = refs[:5], refs[5:]
    me, core = lax.axis_index("tp"), lax.axis_index("fsdp") & 1
    mine = [placement_ref[me * heads + head] for head in range(heads)]
    blocks = [(in_ref, 0) for in_ref in in_refs[:4]] + [(in_refs[4], index) for index in range(4)]
    peaks = None
    for in_ref, index in blocks:
        part = join_parts(in_ref[index, heads * 2 * chans :, :].astype(jnp.float32), chans)
        peaks = part if peaks is None else jnp.maximum(peaks, part)
    row_id = lax.broadcasted_iota(jnp.int32, (TAIL, HAD), 0)
    span = 2 * chans
    for i, out_ref in enumerate(out_refs):
        for j in range(4):
            owner = me ^ pairing_offset(core, 0, i) ^ pairing_offset(core, 1, j)
            head = 0
            for index in range(1, heads):
                head = jnp.where(mine[index] == owner, index, head)
            rows = pl.ds(pl.multiple_of(head * span, 16), span)
            for s, (in_ref, index) in enumerate(blocks):
                out_ref[j, s * span : (s + 1) * span, :] = in_ref[index, rows, :]
            peak = jnp.sum(jnp.where(row_id == head, peaks, 0.0), axis=0, keepdims=True)
            out_ref[j, 8 * span :, :] = split_parts(jnp.broadcast_to(peak, (TAIL, HAD)), chans)


def pack_kernel(owners, heads, chunk, has_past, placement_ref, *refs):
    first, chans = chunk
    peak_ref, out_ref, buffer, sems, live_ref, slot_ref = refs[-6:]
    past_ref = refs[-8] if has_past else None
    in_refs = refs[: -8 if has_past else -6]
    me, group = lax.axis_index("tp"), lax.axis_index("fsdp")
    count = 0
    for source in range(owners):
        live = 0
        for head in range(heads):
            live = jnp.where(placement_ref[source * heads + head] == me, 1, live)
        live_ref[source] = live
        slot_ref[source] = count
        count = count + live
    lane = lax.broadcasted_iota(jnp.int32, (TAIL, HAD), 1)
    depth = buffer.shape[0]
    copies = [None] * depth
    core = group & 1
    pair = jnp.where(core == 0, 2, 6)
    offsets = (0, 1, pair, pair ^ 1, pair ^ 4, pair ^ 5, 4, 5)
    blocks, rows = [], []
    for origin in range(owners):
        i, j = origin % 4, origin // 4
        in_ref, index = (in_refs[3 + j], i) if j else (in_refs[i], 0)
        source = me ^ pairing_offset(core, 0, i) ^ pairing_offset(core, 1, j)
        live = live_ref[source] != 0
        slot = jnp.where(live, slot_ref[source], count + source - slot_ref[source])
        tail = in_ref[index, 16 * chans :, :].astype(jnp.float32)
        row = jnp.where((lane < chans) & live, join_parts(tail, chans), 0.0)
        rows.append(jnp.where(live, 1.0 / (row[:1, :] + 1e-06), 0.0))
        row = (pltpu.roll(row, first, 1) if first else row)[:1, :]
        if has_past:
            row = row + past_ref[pl.ds(slot, 1), :]
        peak_ref[pl.ds(slot, 1), :] = row
        blocks.append((in_ref, index, slot))
    rows.append(jnp.zeros((HAD - owners, HAD), jnp.float32))
    scales = jnp.concatenate(rows, axis=0).T
    for origin, (in_ref, index, slot) in enumerate(blocks):
        part = origin % depth
        if copies[part] is not None:
            copies[part].wait()
        scale = scales[:chans, origin : origin + 1]
        for s in range(8):
            for e in range(2):
                start = (s * 2 + e) * chans
                lanes = pl.ds(pl.multiple_of(((group ^ offsets[s]) * 2 + e) * HAD, HAD), HAD)
                block = in_ref[index, start : start + chans, :]
                buffer[part, :, lanes] = (block.astype(jnp.float32) * scale).astype(jnp.bfloat16)
        copies[part] = pltpu.make_async_copy(
            buffer.at[part], out_ref.at[0, slot, first : first + chans, :], sems.at[part]
        )
        copies[part].start()
    for copy in copies:
        copy.wait()


def per_device(qkv_weight, placement):
    rows_local, cols_local = qkv_weight.shape
    heads = cols_local // HEAD_DIM
    owners = lax.axis_size("tp")
    rows_a = rows_local // HAD
    params = pltpu.CompilerParams(vmem_limit_bytes=VMEM_BYTES)
    any_spec = pl.BlockSpec(memory_space=pl.ANY)
    smem_spec = pl.BlockSpec(memory_space=pltpu.SMEM)
    vmem_spec = pl.BlockSpec(memory_space=pltpu.VMEM)

    def call(kernel, name, shapes, *arrays, table=False):
        return pl.pallas_call(
            kernel,
            in_specs=[smem_spec] * table + [vmem_spec] * (len(arrays) - table),
            out_specs=[vmem_spec] * len(shapes),
            out_shape=[jax.ShapeDtypeStruct(shape + (HAD,), jnp.bfloat16) for shape in shapes],
            compiler_params=params,
            name=name,
        )(*arrays)

    signs = jnp.asarray(hadamard_table(HAD), jnp.bfloat16)
    widths = [2 * chans for _, chans in CHUNKS for _ in range(4)]
    turned = pl.pallas_call(
        functools.partial(local_turn_kernel, rows_a),
        grid=(heads,),
        in_specs=[
            pl.BlockSpec((rows_local, HEAD_DIM), lambda h: (0, h)),
            pl.BlockSpec((HAD, HAD), lambda h: (0, 0)),
        ],
        out_specs=[pl.BlockSpec((2, width, HAD), lambda h: (0, h, 0)) for width in widths],
        out_shape=[jax.ShapeDtypeStruct((2, heads * width, HAD), jnp.bfloat16) for width in widths],
        scratch_shapes=[pltpu.VMEM((rows_local, HAD), jnp.float32)],
        compiler_params=params,
        name="local_turn",
    )(qkv_weight, signs)

    state = [turned[4 * index : 4 * index + 4] for index in range(len(CHUNKS))]
    token = None
    past = []

    def tie(arrays):
        if token is None:
            return list(arrays)
        return list(lax.optimization_barrier((list(arrays), token))[0])

    for stage, index in ORDER:
        first, chans = chunk = CHUNKS[index]
        arrays = tie(state[index])
        if stage == "start":
            state[index] = y_first(arrays)
        elif stage == "y_regroup":
            (token,) = call(y_regroup_kernel, stage, [(4,) + arrays[0].shape[1:2]], *arrays)
            state[index] = arrays + [y_second(token)]
        elif stage == "cross":
            shapes = [(2, heads * 2 * chans + TAIL)] * 4
            outs = call(functools.partial(cross_turn_kernel, heads, chans), stage, shapes, *arrays)
            token = outs[0]
            state[index] = y_first(outs)
        elif stage == "spread":
            shapes = [(4, 16 * chans + TAIL)] * 4
            kernel = functools.partial(spread_kernel, heads, chans)
            outs = call(kernel, stage, shapes, placement, *arrays, table=True)
            token = outs[0]
            state[index] = [outs[0]] + owner_hops(outs[1:], 0)
        elif stage == "regroup":
            outs = call(regroup_kernel, stage, [arrays[0].shape[:2]] * 3, *arrays)
            token = outs[0]
            state[index] = arrays + owner_hops(outs, 1)
        else:
            past = pl.pallas_call(
                functools.partial(pack_kernel, owners, heads, chunk, bool(past)),
                in_specs=[smem_spec] + [vmem_spec] * len(arrays) + ([vmem_spec, any_spec] if past else []),
                out_specs=[vmem_spec, any_spec],
                out_shape=[
                    jax.ShapeDtypeStruct((owners, HEAD_DIM), jnp.float32),
                    jax.ShapeDtypeStruct((1, owners, HEAD_DIM, rows_local), jnp.bfloat16),
                ],
                scratch_shapes=[
                    pltpu.VMEM((3, chans, rows_local), jnp.bfloat16),
                    pltpu.SemaphoreType.DMA((3,)),
                    pltpu.SMEM((owners,), jnp.int32),
                    pltpu.SMEM((owners,), jnp.int32),
                ],
                input_output_aliases={2 + len(arrays): 1} if past else {},
                compiler_params=params,
                name="pack",
            )(placement, *arrays, *past)
            token = past[0]
    peaks, packed = past
    return packed, peaks[None]


def solution(mesh):
    in_specs = (P("fsdp", "tp"), P())
    out_specs = (P("tp", None, None, "fsdp"), P("tp", None, None))
    return jax.shard_map(
        per_device, mesh=mesh, in_specs=in_specs, out_specs=out_specs, check_vma=False
    )
```

```python
import functools

import numpy as np
import jax
import jax.numpy as jnp
from jax import lax
from jax.experimental import pallas as pl
from jax.experimental.pallas import tpu as pltpu
from jax.sharding import PartitionSpec as P

HEAD_DIM = 128
HAD = 128
CHUNKS = ((0, 48), (48, 48), (96, 32))
DIRECT = 1
ORDER = (
    ("start", 0),
    ("y_regroup", 0),
    ("start", 1),
    ("cross", 0),
    ("y_regroup", 1),
    ("y_regroup", 0),
    ("start", 2),
    ("cross", 1),
    ("spread", 0),
    ("y_regroup", 1),
    ("y_regroup", 2),
    ("cross", 2),
    ("spread", 1),
    ("y_regroup", 2),
    ("regroup", 1),
    ("spread", 2),
    ("pack", 0),
    ("regroup", 2),
    ("pack", 1),
    ("pack", 2),
)
TAIL = 16
VMEM_BYTES = 12 * 1024 * 1024
BOTH = ("fsdp", "tp")


def hadamard_table(order):
    matrix = np.ones((1, 1), np.float32)
    while matrix.shape[0] < order:
        matrix = np.block([[matrix, matrix], [matrix, -matrix]])
    return matrix


def butterfly(values):
    values = list(values)
    half = 1
    while half < len(values):
        for low in range(len(values)):
            if not low & half:
                first, second = values[low], values[low + half]
                values[low], values[low + half] = first + second, first - second
        half *= 2
    return values


PAIRINGS = ((1, 3), (3, 1))


def hop(array, rule):
    groups, owners = lax.axis_size("fsdp"), lax.axis_size("tp")
    pairs = []
    for f in range(groups):
        for t in range(owners):
            to_f, to_t = rule(f, t)
            pairs.append((f * owners + t, to_f * owners + to_t))
    return lax.ppermute(array, BOTH, pairs)


def y_first(blocks):
    own, core, pair, both = blocks
    pair = hop(pair, lambda f, t: (f ^ 2 * PAIRINGS[f & 1][0], t))
    both = hop(both, lambda f, t: (f ^ 1 ^ 2 * PAIRINGS[1 - (f & 1)][0], t))
    core = hop(core, lambda f, t: (f ^ 1, t))
    return [own, core, pair, both]


def y_second(payload):
    return hop(payload, lambda f, t: (f ^ 2 * PAIRINGS[f & 1][1], t))


def owner_hops(blocks, which):
    out = [None] * 3
    for place in (2, 0, 1):
        factor = (1, 4, 5)[place]
        out[place] = hop(blocks[place], lambda f, t: (f, t ^ factor * PAIRINGS[f & 1][which]))
    return out


def to_slots(values, swap):
    return (
        (values[0], jnp.where(swap, values[2], values[6])),
        (values[1], jnp.where(swap, values[7], values[3])),
        (jnp.where(swap, values[6], values[2]), values[4]),
        (jnp.where(swap, values[3], values[7]), values[5]),
    )


def from_origins(values, swap):
    return (
        values[0],
        values[1],
        jnp.where(swap, values[4], values[2]),
        jnp.where(swap, values[5], values[3]),
        values[6],
        values[7],
        jnp.where(swap, values[2], values[4]),
        jnp.where(swap, values[3], values[5]),
    )


def y_regroup_kernel(*refs):
    for index, in_ref in enumerate(refs[:4]):
        refs[4][index] = in_ref[1]


def regroup_kernel(*refs):
    in_refs, out_refs = refs[:4], refs[4:]
    for slot, out_ref in enumerate(out_refs):
        for index, in_ref in enumerate(in_refs):
            out_ref[index] = in_ref[slot + 1]


def sign_of(value, bits):
    both = value & bits
    both = both ^ (both >> 2)
    both = both ^ (both >> 1)
    return (1 - 2 * (both & 1)).astype(jnp.float32)


def local_turn_kernel(rows_a, weight_ref, signs_ref, *refs):
    out_refs, turned = refs[:-1], refs[-1]
    group = lax.axis_index("fsdp")
    swap = group & 1 != 0
    flips = [sign_of(group, a >> 1) * (1.0 / HAD) for a in range(rows_a)]
    columns = jnp.concatenate([weight_ref[a * HAD : (a + 1) * HAD, :].T for a in range(rows_a)], axis=0)
    turned[...] = jnp.dot(columns, signs_ref[...], preferred_element_type=jnp.float32)
    for index, (first, chans) in enumerate(CHUNKS):
        for low in range(0, chans, 16):
            outs = []
            for a in range(rows_a):
                start = a * HEAD_DIM + first + low
                outs.append(turned[start : start + 16, :] * flips[a])
            outs = butterfly(outs)
            for e in range(2):
                row = e * chans + low
                for array, values in enumerate(to_slots(outs[e::2], swap)):
                    for slot, value in enumerate(values):
                        out_refs[4 * index + array][slot, row : row + 16, :] = value.astype(jnp.bfloat16)


def join_parts(value, chans):
    return value + pltpu.roll(value, HAD - chans, 1)


def split_parts(value, chans):
    high = value.astype(jnp.bfloat16).astype(jnp.float32)
    lane = lax.broadcasted_iota(jnp.int32, value.shape, 1)
    both = jnp.where(lane < chans, high, pltpu.roll(value - high, chans, 1))
    return jnp.where(lane < 2 * chans, both, 0.0).astype(jnp.bfloat16)


def cross_turn_kernel(heads, chans, *refs):
    in_refs, out_refs = refs[:5], refs[5:]
    group = lax.axis_index("fsdp")
    swap = group & 1 != 0
    flips_in = [sign_of(group, s) for s in range(8)]
    flips_out = [flip * sign_of(group, group) for flip in flips_in]
    row_id = lax.broadcasted_iota(jnp.int32, (TAIL, HAD), 0)
    tail = jnp.zeros((TAIL, HAD), jnp.float32)
    for head in range(heads):
        columns = []
        for low in range(0, chans, 16):
            largest = None
            for e in range(2):
                rows = slice((head * 2 + e) * chans + low, (head * 2 + e) * chans + low + 16)
                got = [in_ref[0, rows, :] for in_ref in in_refs[:4]] + [in_refs[4][i, rows, :] for i in range(4)]
                got = from_origins([value.astype(jnp.float32) for value in got], swap)
                outs = butterfly([got[s] * flips_in[s] for s in range(8)])
                for s in range(8):
                    magnitude = jnp.abs(outs[s])
                    largest = magnitude if largest is None else jnp.maximum(largest, magnitude)
                outs = [outs[s] * flips_out[s] for s in range(8)]
                for array, values in enumerate(to_slots(outs, swap)):
                    for slot, value in enumerate(values):
                        out_refs[array][slot, rows, :] = value.astype(jnp.bfloat16)
            columns.append(largest)
        columns.append(jnp.zeros((HAD - chans, HAD), jnp.float32))
        peak = jnp.max(jnp.concatenate(columns, axis=0).T, axis=0, keepdims=True)
        tail = jnp.where(row_id == head, peak, tail)
    tail = split_parts(tail, chans)
    for out_ref in out_refs:
        for slot in range(2):
            out_ref[slot, heads * 2 * chans :, :] = tail


def pairing_offset(core, which, index):
    factor = (index & 1) + 4 * (index >> 1)
    return factor * jnp.where(core == 0, PAIRINGS[0][which], PAIRINGS[1][which])


def spread_kernel(heads, chans, placement_ref, *refs):
    in_refs, out_refs = refs[:5], refs[5:]
    me, core = lax.axis_index("tp"), lax.axis_index("fsdp") & 1
    mine = [placement_ref[me * heads + head] for head in range(heads)]
    blocks = [(in_ref, 0) for in_ref in in_refs[:4]] + [(in_refs[4], index) for index in range(4)]
    peaks = None
    for in_ref, index in blocks:
        part = join_parts(in_ref[index, heads * 2 * chans :, :].astype(jnp.float32), chans)
        peaks = part if peaks is None else jnp.maximum(peaks, part)
    row_id = lax.broadcasted_iota(jnp.int32, (TAIL, HAD), 0)
    span = 2 * chans
    direct = len(out_refs) == 1
    for i in range(4):
        for j in range(4):
            owner = 4 * i + j if direct else me ^ pairing_offset(core, 0, i) ^ pairing_offset(core, 1, j)
            out_ref, to = (out_refs[0], 4 * i + j) if direct else (out_refs[i], j)
            head = 0
            for index in range(1, heads):
                head = jnp.where(mine[index] == owner, index, head)
            rows = pl.ds(pl.multiple_of(head * span, 16), span)
            for s, (in_ref, index) in enumerate(blocks):
                out_ref[to, s * span : (s + 1) * span, :] = in_ref[index, rows, :]
            peak = jnp.sum(jnp.where(row_id == head, peaks, 0.0), axis=0, keepdims=True)
            out_ref[to, 8 * span :, :] = split_parts(jnp.broadcast_to(peak, (TAIL, HAD)), chans)


def pack_kernel(owners, heads, chunk, has_past, placement_ref, *refs):
    first, chans = chunk
    peak_ref, out_ref, buffer, sems, live_ref, slot_ref = refs[-6:]
    past_ref = refs[-8] if has_past else None
    in_refs = refs[: -8 if has_past else -6]
    me, group = lax.axis_index("tp"), lax.axis_index("fsdp")
    count = 0
    for source in range(owners):
        live = 0
        for head in range(heads):
            live = jnp.where(placement_ref[source * heads + head] == me, 1, live)
        live_ref[source] = live
        slot_ref[source] = count
        count = count + live
    lane = lax.broadcasted_iota(jnp.int32, (TAIL, HAD), 1)
    copies = []
    core = group & 1
    pair = jnp.where(core == 0, 2, 6)
    offsets = (0, 1, pair, pair ^ 1, pair ^ 4, pair ^ 5, 4, 5)
    blocks, rows = [], []
    for origin in range(owners):
        i, j = origin % 4, origin // 4
        if len(in_refs) == 1:
            in_ref, index, source = in_refs[0], origin, origin
        else:
            in_ref, index = (in_refs[3 + j], i) if j else (in_refs[i], 0)
            source = me ^ pairing_offset(core, 0, i) ^ pairing_offset(core, 1, j)
        live = live_ref[source] != 0
        slot = jnp.where(live, slot_ref[source], count + source - slot_ref[source])
        tail = in_ref[index, 16 * chans :, :].astype(jnp.float32)
        row = jnp.where((lane < chans) & live, join_parts(tail, chans), 0.0)
        rows.append(jnp.where(live, 1.0 / (row[:1, :] + 1e-06), 0.0))
        row = (pltpu.roll(row, first, 1) if first else row)[:1, :]
        if has_past:
            row = row + past_ref[pl.ds(slot, 1), :]
        peak_ref[pl.ds(slot, 1), :] = row
        blocks.append((in_ref, index, slot))
    rows.append(jnp.zeros((HAD - owners, HAD), jnp.float32))
    scales = jnp.concatenate(rows, axis=0).T
    for origin, (in_ref, index, slot) in enumerate(blocks):
        scale = scales[:chans, origin : origin + 1]
        for s in range(8):
            for e in range(2):
                start = (s * 2 + e) * chans
                lanes = pl.ds(pl.multiple_of(((group ^ offsets[s]) * 2 + e) * HAD, HAD), HAD)
                block = in_ref[index, start : start + chans, :]
                buffer[origin, :, lanes] = (block.astype(jnp.float32) * scale).astype(jnp.bfloat16)
        rows = out_ref.at[0, slot, first : first + chans, :]
        copies.append(pltpu.make_async_copy(buffer.at[origin], rows, sems.at[origin]))
        copies[-1].start()
    for copy in copies:
        copy.wait()


def per_device(qkv_weight, placement):
    rows_local, cols_local = qkv_weight.shape
    heads = cols_local // HEAD_DIM
    owners = lax.axis_size("tp")
    rows_a = rows_local // HAD
    params = pltpu.CompilerParams(vmem_limit_bytes=VMEM_BYTES)
    any_spec = pl.BlockSpec(memory_space=pl.ANY)
    smem_spec = pl.BlockSpec(memory_space=pltpu.SMEM)
    vmem_spec = pl.BlockSpec(memory_space=pltpu.VMEM)

    def call(kernel, name, shapes, *arrays, table=False):
        return pl.pallas_call(
            kernel,
            in_specs=[smem_spec] * table + [vmem_spec] * (len(arrays) - table),
            out_specs=[vmem_spec] * len(shapes),
            out_shape=[jax.ShapeDtypeStruct(shape + (HAD,), jnp.bfloat16) for shape in shapes],
            compiler_params=params,
            name=name,
        )(*arrays)

    signs = jnp.asarray(hadamard_table(HAD), jnp.bfloat16)
    widths = [2 * chans for _, chans in CHUNKS for _ in range(4)]
    turned = pl.pallas_call(
        functools.partial(local_turn_kernel, rows_a),
        grid=(heads,),
        in_specs=[
            pl.BlockSpec((rows_local, HEAD_DIM), lambda h: (0, h)),
            pl.BlockSpec((HAD, HAD), lambda h: (0, 0)),
        ],
        out_specs=[pl.BlockSpec((2, width, HAD), lambda h: (0, h, 0)) for width in widths],
        out_shape=[jax.ShapeDtypeStruct((2, heads * width, HAD), jnp.bfloat16) for width in widths],
        scratch_shapes=[pltpu.VMEM((rows_local, HAD), jnp.float32)],
        compiler_params=params,
        name="local_turn",
    )(qkv_weight, signs)

    state = [turned[4 * index : 4 * index + 4] for index in range(len(CHUNKS))]
    token = None
    past = []

    def tie(arrays):
        if token is None:
            return list(arrays)
        return list(lax.optimization_barrier((list(arrays), token))[0])

    for stage, index in ORDER:
        first, chans = chunk = CHUNKS[index]
        arrays = tie(state[index])
        if stage == "start":
            state[index] = y_first(arrays)
        elif stage == "y_regroup":
            (token,) = call(y_regroup_kernel, stage, [(4,) + arrays[0].shape[1:2]], *arrays)
            state[index] = arrays + [y_second(token)]
        elif stage == "cross":
            shapes = [(2, heads * 2 * chans + TAIL)] * 4
            outs = call(functools.partial(cross_turn_kernel, heads, chans), stage, shapes, *arrays)
            token = outs[0]
            state[index] = y_first(outs)
        elif stage == "spread":
            direct = index < DIRECT
            shapes = [(owners, 16 * chans + TAIL)] if direct else [(4, 16 * chans + TAIL)] * 4
            kernel = functools.partial(spread_kernel, heads, chans)
            outs = call(kernel, stage, shapes, placement, *arrays, table=True)
            token = outs[0]
            if direct:
                state[index] = [lax.all_to_all(token, "tp", split_axis=0, concat_axis=0, tiled=True)]
            else:
                state[index] = [token] + owner_hops(outs[1:], 0)
        elif stage == "regroup":
            outs = call(regroup_kernel, stage, [arrays[0].shape[:2]] * 3, *arrays)
            token = outs[0]
            state[index] = arrays + owner_hops(outs, 1)
        else:
            past = pl.pallas_call(
                functools.partial(pack_kernel, owners, heads, chunk, bool(past)),
                in_specs=[smem_spec] + [vmem_spec] * len(arrays) + ([vmem_spec, any_spec] if past else []),
                out_specs=[vmem_spec, any_spec],
                out_shape=[
                    jax.ShapeDtypeStruct((owners, HEAD_DIM), jnp.float32),
                    jax.ShapeDtypeStruct((1, owners, HEAD_DIM, rows_local), jnp.bfloat16),
                ],
                scratch_shapes=[
                    pltpu.VMEM((owners, chans, rows_local), jnp.bfloat16),
                    pltpu.SemaphoreType.DMA((owners,)),
                    pltpu.SMEM((owners,), jnp.int32),
                    pltpu.SMEM((owners,), jnp.int32),
                ],
                input_output_aliases={2 + len(arrays): 1} if past else {},
                compiler_params=params,
                name="pack",
            )(placement, *arrays, *past)
            token = past[0]
    peaks, packed = past
    return packed, peaks[None]


def solution(mesh):
    in_specs = (P("fsdp", "tp"), P())
    out_specs = (P("tp", None, None, "fsdp"), P("tp", None, None))
    return jax.shard_map(
        per_device, mesh=mesh, in_specs=in_specs, out_specs=out_specs, check_vma=False
    )
```

```python
import functools

import numpy as np
import jax
import jax.numpy as jnp
from jax import lax
from jax.experimental import pallas as pl
from jax.experimental.pallas import tpu as pltpu
from jax.sharding import PartitionSpec as P

HEAD_DIM = 128
HAD = 128
CHUNKS = ((0, 32), (32, 48), (80, 48))
DIRECT = 0
ORDER = (
    ("start", 0),
    ("start", 1),
    ("y_regroup", 0),
    ("cross", 0, 1),
    ("y_regroup", 0),
    ("y_regroup", 1),
    ("spread", 0),
    ("cross", 1),
    ("start", 2),
    ("regroup", 0, 2),
    ("y_regroup", 2),
    ("y_regroup", 1),
    ("cross", 2),
    ("y_regroup", 2),
    ("spread", 1),
    ("pack", 0),
    ("spread", 2),
    ("regroup", 1),
    ("regroup", 2),
    ("pack", 1),
    ("pack", 2),
)
TAIL = 16
VMEM_BYTES = 12 * 1024 * 1024
BOTH = ("fsdp", "tp")


def hadamard_table(order):
    matrix = np.ones((1, 1), np.float32)
    while matrix.shape[0] < order:
        matrix = np.block([[matrix, matrix], [matrix, -matrix]])
    return matrix


def butterfly(values):
    values = list(values)
    half = 1
    while half < len(values):
        for low in range(len(values)):
            if not low & half:
                first, second = values[low], values[low + half]
                values[low], values[low + half] = first + second, first - second
        half *= 2
    return values


PAIRINGS = ((1, 3), (3, 1))


def hop(array, rule):
    groups, owners = lax.axis_size("fsdp"), lax.axis_size("tp")
    pairs = []
    for f in range(groups):
        for t in range(owners):
            to_f, to_t = rule(f, t)
            pairs.append((f * owners + t, to_f * owners + to_t))
    return lax.ppermute(array, BOTH, pairs)


def y_first(blocks):
    own, core, pair, both = blocks
    pair = hop(pair, lambda f, t: (f ^ 2 * PAIRINGS[f & 1][0], t))
    both = hop(both, lambda f, t: (f ^ 1 ^ 2 * PAIRINGS[1 - (f & 1)][0], t))
    core = hop(core, lambda f, t: (f ^ 1, t))
    return [own, core, pair, both]


def y_second(payload):
    return hop(payload, lambda f, t: (f ^ 2 * PAIRINGS[f & 1][1], t))


def owner_hops(blocks, which):
    out = [None] * 3
    for place in (2, 0, 1):
        factor = (1, 4, 5)[place]
        out[place] = hop(blocks[place], lambda f, t: (f, t ^ factor * PAIRINGS[f & 1][which]))
    return out


def to_slots(values, swap):
    return (
        (values[0], jnp.where(swap, values[2], values[6])),
        (values[1], jnp.where(swap, values[7], values[3])),
        (jnp.where(swap, values[6], values[2]), values[4]),
        (jnp.where(swap, values[3], values[7]), values[5]),
    )


def from_origins(values, swap):
    return (
        values[0],
        values[1],
        jnp.where(swap, values[4], values[2]),
        jnp.where(swap, values[5], values[3]),
        values[6],
        values[7],
        jnp.where(swap, values[2], values[4]),
        jnp.where(swap, values[3], values[5]),
    )


def y_regroup_kernel(*refs):
    for index, in_ref in enumerate(refs[:4]):
        refs[4][index] = in_ref[1]


def regroup_kernel(*refs):
    in_refs, out_refs = refs[:4], refs[4:]
    for slot, out_ref in enumerate(out_refs):
        for index, in_ref in enumerate(in_refs):
            out_ref[index] = in_ref[slot + 1]


def sign_of(value, bits):
    both = value & bits
    both = both ^ (both >> 2)
    both = both ^ (both >> 1)
    return (1 - 2 * (both & 1)).astype(jnp.float32)


def local_turn_kernel(rows_a, weight_ref, signs_ref, *refs):
    out_refs, turned = refs[:-1], refs[-1]
    group = lax.axis_index("fsdp")
    swap = group & 1 != 0
    flips = [sign_of(group, a >> 1) * (1.0 / HAD) for a in range(rows_a)]
    columns = jnp.concatenate([weight_ref[a * HAD : (a + 1) * HAD, :].T for a in range(rows_a)], axis=0)
    turned[...] = jnp.dot(columns, signs_ref[...], preferred_element_type=jnp.float32)
    for index, (first, chans) in enumerate(CHUNKS):
        for low in range(0, chans, 16):
            outs = []
            for a in range(rows_a):
                start = a * HEAD_DIM + first + low
                outs.append(turned[start : start + 16, :] * flips[a])
            outs = butterfly(outs)
            for e in range(2):
                row = e * chans + low
                for array, values in enumerate(to_slots(outs[e::2], swap)):
                    for slot, value in enumerate(values):
                        out_refs[4 * index + array][slot, row : row + 16, :] = value.astype(jnp.bfloat16)


def join_parts(value, chans):
    return value + pltpu.roll(value, HAD - chans, 1)


def split_parts(value, chans):
    high = value.astype(jnp.bfloat16).astype(jnp.float32)
    lane = lax.broadcasted_iota(jnp.int32, value.shape, 1)
    both = jnp.where(lane < chans, high, pltpu.roll(value - high, chans, 1))
    return jnp.where(lane < 2 * chans, both, 0.0).astype(jnp.bfloat16)


def cross_turn_kernel(heads, chans, *refs):
    in_refs, out_refs = refs[:5], refs[5:]
    group = lax.axis_index("fsdp")
    swap = group & 1 != 0
    flips_in = [sign_of(group, s) for s in range(8)]
    flips_out = [flip * sign_of(group, group) for flip in flips_in]
    row_id = lax.broadcasted_iota(jnp.int32, (TAIL, HAD), 0)
    tail = jnp.zeros((TAIL, HAD), jnp.float32)
    for head in range(heads):
        columns = []
        for low in range(0, chans, 16):
            largest = None
            for e in range(2):
                rows = slice((head * 2 + e) * chans + low, (head * 2 + e) * chans + low + 16)
                got = [in_ref[0, rows, :] for in_ref in in_refs[:4]] + [in_refs[4][i, rows, :] for i in range(4)]
                got = from_origins([value.astype(jnp.float32) for value in got], swap)
                outs = butterfly([got[s] * flips_in[s] for s in range(8)])
                for s in range(8):
                    magnitude = jnp.abs(outs[s])
                    largest = magnitude if largest is None else jnp.maximum(largest, magnitude)
                outs = [outs[s] * flips_out[s] for s in range(8)]
                for array, values in enumerate(to_slots(outs, swap)):
                    for slot, value in enumerate(values):
                        out_refs[array][slot, rows, :] = value.astype(jnp.bfloat16)
            columns.append(largest)
        columns.append(jnp.zeros((HAD - chans, HAD), jnp.float32))
        peak = jnp.max(jnp.concatenate(columns, axis=0).T, axis=0, keepdims=True)
        tail = jnp.where(row_id == head, peak, tail)
    tail = split_parts(tail, chans)
    for out_ref in out_refs:
        for slot in range(2):
            out_ref[slot, heads * 2 * chans :, :] = tail


def pairing_offset(core, which, index):
    factor = (index & 1) + 4 * (index >> 1)
    return factor * jnp.where(core == 0, PAIRINGS[0][which], PAIRINGS[1][which])


def spread_kernel(heads, chans, placement_ref, *refs):
    in_refs, out_refs = refs[:5], refs[5:]
    me, core = lax.axis_index("tp"), lax.axis_index("fsdp") & 1
    mine = [placement_ref[me * heads + head] for head in range(heads)]
    blocks = [(in_ref, 0) for in_ref in in_refs[:4]] + [(in_refs[4], index) for index in range(4)]
    peaks = None
    for in_ref, index in blocks:
        part = join_parts(in_ref[index, heads * 2 * chans :, :].astype(jnp.float32), chans)
        peaks = part if peaks is None else jnp.maximum(peaks, part)
    row_id = lax.broadcasted_iota(jnp.int32, (TAIL, HAD), 0)
    span = 2 * chans
    direct = len(out_refs) == 1
    for i in range(4):
        for j in range(4):
            owner = 4 * i + j if direct else me ^ pairing_offset(core, 0, i) ^ pairing_offset(core, 1, j)
            out_ref, to = (out_refs[0], 4 * i + j) if direct else (out_refs[i], j)
            head = 0
            for index in range(1, heads):
                head = jnp.where(mine[index] == owner, index, head)
            rows = pl.ds(pl.multiple_of(head * span, 16), span)
            for s, (in_ref, index) in enumerate(blocks):
                out_ref[to, s * span : (s + 1) * span, :] = in_ref[index, rows, :]
            peak = jnp.sum(jnp.where(row_id == head, peaks, 0.0), axis=0, keepdims=True)
            out_ref[to, 8 * span :, :] = split_parts(jnp.broadcast_to(peak, (TAIL, HAD)), chans)


def pack_kernel(owners, heads, chunk, has_past, placement_ref, *refs):
    first, chans = chunk
    peak_ref, out_ref, buffer, sems, live_ref, slot_ref = refs[-6:]
    past_ref = refs[-8] if has_past else None
    in_refs = refs[: -8 if has_past else -6]
    me, group = lax.axis_index("tp"), lax.axis_index("fsdp")
    count = 0
    for source in range(owners):
        live = 0
        for head in range(heads):
            live = jnp.where(placement_ref[source * heads + head] == me, 1, live)
        live_ref[source] = live
        slot_ref[source] = count
        count = count + live
    lane = lax.broadcasted_iota(jnp.int32, (TAIL, HAD), 1)
    copies = []
    core = group & 1
    pair = jnp.where(core == 0, 2, 6)
    offsets = (0, 1, pair, pair ^ 1, pair ^ 4, pair ^ 5, 4, 5)
    blocks, rows = [], []
    for origin in range(owners):
        i, j = origin % 4, origin // 4
        if len(in_refs) == 1:
            in_ref, index, source = in_refs[0], origin, origin
        else:
            in_ref, index = (in_refs[3 + j], i) if j else (in_refs[i], 0)
            source = me ^ pairing_offset(core, 0, i) ^ pairing_offset(core, 1, j)
        live = live_ref[source] != 0
        slot = jnp.where(live, slot_ref[source], count + source - slot_ref[source])
        tail = in_ref[index, 16 * chans :, :].astype(jnp.float32)
        row = jnp.where((lane < chans) & live, join_parts(tail, chans), 0.0)
        rows.append(jnp.where(live, 1.0 / (row[:1, :] + 1e-06), 0.0))
        row = (pltpu.roll(row, first, 1) if first else row)[:1, :]
        if has_past:
            row = row + past_ref[pl.ds(slot, 1), :]
        peak_ref[pl.ds(slot, 1), :] = row
        blocks.append((in_ref, index, slot))
    rows.append(jnp.zeros((HAD - owners, HAD), jnp.float32))
    scales = jnp.concatenate(rows, axis=0).T
    for origin, (in_ref, index, slot) in enumerate(blocks):
        scale = scales[:chans, origin : origin + 1]
        for s in range(8):
            for e in range(2):
                start = (s * 2 + e) * chans
                lanes = pl.ds(pl.multiple_of(((group ^ offsets[s]) * 2 + e) * HAD, HAD), HAD)
                block = in_ref[index, start : start + chans, :]
                buffer[origin, :, lanes] = (block.astype(jnp.float32) * scale).astype(jnp.bfloat16)
        rows = out_ref.at[0, slot, first : first + chans, :]
        copies.append(pltpu.make_async_copy(buffer.at[origin], rows, sems.at[origin]))
        copies[-1].start()
    for copy in copies:
        copy.wait()


def per_device(qkv_weight, placement):
    rows_local, cols_local = qkv_weight.shape
    heads = cols_local // HEAD_DIM
    owners = lax.axis_size("tp")
    rows_a = rows_local // HAD
    params = pltpu.CompilerParams(vmem_limit_bytes=VMEM_BYTES)
    any_spec = pl.BlockSpec(memory_space=pl.ANY)
    smem_spec = pl.BlockSpec(memory_space=pltpu.SMEM)
    vmem_spec = pl.BlockSpec(memory_space=pltpu.VMEM)

    def call(kernel, name, shapes, *arrays, table=False):
        return pl.pallas_call(
            kernel,
            in_specs=[smem_spec] * table + [vmem_spec] * (len(arrays) - table),
            out_specs=[vmem_spec] * len(shapes),
            out_shape=[jax.ShapeDtypeStruct(shape + (HAD,), jnp.bfloat16) for shape in shapes],
            compiler_params=params,
            name=name,
        )(*arrays)

    signs = jnp.asarray(hadamard_table(HAD), jnp.bfloat16)
    widths = [2 * chans for _, chans in CHUNKS for _ in range(4)]
    turned = pl.pallas_call(
        functools.partial(local_turn_kernel, rows_a),
        grid=(heads,),
        in_specs=[
            pl.BlockSpec((rows_local, HEAD_DIM), lambda h: (0, h)),
            pl.BlockSpec((HAD, HAD), lambda h: (0, 0)),
        ],
        out_specs=[pl.BlockSpec((2, width, HAD), lambda h: (0, h, 0)) for width in widths],
        out_shape=[jax.ShapeDtypeStruct((2, heads * width, HAD), jnp.bfloat16) for width in widths],
        scratch_shapes=[pltpu.VMEM((rows_local, HAD), jnp.float32)],
        compiler_params=params,
        name="local_turn",
    )(qkv_weight, signs)

    state = [turned[4 * index : 4 * index + 4] for index in range(len(CHUNKS))]
    token = None
    past = []

    def tie(arrays):
        if token is None:
            return list(arrays)
        return list(lax.optimization_barrier((list(arrays), token))[0])

    for stage, index, *others in ORDER:
        first, chans = chunk = CHUNKS[index]
        arrays = tie(state[index])
        for other in others:
            arrays, state[other] = lax.optimization_barrier((arrays, state[other]))
        if stage == "start":
            state[index] = y_first(arrays)
        elif stage == "y_regroup":
            (token,) = call(y_regroup_kernel, stage, [(4,) + arrays[0].shape[1:2]], *arrays)
            state[index] = arrays + [y_second(token)]
        elif stage == "cross":
            shapes = [(2, heads * 2 * chans + TAIL)] * 4
            outs = call(functools.partial(cross_turn_kernel, heads, chans), stage, shapes, *arrays)
            token = outs[0]
            state[index] = y_first(outs)
        elif stage == "spread":
            direct = index < DIRECT
            shapes = [(owners, 16 * chans + TAIL)] if direct else [(4, 16 * chans + TAIL)] * 4
            kernel = functools.partial(spread_kernel, heads, chans)
            outs = call(kernel, stage, shapes, placement, *arrays, table=True)
            token = outs[0]
            if direct:
                state[index] = [lax.all_to_all(token, "tp", split_axis=0, concat_axis=0, tiled=True)]
            else:
                state[index] = [token] + owner_hops(outs[1:], 0)
        elif stage == "regroup":
            outs = call(regroup_kernel, stage, [arrays[0].shape[:2]] * 3, *arrays)
            token = outs[0]
            state[index] = arrays + owner_hops(outs, 1)
        else:
            past = pl.pallas_call(
                functools.partial(pack_kernel, owners, heads, chunk, bool(past)),
                in_specs=[smem_spec] + [vmem_spec] * len(arrays) + ([vmem_spec, any_spec] if past else []),
                out_specs=[vmem_spec, any_spec],
                out_shape=[
                    jax.ShapeDtypeStruct((owners, HEAD_DIM), jnp.float32),
                    jax.ShapeDtypeStruct((1, owners, HEAD_DIM, rows_local), jnp.bfloat16),
                ],
                scratch_shapes=[
                    pltpu.VMEM((owners, chans, rows_local), jnp.bfloat16),
                    pltpu.SemaphoreType.DMA((owners,)),
                    pltpu.SMEM((owners,), jnp.int32),
                    pltpu.SMEM((owners,), jnp.int32),
                ],
                input_output_aliases={2 + len(arrays): 1} if past else {},
                compiler_params=params,
                name="pack",
            )(placement, *arrays, *past)
            token = past[0]
    peaks, packed = past
    return packed, peaks[None]


def solution(mesh):
    in_specs = (P("fsdp", "tp"), P())
    out_specs = (P("tp", None, None, "fsdp"), P("tp", None, None))
    return jax.shard_map(
        per_device, mesh=mesh, in_specs=in_specs, out_specs=out_specs, check_vma=False
    )
```

```python
import functools

import jax
import jax.numpy as jnp
from jax import lax
from jax.experimental import pallas as pl
from jax.experimental.pallas import tpu as pltpu
from jax.sharding import PartitionSpec as P

HEAD_DIM = 128
HAD = 128
CHUNKS = ((0, 32), (32, 48), (80, 48))
ORDER = (
    ("start", 0),
    ("start", 1),
    ("y_regroup", 0),
    ("y_regroup", 1),
    ("cross", 0),
    ("start", 2),
    ("y_regroup", 0),
    ("cross", 1),
    ("spread", 0),
    ("y_regroup", 2),
    ("y_regroup", 1),
    ("regroup", 0),
    ("cross", 2),
    ("spread", 1),
    ("pack", 0),
    ("y_regroup", 2),
    ("regroup", 1),
    ("spread", 2),
    ("pack", 1),
    ("regroup", 2),
    ("pack", 2),
)
TAIL = 16
VMEM_BYTES = 12 * 1024 * 1024
BOTH = ("fsdp", "tp")


def butterfly(values):
    values = list(values)
    half = 1
    while half < len(values):
        for low in range(len(values)):
            if not low & half:
                first, second = values[low], values[low + half]
                values[low], values[low + half] = first + second, first - second
        half *= 2
    return values


PAIRINGS = ((1, 3), (3, 1))


def hop(array, rule):
    groups, owners = lax.axis_size("fsdp"), lax.axis_size("tp")
    pairs = []
    for f in range(groups):
        for t in range(owners):
            to_f, to_t = rule(f, t)
            pairs.append((f * owners + t, to_f * owners + to_t))
    return lax.ppermute(array, BOTH, pairs)


def y_first(blocks):
    own, core, pair, both = blocks
    pair = hop(pair, lambda f, t: (f ^ 2 * PAIRINGS[f & 1][0], t))
    both = hop(both, lambda f, t: (f ^ 1 ^ 2 * PAIRINGS[1 - (f & 1)][0], t))
    core = hop(core, lambda f, t: (f ^ 1, t))
    return [own, core, pair, both]


def y_second(payload):
    return hop(payload, lambda f, t: (f ^ 2 * PAIRINGS[f & 1][1], t))


def owner_hops(blocks, which):
    out = [None] * 3
    for place in (2, 0, 1):
        factor = (1, 4, 5)[place]
        out[place] = hop(blocks[place], lambda f, t: (f, t ^ factor * PAIRINGS[f & 1][which]))
    return out


def to_slots(values, swap):
    return (
        (values[0], jnp.where(swap, values[2], values[6])),
        (values[1], jnp.where(swap, values[7], values[3])),
        (jnp.where(swap, values[6], values[2]), values[4]),
        (jnp.where(swap, values[3], values[7]), values[5]),
    )


def from_origins(values, swap):
    return (
        values[0],
        values[1],
        jnp.where(swap, values[4], values[2]),
        jnp.where(swap, values[5], values[3]),
        values[6],
        values[7],
        jnp.where(swap, values[2], values[4]),
        jnp.where(swap, values[3], values[5]),
    )


def y_regroup_kernel(*refs):
    for index, in_ref in enumerate(refs[:4]):
        refs[4][index] = in_ref[1]


def regroup_kernel(*refs):
    in_refs, out_refs = refs[:4], refs[4:]
    for slot, out_ref in enumerate(out_refs):
        for index, in_ref in enumerate(in_refs):
            out_ref[index] = in_ref[slot + 1]


def sign_of(value, bits):
    both = value & bits
    both = both ^ (both >> 2)
    both = both ^ (both >> 1)
    return (1 - 2 * (both & 1)).astype(jnp.float32)


def local_turn_kernel(rows_a, weight_ref, *refs):
    out_refs, turned = refs[:-1], refs[-1]
    group = lax.axis_index("fsdp")
    swap = group & 1 != 0
    flips = [sign_of(group, a >> 1) * (1.0 / HAD) for a in range(rows_a)]
    columns = jnp.concatenate([weight_ref[a * HAD : (a + 1) * HAD, :].T for a in range(rows_a)], axis=0)
    both = [lax.broadcasted_iota(jnp.int32, (HAD, HAD), dim) for dim in range(2)]
    both = both[0] & both[1]
    for shift in (4, 2, 1):
        both = both ^ (both >> shift)
    signs = (1 - 2 * (both & 1)).astype(jnp.float32).astype(jnp.bfloat16)
    turned[...] = jnp.dot(columns, signs, preferred_element_type=jnp.float32)
    for index, (first, chans) in enumerate(CHUNKS):
        for low in range(0, chans, 16):
            outs = []
            for a in range(rows_a):
                start = a * HEAD_DIM + first + low
                outs.append(turned[start : start + 16, :] * flips[a])
            outs = butterfly(outs)
            for e in range(2):
                row = e * chans + low
                for array, values in enumerate(to_slots(outs[e::2], swap)):
                    for slot, value in enumerate(values):
                        out_refs[4 * index + array][slot, row : row + 16, :] = value.astype(jnp.bfloat16)


def join_parts(value, chans):
    return value + pltpu.roll(value, HAD - chans, 1)


def split_parts(value, chans):
    high = value.astype(jnp.bfloat16).astype(jnp.float32)
    lane = lax.broadcasted_iota(jnp.int32, value.shape, 1)
    both = jnp.where(lane < chans, high, pltpu.roll(value - high, chans, 1))
    return jnp.where(lane < 2 * chans, both, 0.0).astype(jnp.bfloat16)


def cross_turn_kernel(heads, chans, *refs):
    in_refs, out_refs = refs[:5], refs[5:]
    group = lax.axis_index("fsdp")
    swap = group & 1 != 0
    flips_in = [sign_of(group, s) for s in range(8)]
    flips_out = [flip * sign_of(group, group) for flip in flips_in]
    row_id = lax.broadcasted_iota(jnp.int32, (TAIL, HAD), 0)
    tail = jnp.zeros((TAIL, HAD), jnp.float32)
    for head in range(heads):
        columns = []
        for low in range(0, chans, 16):
            largest = None
            for e in range(2):
                rows = slice((head * 2 + e) * chans + low, (head * 2 + e) * chans + low + 16)
                got = [in_ref[0, rows, :] for in_ref in in_refs[:4]] + [in_refs[4][i, rows, :] for i in range(4)]
                got = from_origins([value.astype(jnp.float32) for value in got], swap)
                outs = butterfly([got[s] * flips_in[s] for s in range(8)])
                for s in range(8):
                    magnitude = jnp.abs(outs[s])
                    largest = magnitude if largest is None else jnp.maximum(largest, magnitude)
                outs = [outs[s] * flips_out[s] for s in range(8)]
                for array, values in enumerate(to_slots(outs, swap)):
                    for slot, value in enumerate(values):
                        out_refs[array][slot, rows, :] = value.astype(jnp.bfloat16)
            columns.append(largest)
        columns.append(jnp.zeros((HAD - chans, HAD), jnp.float32))
        peak = jnp.max(jnp.concatenate(columns, axis=0).T, axis=0, keepdims=True)
        tail = jnp.where(row_id == head, peak, tail)
    tail = split_parts(tail, chans)
    for out_ref in out_refs:
        for slot in range(2):
            out_ref[slot, heads * 2 * chans :, :] = tail


def pairing_offset(core, which, index):
    factor = (index & 1) + 4 * (index >> 1)
    return factor * jnp.where(core == 0, PAIRINGS[0][which], PAIRINGS[1][which])


def spread_kernel(heads, chans, placement_ref, *refs):
    in_refs, out_refs = refs[:5], refs[5:]
    me, core = lax.axis_index("tp"), lax.axis_index("fsdp") & 1
    mine = [placement_ref[me * heads + head] for head in range(heads)]
    blocks = [(in_ref, 0) for in_ref in in_refs[:4]] + [(in_refs[4], index) for index in range(4)]
    peaks = None
    for in_ref, index in blocks:
        part = join_parts(in_ref[index, heads * 2 * chans :, :].astype(jnp.float32), chans)
        peaks = part if peaks is None else jnp.maximum(peaks, part)
    row_id = lax.broadcasted_iota(jnp.int32, (TAIL, HAD), 0)
    span = 2 * chans
    for i, out_ref in enumerate(out_refs):
        for j in range(4):
            owner = me ^ pairing_offset(core, 0, i) ^ pairing_offset(core, 1, j)
            head = 0
            for index in range(1, heads):
                head = jnp.where(mine[index] == owner, index, head)
            rows = pl.ds(pl.multiple_of(head * span, 16), span)
            for s, (in_ref, index) in enumerate(blocks):
                out_ref[j, s * span : (s + 1) * span, :] = in_ref[index, rows, :]
            peak = jnp.sum(jnp.where(row_id == head, peaks, 0.0), axis=0, keepdims=True)
            out_ref[j, 8 * span :, :] = split_parts(jnp.broadcast_to(peak, (TAIL, HAD)), chans)


def pack_kernel(owners, heads, chunk, has_past, placement_ref, *refs):
    first, chans = chunk
    peak_ref, out_ref, buffer, sems, live_ref, slot_ref = refs[-6:]
    past_ref = refs[-8] if has_past else None
    in_refs = refs[: -8 if has_past else -6]
    me, group = lax.axis_index("tp"), lax.axis_index("fsdp")
    count = 0
    for source in range(owners):
        live = 0
        for head in range(heads):
            live = jnp.where(placement_ref[source * heads + head] == me, 1, live)
        live_ref[source] = live
        slot_ref[source] = count
        count = count + live
    lane = lax.broadcasted_iota(jnp.int32, (TAIL, HAD), 1)
    copies = []
    core = group & 1
    pair = jnp.where(core == 0, 2, 6)
    offsets = (0, 1, pair, pair ^ 1, pair ^ 4, pair ^ 5, 4, 5)
    blocks, rows = [], []
    for origin in range(owners):
        i, j = origin % 4, origin // 4
        in_ref, index = (in_refs[3 + j], i) if j else (in_refs[i], 0)
        source = me ^ pairing_offset(core, 0, i) ^ pairing_offset(core, 1, j)
        live = live_ref[source] != 0
        slot = jnp.where(live, slot_ref[source], count + source - slot_ref[source])
        tail = in_ref[index, 16 * chans :, :].astype(jnp.float32)
        row = jnp.where((lane < chans) & live, join_parts(tail, chans), 0.0)
        rows.append(jnp.where(live, 1.0 / (row[:1, :] + 1e-06), 0.0))
        row = (pltpu.roll(row, first, 1) if first else row)[:1, :]
        if has_past:
            row = row + past_ref[pl.ds(slot, 1), :]
        peak_ref[pl.ds(slot, 1), :] = row
        blocks.append((in_ref, index, slot))
    rows.append(jnp.zeros((HAD - owners, HAD), jnp.float32))
    scales = jnp.concatenate(rows, axis=0).T
    for origin, (in_ref, index, slot) in enumerate(blocks):
        scale = scales[:chans, origin : origin + 1]
        for s in range(8):
            for e in range(2):
                start = (s * 2 + e) * chans
                lanes = pl.ds(pl.multiple_of(((group ^ offsets[s]) * 2 + e) * HAD, HAD), HAD)
                block = in_ref[index, start : start + chans, :]
                buffer[origin, :, lanes] = (block.astype(jnp.float32) * scale).astype(jnp.bfloat16)
        rows = out_ref.at[0, slot, first : first + chans, :]
        copies.append(pltpu.make_async_copy(buffer.at[origin], rows, sems.at[origin]))
        copies[-1].start()
    for copy in copies:
        copy.wait()


def per_device(qkv_weight, placement):
    rows_local, cols_local = qkv_weight.shape
    heads = cols_local // HEAD_DIM
    owners = lax.axis_size("tp")
    rows_a = rows_local // HAD
    params = pltpu.CompilerParams(vmem_limit_bytes=VMEM_BYTES)
    any_spec = pl.BlockSpec(memory_space=pl.ANY)
    smem_spec = pl.BlockSpec(memory_space=pltpu.SMEM)
    vmem_spec = pl.BlockSpec(memory_space=pltpu.VMEM)

    def call(kernel, name, shapes, *arrays, table=False):
        return pl.pallas_call(
            kernel,
            in_specs=[smem_spec] * table + [vmem_spec] * (len(arrays) - table),
            out_specs=[vmem_spec] * len(shapes),
            out_shape=[jax.ShapeDtypeStruct(shape + (HAD,), jnp.bfloat16) for shape in shapes],
            compiler_params=params,
            name=name,
        )(*arrays)

    widths = [2 * chans for _, chans in CHUNKS for _ in range(4)]
    turned = pl.pallas_call(
        functools.partial(local_turn_kernel, rows_a),
        grid=(heads,),
        in_specs=[pl.BlockSpec((rows_local, HEAD_DIM), lambda h: (0, h))],
        out_specs=[pl.BlockSpec((2, width, HAD), lambda h: (0, h, 0)) for width in widths],
        out_shape=[jax.ShapeDtypeStruct((2, heads * width, HAD), jnp.bfloat16) for width in widths],
        scratch_shapes=[pltpu.VMEM((rows_local, HAD), jnp.float32)],
        compiler_params=params,
        name="local_turn",
    )(qkv_weight)

    state = [turned[4 * index : 4 * index + 4] for index in range(len(CHUNKS))]
    token = None
    past = []

    def tie(arrays):
        if token is None:
            return list(arrays)
        return list(lax.optimization_barrier((list(arrays), token))[0])

    for stage, index in ORDER:
        first, chans = chunk = CHUNKS[index]
        arrays = tie(state[index])
        if stage == "start":
            state[index] = y_first(arrays)
        elif stage == "y_regroup":
            (token,) = call(y_regroup_kernel, stage, [(4,) + arrays[0].shape[1:2]], *arrays)
            state[index] = arrays + [y_second(token)]
        elif stage == "cross":
            shapes = [(2, heads * 2 * chans + TAIL)] * 4
            outs = call(functools.partial(cross_turn_kernel, heads, chans), stage, shapes, *arrays)
            token = outs[0]
            state[index] = y_first(outs)
        elif stage == "spread":
            shapes = [(4, 16 * chans + TAIL)] * 4
            kernel = functools.partial(spread_kernel, heads, chans)
            outs = call(kernel, stage, shapes, placement, *arrays, table=True)
            token = outs[0]
            state[index] = [token] + owner_hops(outs[1:], 0)
        elif stage == "regroup":
            outs = call(regroup_kernel, stage, [arrays[0].shape[:2]] * 3, *arrays)
            token = outs[0]
            state[index] = arrays + owner_hops(outs, 1)
        else:
            past = pl.pallas_call(
                functools.partial(pack_kernel, owners, heads, chunk, bool(past)),
                in_specs=[smem_spec] + [vmem_spec] * len(arrays) + ([vmem_spec, any_spec] if past else []),
                out_specs=[vmem_spec, any_spec],
                out_shape=[
                    jax.ShapeDtypeStruct((owners, HEAD_DIM), jnp.float32),
                    jax.ShapeDtypeStruct((1, owners, HEAD_DIM, rows_local), jnp.bfloat16),
                ],
                scratch_shapes=[
                    pltpu.VMEM((owners, chans, rows_local), jnp.bfloat16),
                    pltpu.SemaphoreType.DMA((owners,)),
                    pltpu.SMEM((owners,), jnp.int32),
                    pltpu.SMEM((owners,), jnp.int32),
                ],
                input_output_aliases={2 + len(arrays): 1} if past else {},
                compiler_params=params,
                name="pack",
            )(placement, *arrays, *past)
            token = past[0]
    peaks, packed = past
    return packed, peaks[None]


def solution(mesh):
    in_specs = (P("fsdp", "tp"), P())
    out_specs = (P("tp", None, None, "fsdp"), P("tp", None, None))
    return jax.shard_map(
        per_device, mesh=mesh, in_specs=in_specs, out_specs=out_specs, check_vma=False
    )
```

```python
import functools

import jax
import jax.numpy as jnp
from jax import lax
from jax.experimental import pallas as pl
from jax.experimental.pallas import tpu as pltpu
from jax.sharding import PartitionSpec as P

HEAD_DIM = 128
HAD = 128
CHUNKS = ((0, 32), (32, 48), (80, 48))
ORDER = (
    ("start", 0),
    ("start", 1),
    ("y_regroup", 0),
    ("y_regroup", 1),
    ("cross", 0),
    ("y_regroup", 0),
    ("cross", 1),
    ("spread", 0),
    ("start", 2),
    ("y_regroup", 1),
    ("regroup", 0),
    ("spread", 1),
    ("y_regroup", 2),
    ("pack", 0),
    ("cross", 2, 1),
    ("y_regroup", 2),
    ("regroup", 1),
    ("spread", 2),
    ("pack", 1),
    ("regroup", 2),
    ("pack", 2),
)
TAIL = 16
VMEM_BYTES = 12 * 1024 * 1024
BOTH = ("fsdp", "tp")


def butterfly(values):
    values = list(values)
    half = 1
    while half < len(values):
        for low in range(len(values)):
            if not low & half:
                first, second = values[low], values[low + half]
                values[low], values[low + half] = first + second, first - second
        half *= 2
    return values


PAIRINGS = ((1, 3), (3, 1))


def hop(array, rule):
    groups, owners = lax.axis_size("fsdp"), lax.axis_size("tp")
    pairs = []
    for f in range(groups):
        for t in range(owners):
            to_f, to_t = rule(f, t)
            pairs.append((f * owners + t, to_f * owners + to_t))
    return lax.ppermute(array, BOTH, pairs)


def y_first(blocks):
    own, core, pair, both = blocks
    pair = hop(pair, lambda f, t: (f ^ 2 * PAIRINGS[f & 1][0], t))
    both = hop(both, lambda f, t: (f ^ 1 ^ 2 * PAIRINGS[1 - (f & 1)][0], t))
    core = hop(core, lambda f, t: (f ^ 1, t))
    return [own, core, pair, both]


def y_second(payload):
    return hop(payload, lambda f, t: (f ^ 2 * PAIRINGS[f & 1][1], t))


def owner_hops(blocks, which):
    out = [None] * 3
    for place in (2, 0, 1):
        factor = (1, 4, 5)[place]
        out[place] = hop(blocks[place], lambda f, t: (f, t ^ factor * PAIRINGS[f & 1][which]))
    return out


def to_slots(values, swap):
    return (
        (values[0], jnp.where(swap, values[2], values[6])),
        (values[1], jnp.where(swap, values[7], values[3])),
        (jnp.where(swap, values[6], values[2]), values[4]),
        (jnp.where(swap, values[3], values[7]), values[5]),
    )


def from_origins(values, swap):
    return (
        values[0],
        values[1],
        jnp.where(swap, values[4], values[2]),
        jnp.where(swap, values[5], values[3]),
        values[6],
        values[7],
        jnp.where(swap, values[2], values[4]),
        jnp.where(swap, values[3], values[5]),
    )


def y_regroup_kernel(*refs):
    for index, in_ref in enumerate(refs[:4]):
        refs[4][index] = in_ref[1]


def regroup_kernel(*refs):
    in_refs, out_refs = refs[:4], refs[4:]
    for slot, out_ref in enumerate(out_refs):
        for index, in_ref in enumerate(in_refs):
            out_ref[index] = in_ref[slot + 1]


def sign_of(value, bits):
    both = value & bits
    both = both ^ (both >> 2)
    both = both ^ (both >> 1)
    return (1 - 2 * (both & 1)).astype(jnp.float32)


def local_turn_kernel(rows_a, chunks, weight_ref, *refs):
    out_refs, turned = refs[:-1], refs[-1]
    group = lax.axis_index("fsdp")
    swap = group & 1 != 0
    flips = [sign_of(group, a >> 1) * (1.0 / HAD) for a in range(rows_a)]
    width = turned.shape[0] // rows_a
    columns = jnp.concatenate([weight_ref[a * HAD : (a + 1) * HAD, :width].T for a in range(rows_a)], axis=0)
    both = [lax.broadcasted_iota(jnp.int32, (HAD, HAD), dim) for dim in range(2)]
    both = both[0] & both[1]
    for shift in (4, 2, 1):
        both = both ^ (both >> shift)
    signs = (1 - 2 * (both & 1)).astype(jnp.float32).astype(jnp.bfloat16)
    turned[...] = jnp.dot(columns, signs, preferred_element_type=jnp.float32)
    for index, (first, chans) in enumerate(chunks):
        for low in range(0, chans, 16):
            outs = []
            for a in range(rows_a):
                start = a * width + first + low
                outs.append(turned[start : start + 16, :] * flips[a])
            outs = butterfly(outs)
            for e in range(2):
                row = e * chans + low
                for array, values in enumerate(to_slots(outs[e::2], swap)):
                    for slot, value in enumerate(values):
                        out_refs[4 * index + array][slot, row : row + 16, :] = value.astype(jnp.bfloat16)


def join_parts(value, chans):
    return value + pltpu.roll(value, HAD - chans, 1)


def split_parts(value, chans):
    high = value.astype(jnp.bfloat16).astype(jnp.float32)
    lane = lax.broadcasted_iota(jnp.int32, value.shape, 1)
    both = jnp.where(lane < chans, high, pltpu.roll(value - high, chans, 1))
    return jnp.where(lane < 2 * chans, both, 0.0).astype(jnp.bfloat16)


def cross_turn_kernel(heads, chans, *refs):
    in_refs, out_refs = refs[:5], refs[5:]
    group = lax.axis_index("fsdp")
    swap = group & 1 != 0
    flips_in = [sign_of(group, s) for s in range(8)]
    flips_out = [flip * sign_of(group, group) for flip in flips_in]
    row_id = lax.broadcasted_iota(jnp.int32, (TAIL, HAD), 0)
    tail = jnp.zeros((TAIL, HAD), jnp.float32)
    for head in range(heads):
        columns = []
        for low in range(0, chans, 16):
            largest = None
            for e in range(2):
                rows = slice((head * 2 + e) * chans + low, (head * 2 + e) * chans + low + 16)
                got = [in_ref[0, rows, :] for in_ref in in_refs[:4]] + [in_refs[4][i, rows, :] for i in range(4)]
                got = from_origins([value.astype(jnp.float32) for value in got], swap)
                outs = butterfly([got[s] * flips_in[s] for s in range(8)])
                for s in range(8):
                    magnitude = jnp.abs(outs[s])
                    largest = magnitude if largest is None else jnp.maximum(largest, magnitude)
                outs = [outs[s] * flips_out[s] for s in range(8)]
                for array, values in enumerate(to_slots(outs, swap)):
                    for slot, value in enumerate(values):
                        out_refs[array][slot, rows, :] = value.astype(jnp.bfloat16)
            columns.append(largest)
        columns.append(jnp.zeros((HAD - chans, HAD), jnp.float32))
        peak = jnp.max(jnp.concatenate(columns, axis=0).T, axis=0, keepdims=True)
        tail = jnp.where(row_id == head, peak, tail)
    tail = split_parts(tail, chans)
    for out_ref in out_refs:
        for slot in range(2):
            out_ref[slot, heads * 2 * chans :, :] = tail


def pairing_offset(core, which, index):
    factor = (index & 1) + 4 * (index >> 1)
    return factor * jnp.where(core == 0, PAIRINGS[0][which], PAIRINGS[1][which])


def spread_kernel(heads, chans, placement_ref, *refs):
    in_refs, out_refs = refs[:5], refs[5:]
    me, core = lax.axis_index("tp"), lax.axis_index("fsdp") & 1
    mine = [placement_ref[me * heads + head] for head in range(heads)]
    blocks = [(in_ref, 0) for in_ref in in_refs[:4]] + [(in_refs[4], index) for index in range(4)]
    peaks = None
    for in_ref, index in blocks:
        part = join_parts(in_ref[index, heads * 2 * chans :, :].astype(jnp.float32), chans)
        peaks = part if peaks is None else jnp.maximum(peaks, part)
    row_id = lax.broadcasted_iota(jnp.int32, (TAIL, HAD), 0)
    span = 2 * chans
    for i, out_ref in enumerate(out_refs):
        for j in range(4):
            owner = me ^ pairing_offset(core, 0, i) ^ pairing_offset(core, 1, j)
            head = 0
            for index in range(1, heads):
                head = jnp.where(mine[index] == owner, index, head)
            rows = pl.ds(pl.multiple_of(head * span, 16), span)
            for s, (in_ref, index) in enumerate(blocks):
                out_ref[j, s * span : (s + 1) * span, :] = in_ref[index, rows, :]
            peak = jnp.sum(jnp.where(row_id == head, peaks, 0.0), axis=0, keepdims=True)
            out_ref[j, 8 * span :, :] = split_parts(jnp.broadcast_to(peak, (TAIL, HAD)), chans)


def pack_kernel(owners, heads, chunk, has_past, placement_ref, *refs):
    first, chans = chunk
    peak_ref, out_ref, buffer, sems, live_ref, slot_ref = refs[-6:]
    past_ref = refs[-8] if has_past else None
    in_refs = refs[: -8 if has_past else -6]
    me, group = lax.axis_index("tp"), lax.axis_index("fsdp")
    count = 0
    for source in range(owners):
        live = 0
        for head in range(heads):
            live = jnp.where(placement_ref[source * heads + head] == me, 1, live)
        live_ref[source] = live
        slot_ref[source] = count
        count = count + live
    lane = lax.broadcasted_iota(jnp.int32, (TAIL, HAD), 1)
    copies = []
    core = group & 1
    pair = jnp.where(core == 0, 2, 6)
    offsets = (0, 1, pair, pair ^ 1, pair ^ 4, pair ^ 5, 4, 5)
    blocks, rows = [], []
    for origin in range(owners):
        i, j = origin % 4, origin // 4
        in_ref, index = (in_refs[3 + j], i) if j else (in_refs[i], 0)
        source = me ^ pairing_offset(core, 0, i) ^ pairing_offset(core, 1, j)
        live = live_ref[source] != 0
        slot = jnp.where(live, slot_ref[source], count + source - slot_ref[source])
        tail = in_ref[index, 16 * chans :, :].astype(jnp.float32)
        row = jnp.where((lane < chans) & live, join_parts(tail, chans), 0.0)
        rows.append(jnp.where(live, 1.0 / (row[:1, :] + 1e-06), 0.0))
        row = (pltpu.roll(row, first, 1) if first else row)[:1, :]
        if has_past:
            row = row + past_ref[pl.ds(slot, 1), :]
        peak_ref[pl.ds(slot, 1), :] = row
        blocks.append((in_ref, index, slot))
    rows.append(jnp.zeros((HAD - owners, HAD), jnp.float32))
    scales = jnp.concatenate(rows, axis=0).T
    for origin, (in_ref, index, slot) in enumerate(blocks):
        scale = scales[:chans, origin : origin + 1]
        for s in range(8):
            for e in range(2):
                start = (s * 2 + e) * chans
                lanes = pl.ds(pl.multiple_of(((group ^ offsets[s]) * 2 + e) * HAD, HAD), HAD)
                block = in_ref[index, start : start + chans, :]
                buffer[origin, :, lanes] = (block.astype(jnp.float32) * scale).astype(jnp.bfloat16)
        rows = out_ref.at[0, slot, first : first + chans, :]
        copies.append(pltpu.make_async_copy(buffer.at[origin], rows, sems.at[origin]))
        copies[-1].start()
    for copy in copies:
        copy.wait()


def per_device(qkv_weight, placement):
    rows_local, cols_local = qkv_weight.shape
    heads = cols_local // HEAD_DIM
    owners = lax.axis_size("tp")
    rows_a = rows_local // HAD
    params = pltpu.CompilerParams(vmem_limit_bytes=VMEM_BYTES)
    any_spec = pl.BlockSpec(memory_space=pl.ANY)
    smem_spec = pl.BlockSpec(memory_space=pltpu.SMEM)
    vmem_spec = pl.BlockSpec(memory_space=pltpu.VMEM)

    def call(kernel, name, shapes, *arrays, table=False):
        return pl.pallas_call(
            kernel,
            in_specs=[smem_spec] * table + [vmem_spec] * (len(arrays) - table),
            out_specs=[vmem_spec] * len(shapes),
            out_shape=[jax.ShapeDtypeStruct(shape + (HAD,), jnp.bfloat16) for shape in shapes],
            compiler_params=params,
            name=name,
        )(*arrays)

    def local_turn(weight, chunks):
        widths = [2 * chans for _, chans in chunks for _ in range(4)]
        last = sum(chunks[-1])
        return pl.pallas_call(
            functools.partial(local_turn_kernel, rows_a, chunks),
            grid=(heads,),
            in_specs=[pl.BlockSpec((rows_local, HEAD_DIM), lambda h: (0, h))],
            out_specs=[pl.BlockSpec((2, width, HAD), lambda h: (0, h, 0)) for width in widths],
            out_shape=[jax.ShapeDtypeStruct((2, heads * width, HAD), jnp.bfloat16) for width in widths],
            scratch_shapes=[pltpu.VMEM((rows_a * last, HAD), jnp.float32)],
            compiler_params=params,
            name="local_turn",
        )(weight)

    turned = list(local_turn(qkv_weight, CHUNKS[:1]))
    qkv_weight, turned = lax.optimization_barrier((qkv_weight, turned))
    turned += list(local_turn(qkv_weight, CHUNKS[1:]))
    state = [turned[4 * index : 4 * index + 4] for index in range(len(CHUNKS))]
    token = None
    past = []

    def tie(arrays):
        if token is None:
            return list(arrays)
        return list(lax.optimization_barrier((list(arrays), token))[0])

    for stage, index, *others in ORDER:
        first, chans = chunk = CHUNKS[index]
        arrays = tie(state[index])
        for other in others:
            arrays, state[other][3] = lax.optimization_barrier((arrays, state[other][3]))
        if stage == "start":
            state[index] = y_first(arrays)
            token = turned[4] if index == 0 else token
        elif stage == "y_regroup":
            (token,) = call(y_regroup_kernel, stage, [(4,) + arrays[0].shape[1:2]], *arrays)
            state[index] = arrays + [y_second(token)]
        elif stage == "cross":
            shapes = [(2, heads * 2 * chans + TAIL)] * 4
            outs = call(functools.partial(cross_turn_kernel, heads, chans), stage, shapes, *arrays)
            token = outs[0]
            state[index] = y_first(outs)
        elif stage == "spread":
            shapes = [(4, 16 * chans + TAIL)] * 4
            kernel = functools.partial(spread_kernel, heads, chans)
            outs = call(kernel, stage, shapes, placement, *arrays, table=True)
            token = outs[0]
            state[index] = [token] + owner_hops(outs[1:], 0)
        elif stage == "regroup":
            outs = call(regroup_kernel, stage, [arrays[0].shape[:2]] * 3, *arrays)
            token = outs[0]
            state[index] = arrays + owner_hops(outs, 1)
        else:
            past = pl.pallas_call(
                functools.partial(pack_kernel, owners, heads, chunk, bool(past)),
                in_specs=[smem_spec] + [vmem_spec] * len(arrays) + ([vmem_spec, any_spec] if past else []),
                out_specs=[vmem_spec, any_spec],
                out_shape=[
                    jax.ShapeDtypeStruct((owners, HEAD_DIM), jnp.float32),
                    jax.ShapeDtypeStruct((1, owners, HEAD_DIM, rows_local), jnp.bfloat16),
                ],
                scratch_shapes=[
                    pltpu.VMEM((owners, chans, rows_local), jnp.bfloat16),
                    pltpu.SemaphoreType.DMA((owners,)),
                    pltpu.SMEM((owners,), jnp.int32),
                    pltpu.SMEM((owners,), jnp.int32),
                ],
                input_output_aliases={2 + len(arrays): 1} if past else {},
                compiler_params=params,
                name="pack",
            )(placement, *arrays, *past)
            token = past[0]
    peaks, packed = past
    return packed, peaks[None]


def solution(mesh):
    in_specs = (P("fsdp", "tp"), P())
    out_specs = (P("tp", None, None, "fsdp"), P("tp", None, None))
    return jax.shard_map(
        per_device, mesh=mesh, in_specs=in_specs, out_specs=out_specs, check_vma=False
    )
```

```python
import functools

import jax
import jax.numpy as jnp
from jax import lax
from jax.experimental import pallas as pl
from jax.experimental.pallas import tpu as pltpu
from jax.sharding import PartitionSpec as P

HEAD_DIM = 128
HAD = 128
CHUNKS = ((0, 48), (48, 48), (96, 32))
ORDER = (
    ("start", 0),
    ("start", 1),
    ("y_regroup", 0),
    ("y_regroup", 1),
    ("cross", 0),
    ("start", 2),
    ("y_regroup", 0),
    ("cross", 1),
    ("spread", 0),
    ("y_regroup", 2),
    ("y_regroup", 1),
    ("regroup", 0),
    ("cross", 2),
    ("spread", 1),
    ("pack", 0),
    ("y_regroup", 2),
    ("regroup", 1),
    ("spread", 2),
    ("pack", 1),
    ("regroup", 2),
    ("pack", 2),
)
TAIL = 16
VMEM_BYTES = 12 * 1024 * 1024
BOTH = ("fsdp", "tp")


def butterfly(values):
    values = list(values)
    half = 1
    while half < len(values):
        for low in range(len(values)):
            if not low & half:
                first, second = values[low], values[low + half]
                values[low], values[low + half] = first + second, first - second
        half *= 2
    return values


PAIRINGS = ((1, 3), (3, 1))


def hop(array, rule):
    groups, owners = lax.axis_size("fsdp"), lax.axis_size("tp")
    pairs = []
    for f in range(groups):
        for t in range(owners):
            to_f, to_t = rule(f, t)
            pairs.append((f * owners + t, to_f * owners + to_t))
    return lax.ppermute(array, BOTH, pairs)


def y_first(blocks):
    own, core, pair, both = blocks
    pair = hop(pair, lambda f, t: (f ^ 2 * PAIRINGS[f & 1][0], t))
    both = hop(both, lambda f, t: (f ^ 1 ^ 2 * PAIRINGS[1 - (f & 1)][0], t))
    core = hop(core, lambda f, t: (f ^ 1, t))
    return [own, core, pair, both]


def y_second(payload):
    return hop(payload, lambda f, t: (f ^ 2 * PAIRINGS[f & 1][1], t))


def owner_hops(blocks, which):
    out = [None] * 3
    for place in (2, 0, 1):
        factor = (1, 4, 5)[place]
        out[place] = hop(blocks[place], lambda f, t: (f, t ^ factor * PAIRINGS[f & 1][which]))
    return out


def to_slots(values, swap):
    return (
        (values[0], jnp.where(swap, values[2], values[6])),
        (values[1], jnp.where(swap, values[7], values[3])),
        (jnp.where(swap, values[6], values[2]), values[4]),
        (jnp.where(swap, values[3], values[7]), values[5]),
    )


def from_origins(values, swap):
    return (
        values[0],
        values[1],
        jnp.where(swap, values[4], values[2]),
        jnp.where(swap, values[5], values[3]),
        values[6],
        values[7],
        jnp.where(swap, values[2], values[4]),
        jnp.where(swap, values[3], values[5]),
    )


def y_regroup_kernel(*refs):
    for index, in_ref in enumerate(refs[:4]):
        refs[4][index] = in_ref[1]


def regroup_kernel(*refs):
    in_refs, out_refs = refs[:4], refs[4:]
    for slot, out_ref in enumerate(out_refs):
        for index, in_ref in enumerate(in_refs):
            out_ref[index] = in_ref[slot + 1]


def sign_of(value, bits):
    both = value & bits
    both = both ^ (both >> 2)
    both = both ^ (both >> 1)
    return (1 - 2 * (both & 1)).astype(jnp.float32)


def local_turn_kernel(rows_a, weight_ref, *refs):
    out_refs, turned = refs[:-1], refs[-1]
    group = lax.axis_index("fsdp")
    swap = group & 1 != 0
    flips = [sign_of(group, a >> 1) * (1.0 / HAD) for a in range(rows_a)]
    columns = jnp.concatenate([weight_ref[a * HAD : (a + 1) * HAD, :].T for a in range(rows_a)], axis=0)
    both = [lax.broadcasted_iota(jnp.int32, (HAD, HAD), dim) for dim in range(2)]
    both = both[0] & both[1]
    for shift in (4, 2, 1):
        both = both ^ (both >> shift)
    signs = (1 - 2 * (both & 1)).astype(jnp.float32).astype(jnp.bfloat16)
    turned[...] = jnp.dot(columns, signs, preferred_element_type=jnp.float32)
    for index, (first, chans) in enumerate(CHUNKS):
        for low in range(0, chans, 16):
            outs = []
            for a in range(rows_a):
                start = a * HEAD_DIM + first + low
                outs.append(turned[start : start + 16, :] * flips[a])
            outs = butterfly(outs)
            for e in range(2):
                row = e * chans + low
                for array, values in enumerate(to_slots(outs[e::2], swap)):
                    for slot, value in enumerate(values):
                        out_refs[4 * index + array][slot, row : row + 16, :] = value.astype(jnp.bfloat16)


def join_parts(value, chans):
    return value + pltpu.roll(value, HAD - chans, 1)


def split_parts(value, chans):
    high = value.astype(jnp.bfloat16).astype(jnp.float32)
    lane = lax.broadcasted_iota(jnp.int32, value.shape, 1)
    both = jnp.where(lane < chans, high, pltpu.roll(value - high, chans, 1))
    return jnp.where(lane < 2 * chans, both, 0.0).astype(jnp.bfloat16)


def cross_turn_kernel(heads, chans, *refs):
    in_refs, out_refs = refs[:5], refs[5:]
    group = lax.axis_index("fsdp")
    swap = group & 1 != 0
    flips_in = [sign_of(group, s) for s in range(8)]
    flips_out = [flip * sign_of(group, group) for flip in flips_in]
    row_id = lax.broadcasted_iota(jnp.int32, (TAIL, HAD), 0)
    tail = jnp.zeros((TAIL, HAD), jnp.float32)
    for head in range(heads):
        columns = []
        for low in range(0, chans, 16):
            largest = None
            for e in range(2):
                rows = slice((head * 2 + e) * chans + low, (head * 2 + e) * chans + low + 16)
                got = [in_ref[0, rows, :] for in_ref in in_refs[:4]] + [in_refs[4][i, rows, :] for i in range(4)]
                got = from_origins([value.astype(jnp.float32) for value in got], swap)
                outs = butterfly([got[s] * flips_in[s] for s in range(8)])
                for s in range(8):
                    magnitude = jnp.abs(outs[s])
                    largest = magnitude if largest is None else jnp.maximum(largest, magnitude)
                outs = [outs[s] * flips_out[s] for s in range(8)]
                for array, values in enumerate(to_slots(outs, swap)):
                    for slot, value in enumerate(values):
                        out_refs[array][slot, rows, :] = value.astype(jnp.bfloat16)
            columns.append(largest)
        columns.append(jnp.zeros((HAD - chans, HAD), jnp.float32))
        peak = jnp.max(jnp.concatenate(columns, axis=0).T, axis=0, keepdims=True)
        tail = jnp.where(row_id == head, peak, tail)
    tail = split_parts(tail, chans)
    for out_ref in out_refs:
        for slot in range(2):
            out_ref[slot, heads * 2 * chans :, :] = tail


def pairing_offset(core, which, index):
    factor = (index & 1) + 4 * (index >> 1)
    return factor * jnp.where(core == 0, PAIRINGS[0][which], PAIRINGS[1][which])


def spread_kernel(heads, chans, placement_ref, *refs):
    in_refs, out_refs = refs[:5], refs[5:]
    me, core = lax.axis_index("tp"), lax.axis_index("fsdp") & 1
    mine = [placement_ref[me * heads + head] for head in range(heads)]
    blocks = [(in_ref, 0) for in_ref in in_refs[:4]] + [(in_refs[4], index) for index in range(4)]
    peaks = None
    for in_ref, index in blocks:
        part = join_parts(in_ref[index, heads * 2 * chans :, :].astype(jnp.float32), chans)
        peaks = part if peaks is None else jnp.maximum(peaks, part)
    row_id = lax.broadcasted_iota(jnp.int32, (TAIL, HAD), 0)
    span = 2 * chans
    for i, out_ref in enumerate(out_refs):
        for j in range(4):
            owner = me ^ pairing_offset(core, 0, i) ^ pairing_offset(core, 1, j)
            head = 0
            for index in range(1, heads):
                head = jnp.where(mine[index] == owner, index, head)
            rows = pl.ds(pl.multiple_of(head * span, 16), span)
            for s, (in_ref, index) in enumerate(blocks):
                out_ref[j, s * span : (s + 1) * span, :] = in_ref[index, rows, :]
            peak = jnp.sum(jnp.where(row_id == head, peaks, 0.0), axis=0, keepdims=True)
            out_ref[j, 8 * span :, :] = split_parts(jnp.broadcast_to(peak, (TAIL, HAD)), chans)


def pack_kernel(owners, heads, chunk, has_past, placement_ref, *refs):
    first, chans = chunk
    peak_ref, out_ref, buffer, sems, live_ref, slot_ref = refs[-6:]
    past_ref = refs[-8] if has_past else None
    in_refs = refs[: -8 if has_past else -6]
    me, group = lax.axis_index("tp"), lax.axis_index("fsdp")
    count = 0
    for source in range(owners):
        live = 0
        for head in range(heads):
            live = jnp.where(placement_ref[source * heads + head] == me, 1, live)
        live_ref[source] = live
        slot_ref[source] = count
        count = count + live
    lane = lax.broadcasted_iota(jnp.int32, (TAIL, HAD), 1)
    copies = []
    core = group & 1
    pair = jnp.where(core == 0, 2, 6)
    offsets = (0, 1, pair, pair ^ 1, pair ^ 4, pair ^ 5, 4, 5)
    blocks, rows = [], []
    for origin in range(owners):
        i, j = origin % 4, origin // 4
        in_ref, index = (in_refs[3 + j], i) if j else (in_refs[i], 0)
        source = me ^ pairing_offset(core, 0, i) ^ pairing_offset(core, 1, j)
        live = live_ref[source] != 0
        slot = jnp.where(live, slot_ref[source], count + source - slot_ref[source])
        tail = in_ref[index, 16 * chans :, :].astype(jnp.float32)
        row = jnp.where((lane < chans) & live, join_parts(tail, chans), 0.0)
        rows.append(jnp.where(live, 1.0 / (row[:1, :] + 1e-06), 0.0))
        row = (pltpu.roll(row, first, 1) if first else row)[:1, :]
        if has_past:
            row = row + past_ref[pl.ds(slot, 1), :]
        peak_ref[pl.ds(slot, 1), :] = row
        blocks.append((in_ref, index, slot))
    rows.append(jnp.zeros((HAD - owners, HAD), jnp.float32))
    scales = jnp.concatenate(rows, axis=0).T
    for origin, (in_ref, index, slot) in enumerate(blocks):
        scale = scales[:chans, origin : origin + 1]
        for s in range(8):
            for e in range(2):
                start = (s * 2 + e) * chans
                lanes = pl.ds(pl.multiple_of(((group ^ offsets[s]) * 2 + e) * HAD, HAD), HAD)
                block = in_ref[index, start : start + chans, :]
                buffer[origin, :, lanes] = (block.astype(jnp.float32) * scale).astype(jnp.bfloat16)
        rows = out_ref.at[0, slot, first : first + chans, :]
        copies.append(pltpu.make_async_copy(buffer.at[origin], rows, sems.at[origin]))
        copies[-1].start()
    for copy in copies:
        copy.wait()


def per_device(qkv_weight, placement):
    rows_local, cols_local = qkv_weight.shape
    heads = cols_local // HEAD_DIM
    owners = lax.axis_size("tp")
    rows_a = rows_local // HAD
    params = pltpu.CompilerParams(vmem_limit_bytes=VMEM_BYTES)
    any_spec = pl.BlockSpec(memory_space=pl.ANY)
    smem_spec = pl.BlockSpec(memory_space=pltpu.SMEM)
    vmem_spec = pl.BlockSpec(memory_space=pltpu.VMEM)

    def call(kernel, name, shapes, *arrays, table=False):
        return pl.pallas_call(
            kernel,
            in_specs=[smem_spec] * table + [vmem_spec] * (len(arrays) - table),
            out_specs=[vmem_spec] * len(shapes),
            out_shape=[jax.ShapeDtypeStruct(shape + (HAD,), jnp.bfloat16) for shape in shapes],
            compiler_params=params,
            name=name,
        )(*arrays)

    widths = [2 * chans for _, chans in CHUNKS for _ in range(4)]
    turned = pl.pallas_call(
        functools.partial(local_turn_kernel, rows_a),
        grid=(heads,),
        in_specs=[pl.BlockSpec((rows_local, HEAD_DIM), lambda h: (0, h))],
        out_specs=[pl.BlockSpec((2, width, HAD), lambda h: (0, h, 0)) for width in widths],
        out_shape=[jax.ShapeDtypeStruct((2, heads * width, HAD), jnp.bfloat16) for width in widths],
        scratch_shapes=[pltpu.VMEM((rows_local, HAD), jnp.float32)],
        compiler_params=params,
        name="local_turn",
    )(qkv_weight)

    state = [turned[4 * index : 4 * index + 4] for index in range(len(CHUNKS))]
    token = None
    past = []

    def tie(arrays):
        if token is None:
            return list(arrays)
        return list(lax.optimization_barrier((list(arrays), token))[0])

    for stage, index in ORDER:
        first, chans = chunk = CHUNKS[index]
        arrays = tie(state[index])
        if stage == "start":
            state[index] = y_first(arrays)
        elif stage == "y_regroup":
            (token,) = call(y_regroup_kernel, stage, [(4,) + arrays[0].shape[1:2]], *arrays)
            state[index] = arrays + [y_second(token)]
        elif stage == "cross":
            shapes = [(2, heads * 2 * chans + TAIL)] * 4
            outs = call(functools.partial(cross_turn_kernel, heads, chans), stage, shapes, *arrays)
            token = outs[0]
            state[index] = y_first(outs)
        elif stage == "spread":
            shapes = [(4, 16 * chans + TAIL)] * 4
            kernel = functools.partial(spread_kernel, heads, chans)
            outs = call(kernel, stage, shapes, placement, *arrays, table=True)
            token = outs[0]
            state[index] = [token] + owner_hops(outs[1:], 0)
        elif stage == "regroup":
            outs = call(regroup_kernel, stage, [arrays[0].shape[:2]] * 3, *arrays)
            token = outs[0]
            state[index] = arrays + owner_hops(outs, 1)
        else:
            past = pl.pallas_call(
                functools.partial(pack_kernel, owners, heads, chunk, bool(past)),
                in_specs=[smem_spec] + [vmem_spec] * len(arrays) + ([vmem_spec, any_spec] if past else []),
                out_specs=[vmem_spec, any_spec],
                out_shape=[
                    jax.ShapeDtypeStruct((owners, HEAD_DIM), jnp.float32),
                    jax.ShapeDtypeStruct((1, owners, HEAD_DIM, rows_local), jnp.bfloat16),
                ],
                scratch_shapes=[
                    pltpu.VMEM((owners, chans, rows_local), jnp.bfloat16),
                    pltpu.SemaphoreType.DMA((owners,)),
                    pltpu.SMEM((owners,), jnp.int32),
                    pltpu.SMEM((owners,), jnp.int32),
                ],
                input_output_aliases={2 + len(arrays): 1} if past else {},
                compiler_params=params,
                name="pack",
            )(placement, *arrays, *past)
            token = past[0]
    peaks, packed = past
    return packed, peaks[None]


def solution(mesh):
    in_specs = (P("fsdp", "tp"), P())
    out_specs = (P("tp", None, None, "fsdp"), P("tp", None, None))
    return jax.shard_map(
        per_device, mesh=mesh, in_specs=in_specs, out_specs=out_specs, check_vma=False
    )
```

```python
import functools

import jax
import jax.numpy as jnp
from jax import lax
from jax.experimental import pallas as pl
from jax.experimental.pallas import tpu as pltpu
from jax.sharding import PartitionSpec as P

HEAD_DIM = 128
HAD = 128
CHUNKS = ((0, 32), (32, 48), (80, 48))
ORDER = (
    ("start", 0),
    ("start", 1),
    ("y_regroup", 0),
    ("y_regroup", 1),
    ("cross", 0),
    ("start", 2),
    ("y_regroup", 0),
    ("cross", 1),
    ("spread", 0),
    ("y_regroup", 1),
    ("regroup", 0),
    ("y_regroup", 2),
    ("spread", 1),
    ("cross", 2),
    ("pack", 0),
    ("y_regroup", 2),
    ("regroup", 1),
    ("spread", 2),
    ("pack", 1),
    ("regroup", 2),
    ("pack", 2),
)
TAIL = 16
VMEM_BYTES = 12 * 1024 * 1024
BOTH = ("fsdp", "tp")


def butterfly(values):
    values = list(values)
    half = 1
    while half < len(values):
        for low in range(len(values)):
            if not low & half:
                first, second = values[low], values[low + half]
                values[low], values[low + half] = first + second, first - second
        half *= 2
    return values


PAIRINGS = ((1, 3), (3, 1))


def hop(array, rule):
    groups, owners = lax.axis_size("fsdp"), lax.axis_size("tp")
    pairs = []
    for f in range(groups):
        for t in range(owners):
            to_f, to_t = rule(f, t)
            pairs.append((f * owners + t, to_f * owners + to_t))
    return lax.ppermute(array, BOTH, pairs)


def y_first(blocks):
    own, core, pair, both = blocks
    pair = hop(pair, lambda f, t: (f ^ 2 * PAIRINGS[f & 1][0], t))
    both = hop(both, lambda f, t: (f ^ 1 ^ 2 * PAIRINGS[1 - (f & 1)][0], t))
    core = hop(core, lambda f, t: (f ^ 1, t))
    return [own, core, pair, both]


def y_second(payload):
    return hop(payload, lambda f, t: (f ^ 2 * PAIRINGS[f & 1][1], t))


def owner_hops(blocks, which):
    out = [None] * 3
    for place in (2, 0, 1):
        factor = (1, 4, 5)[place]
        out[place] = hop(blocks[place], lambda f, t: (f, t ^ factor * PAIRINGS[f & 1][which]))
    return out


def to_slots(values, swap):
    return (
        (values[0], jnp.where(swap, values[2], values[6])),
        (values[1], jnp.where(swap, values[7], values[3])),
        (jnp.where(swap, values[6], values[2]), values[4]),
        (jnp.where(swap, values[3], values[7]), values[5]),
    )


def from_origins(values, swap):
    return (
        values[0],
        values[1],
        jnp.where(swap, values[4], values[2]),
        jnp.where(swap, values[5], values[3]),
        values[6],
        values[7],
        jnp.where(swap, values[2], values[4]),
        jnp.where(swap, values[3], values[5]),
    )


def y_regroup_kernel(*refs):
    for index, in_ref in enumerate(refs[:4]):
        refs[4][index] = in_ref[1]


def regroup_kernel(*refs):
    in_refs, out_refs = refs[:4], refs[4:]
    for slot, out_ref in enumerate(out_refs):
        for index, in_ref in enumerate(in_refs):
            out_ref[index] = in_ref[slot + 1]


def sign_of(value, bits):
    both = value & bits
    both = both ^ (both >> 2)
    both = both ^ (both >> 1)
    return (1 - 2 * (both & 1)).astype(jnp.float32)


def local_turn_kernel(rows_a, weight_ref, *refs):
    out_refs, turned = refs[:-1], refs[-1]
    group = lax.axis_index("fsdp")
    swap = group & 1 != 0
    flips = [sign_of(group, a >> 1) * (1.0 / HAD) for a in range(rows_a)]
    columns = jnp.concatenate([weight_ref[a * HAD : (a + 1) * HAD, :].T for a in range(rows_a)], axis=0)
    both = [lax.broadcasted_iota(jnp.int32, (HAD, HAD), dim) for dim in range(2)]
    both = both[0] & both[1]
    for shift in (4, 2, 1):
        both = both ^ (both >> shift)
    signs = (1 - 2 * (both & 1)).astype(jnp.float32).astype(jnp.bfloat16)
    turned[...] = jnp.dot(columns, signs, preferred_element_type=jnp.float32)
    for index, (first, chans) in enumerate(CHUNKS):
        for low in range(0, chans, 16):
            outs = []
            for a in range(rows_a):
                start = a * HEAD_DIM + first + low
                outs.append(turned[start : start + 16, :] * flips[a])
            outs = butterfly(outs)
            for e in range(2):
                row = e * chans + low
                for array, values in enumerate(to_slots(outs[e::2], swap)):
                    for slot, value in enumerate(values):
                        out_refs[4 * index + array][slot, row : row + 16, :] = value.astype(jnp.bfloat16)


def join_parts(value, chans):
    return value + pltpu.roll(value, HAD - chans, 1)


def split_parts(value, chans):
    high = value.astype(jnp.bfloat16).astype(jnp.float32)
    lane = lax.broadcasted_iota(jnp.int32, value.shape, 1)
    both = jnp.where(lane < chans, high, pltpu.roll(value - high, chans, 1))
    return jnp.where(lane < 2 * chans, both, 0.0).astype(jnp.bfloat16)


def cross_turn_kernel(heads, chans, *refs):
    in_refs, out_refs = refs[:5], refs[5:]
    group = lax.axis_index("fsdp")
    swap = group & 1 != 0
    flips_in = [sign_of(group, s) for s in range(8)]
    flips_out = [flip * sign_of(group, group) for flip in flips_in]
    row_id = lax.broadcasted_iota(jnp.int32, (TAIL, HAD), 0)
    tail = jnp.zeros((TAIL, HAD), jnp.float32)
    for head in range(heads):
        columns = []
        for low in range(0, chans, 16):
            largest = None
            for e in range(2):
                rows = slice((head * 2 + e) * chans + low, (head * 2 + e) * chans + low + 16)
                got = [in_ref[0, rows, :] for in_ref in in_refs[:4]] + [in_refs[4][i, rows, :] for i in range(4)]
                got = from_origins([value.astype(jnp.float32) for value in got], swap)
                outs = butterfly([got[s] * flips_in[s] for s in range(8)])
                for s in range(8):
                    magnitude = jnp.abs(outs[s])
                    largest = magnitude if largest is None else jnp.maximum(largest, magnitude)
                outs = [outs[s] * flips_out[s] for s in range(8)]
                for array, values in enumerate(to_slots(outs, swap)):
                    for slot, value in enumerate(values):
                        out_refs[array][slot, rows, :] = value.astype(jnp.bfloat16)
            columns.append(largest)
        columns.append(jnp.zeros((HAD - chans, HAD), jnp.float32))
        peak = jnp.max(jnp.concatenate(columns, axis=0).T, axis=0, keepdims=True)
        tail = jnp.where(row_id == head, peak, tail)
    tail = split_parts(tail, chans)
    for out_ref in out_refs:
        for slot in range(2):
            out_ref[slot, heads * 2 * chans :, :] = tail


def pairing_offset(core, which, index):
    factor = (index & 1) + 4 * (index >> 1)
    return factor * jnp.where(core == 0, PAIRINGS[0][which], PAIRINGS[1][which])


def spread_kernel(heads, chans, placement_ref, *refs):
    in_refs, out_refs = refs[:5], refs[5:]
    me, core = lax.axis_index("tp"), lax.axis_index("fsdp") & 1
    mine = [placement_ref[me * heads + head] for head in range(heads)]
    blocks = [(in_ref, 0) for in_ref in in_refs[:4]] + [(in_refs[4], index) for index in range(4)]
    peaks = None
    for in_ref, index in blocks:
        part = join_parts(in_ref[index, heads * 2 * chans :, :].astype(jnp.float32), chans)
        peaks = part if peaks is None else jnp.maximum(peaks, part)
    row_id = lax.broadcasted_iota(jnp.int32, (TAIL, HAD), 0)
    span = 2 * chans
    for i, out_ref in enumerate(out_refs):
        for j in range(4):
            owner = me ^ pairing_offset(core, 0, i) ^ pairing_offset(core, 1, j)
            head = 0
            for index in range(1, heads):
                head = jnp.where(mine[index] == owner, index, head)
            rows = pl.ds(pl.multiple_of(head * span, 16), span)
            for s, (in_ref, index) in enumerate(blocks):
                out_ref[j, s * span : (s + 1) * span, :] = in_ref[index, rows, :]
            peak = jnp.sum(jnp.where(row_id == head, peaks, 0.0), axis=0, keepdims=True)
            out_ref[j, 8 * span :, :] = split_parts(jnp.broadcast_to(peak, (TAIL, HAD)), chans)


def pack_kernel(owners, heads, chunk, has_past, placement_ref, *refs):
    first, chans = chunk
    peak_ref, out_ref, buffer, sems, live_ref, slot_ref = refs[-6:]
    past_ref = refs[-8] if has_past else None
    in_refs = refs[: -8 if has_past else -6]
    me, group = lax.axis_index("tp"), lax.axis_index("fsdp")
    count = 0
    for source in range(owners):
        live = 0
        for head in range(heads):
            live = jnp.where(placement_ref[source * heads + head] == me, 1, live)
        live_ref[source] = live
        slot_ref[source] = count
        count = count + live
    lane = lax.broadcasted_iota(jnp.int32, (TAIL, HAD), 1)
    copies = []
    core = group & 1
    pair = jnp.where(core == 0, 2, 6)
    offsets = (0, 1, pair, pair ^ 1, pair ^ 4, pair ^ 5, 4, 5)
    blocks, rows = [], []
    for origin in range(owners):
        i, j = origin % 4, origin // 4
        in_ref, index = (in_refs[3 + j], i) if j else (in_refs[i], 0)
        source = me ^ pairing_offset(core, 0, i) ^ pairing_offset(core, 1, j)
        live = live_ref[source] != 0
        slot = jnp.where(live, slot_ref[source], count + source - slot_ref[source])
        tail = in_ref[index, 16 * chans :, :].astype(jnp.float32)
        row = jnp.where((lane < chans) & live, join_parts(tail, chans), 0.0)
        rows.append(jnp.where(live, 1.0 / (row[:1, :] + 1e-06), 0.0))
        row = (pltpu.roll(row, first, 1) if first else row)[:1, :]
        if has_past:
            row = row + past_ref[pl.ds(slot, 1), :]
        peak_ref[pl.ds(slot, 1), :] = row
        blocks.append((in_ref, index, slot))
    rows.append(jnp.zeros((HAD - owners, HAD), jnp.float32))
    scales = jnp.concatenate(rows, axis=0).T
    for origin, (in_ref, index, slot) in enumerate(blocks):
        scale = scales[:chans, origin : origin + 1]
        for s in range(8):
            for e in range(2):
                start = (s * 2 + e) * chans
                lanes = pl.ds(pl.multiple_of(((group ^ offsets[s]) * 2 + e) * HAD, HAD), HAD)
                block = in_ref[index, start : start + chans, :]
                buffer[origin, :, lanes] = (block.astype(jnp.float32) * scale).astype(jnp.bfloat16)
        rows = out_ref.at[0, slot, first : first + chans, :]
        copies.append(pltpu.make_async_copy(buffer.at[origin], rows, sems.at[origin]))
        copies[-1].start()
    for copy in copies:
        copy.wait()


def per_device(qkv_weight, placement):
    rows_local, cols_local = qkv_weight.shape
    heads = cols_local // HEAD_DIM
    owners = lax.axis_size("tp")
    rows_a = rows_local // HAD
    params = pltpu.CompilerParams(vmem_limit_bytes=VMEM_BYTES)
    any_spec = pl.BlockSpec(memory_space=pl.ANY)
    smem_spec = pl.BlockSpec(memory_space=pltpu.SMEM)
    vmem_spec = pl.BlockSpec(memory_space=pltpu.VMEM)

    def call(kernel, name, shapes, *arrays, table=False):
        return pl.pallas_call(
            kernel,
            in_specs=[smem_spec] * table + [vmem_spec] * (len(arrays) - table),
            out_specs=[vmem_spec] * len(shapes),
            out_shape=[jax.ShapeDtypeStruct(shape + (HAD,), jnp.bfloat16) for shape in shapes],
            compiler_params=params,
            name=name,
        )(*arrays)

    widths = [2 * chans for _, chans in CHUNKS for _ in range(4)]
    turned = pl.pallas_call(
        functools.partial(local_turn_kernel, rows_a),
        grid=(heads,),
        in_specs=[pl.BlockSpec((rows_local, HEAD_DIM), lambda h: (0, h))],
        out_specs=[pl.BlockSpec((2, width, HAD), lambda h: (0, h, 0)) for width in widths],
        out_shape=[jax.ShapeDtypeStruct((2, heads * width, HAD), jnp.bfloat16) for width in widths],
        scratch_shapes=[pltpu.VMEM((rows_local, HAD), jnp.float32)],
        compiler_params=params,
        name="local_turn",
    )(qkv_weight)

    state = [turned[4 * index : 4 * index + 4] for index in range(len(CHUNKS))]
    token = None
    past = []

    def tie(arrays):
        if token is None:
            return list(arrays)
        return list(lax.optimization_barrier((list(arrays), token))[0])

    for stage, index in ORDER:
        first, chans = chunk = CHUNKS[index]
        arrays = tie(state[index])
        if stage == "start":
            state[index] = y_first(arrays)
        elif stage == "y_regroup":
            (token,) = call(y_regroup_kernel, stage, [(4,) + arrays[0].shape[1:2]], *arrays)
            state[index] = arrays + [y_second(token)]
        elif stage == "cross":
            shapes = [(2, heads * 2 * chans + TAIL)] * 4
            outs = call(functools.partial(cross_turn_kernel, heads, chans), stage, shapes, *arrays)
            token = outs[0]
            state[index] = y_first(outs)
        elif stage == "spread":
            shapes = [(4, 16 * chans + TAIL)] * 4
            kernel = functools.partial(spread_kernel, heads, chans)
            outs = call(kernel, stage, shapes, placement, *arrays, table=True)
            token = outs[0]
            state[index] = [token] + owner_hops(outs[1:], 0)
        elif stage == "regroup":
            outs = call(regroup_kernel, stage, [arrays[0].shape[:2]] * 3, *arrays)
            token = outs[0]
            state[index] = arrays + owner_hops(outs, 1)
        else:
            past = pl.pallas_call(
                functools.partial(pack_kernel, owners, heads, chunk, bool(past)),
                in_specs=[smem_spec] + [vmem_spec] * len(arrays) + ([vmem_spec, any_spec] if past else []),
                out_specs=[vmem_spec, any_spec],
                out_shape=[
                    jax.ShapeDtypeStruct((owners, HEAD_DIM), jnp.float32),
                    jax.ShapeDtypeStruct((1, owners, HEAD_DIM, rows_local), jnp.bfloat16),
                ],
                scratch_shapes=[
                    pltpu.VMEM((owners, chans, rows_local), jnp.bfloat16),
                    pltpu.SemaphoreType.DMA((owners,)),
                    pltpu.SMEM((owners,), jnp.int32),
                    pltpu.SMEM((owners,), jnp.int32),
                ],
                input_output_aliases={2 + len(arrays): 1} if past else {},
                compiler_params=params,
                name="pack",
            )(placement, *arrays, *past)
            token = past[0]
    peaks, packed = past
    return packed, peaks[None]


def solution(mesh):
    in_specs = (P("fsdp", "tp"), P())
    out_specs = (P("tp", None, None, "fsdp"), P("tp", None, None))
    return jax.shard_map(
        per_device, mesh=mesh, in_specs=in_specs, out_specs=out_specs, check_vma=False
    )
```

```python
import functools

import jax
import jax.numpy as jnp
from jax import lax
from jax.experimental import pallas as pl
from jax.experimental.pallas import tpu as pltpu
from jax.sharding import PartitionSpec as P

HEAD_DIM = 128
HAD = 128
CHUNKS = ((0, 32), (32, 64), (96, 32))
ORDER = (
    ("start", 0),
    ("start", 1),
    ("y_regroup", 0),
    ("y_regroup", 1),
    ("cross", 0),
    ("start", 2),
    ("y_regroup", 0),
    ("cross", 1),
    ("spread", 0),
    ("y_regroup", 2),
    ("y_regroup", 1),
    ("regroup", 0),
    ("cross", 2),
    ("spread", 1),
    ("pack", 0),
    ("y_regroup", 2),
    ("regroup", 1),
    ("spread", 2),
    ("pack", 1),
    ("regroup", 2),
    ("pack", 2),
)
TAIL = 16
VMEM_BYTES = 12 * 1024 * 1024
BOTH = ("fsdp", "tp")


def butterfly(values):
    values = list(values)
    half = 1
    while half < len(values):
        for low in range(len(values)):
            if not low & half:
                first, second = values[low], values[low + half]
                values[low], values[low + half] = first + second, first - second
        half *= 2
    return values


PAIRINGS = ((1, 3), (3, 1))


def hop(array, rule):
    groups, owners = lax.axis_size("fsdp"), lax.axis_size("tp")
    pairs = []
    for f in range(groups):
        for t in range(owners):
            to_f, to_t = rule(f, t)
            pairs.append((f * owners + t, to_f * owners + to_t))
    return lax.ppermute(array, BOTH, pairs)


def y_first(blocks):
    own, core, pair, both = blocks
    pair = hop(pair, lambda f, t: (f ^ 2 * PAIRINGS[f & 1][0], t))
    both = hop(both, lambda f, t: (f ^ 1 ^ 2 * PAIRINGS[1 - (f & 1)][0], t))
    core = hop(core, lambda f, t: (f ^ 1, t))
    return [own, core, pair, both]


def y_second(payload):
    return hop(payload, lambda f, t: (f ^ 2 * PAIRINGS[f & 1][1], t))


def owner_hops(blocks, which):
    out = [None] * 3
    for place in (2, 0, 1):
        factor = (1, 4, 5)[place]
        out[place] = hop(blocks[place], lambda f, t: (f, t ^ factor * PAIRINGS[f & 1][which]))
    return out


def to_slots(values, swap):
    return (
        (values[0], jnp.where(swap, values[2], values[6])),
        (values[1], jnp.where(swap, values[7], values[3])),
        (jnp.where(swap, values[6], values[2]), values[4]),
        (jnp.where(swap, values[3], values[7]), values[5]),
    )


def from_origins(values, swap):
    return (
        values[0],
        values[1],
        jnp.where(swap, values[4], values[2]),
        jnp.where(swap, values[5], values[3]),
        values[6],
        values[7],
        jnp.where(swap, values[2], values[4]),
        jnp.where(swap, values[3], values[5]),
    )


def y_regroup_kernel(*refs):
    for index, in_ref in enumerate(refs[:4]):
        refs[4][index] = in_ref[1]


def regroup_kernel(*refs):
    in_refs, out_refs = refs[:4], refs[4:]
    for slot, out_ref in enumerate(out_refs):
        for index, in_ref in enumerate(in_refs):
            out_ref[index] = in_ref[slot + 1]


def sign_of(value, bits):
    both = value & bits
    both = both ^ (both >> 2)
    both = both ^ (both >> 1)
    return (1 - 2 * (both & 1)).astype(jnp.float32)


def local_turn_kernel(rows_a, weight_ref, *refs):
    out_refs, turned = refs[:-1], refs[-1]
    group = lax.axis_index("fsdp")
    swap = group & 1 != 0
    flips = [sign_of(group, a >> 1) * (1.0 / HAD) for a in range(rows_a)]
    columns = jnp.concatenate([weight_ref[a * HAD : (a + 1) * HAD, :].T for a in range(rows_a)], axis=0)
    both = [lax.broadcasted_iota(jnp.int32, (HAD, HAD), dim) for dim in range(2)]
    both = both[0] & both[1]
    for shift in (4, 2, 1):
        both = both ^ (both >> shift)
    signs = (1 - 2 * (both & 1)).astype(jnp.float32).astype(jnp.bfloat16)
    turned[...] = jnp.dot(columns, signs, preferred_element_type=jnp.float32)
    for index, (first, chans) in enumerate(CHUNKS):
        for low in range(0, chans, 16):
            outs = []
            for a in range(rows_a):
                start = a * HEAD_DIM + first + low
                outs.append(turned[start : start + 16, :] * flips[a])
            outs = butterfly(outs)
            for e in range(2):
                row = e * chans + low
                for array, values in enumerate(to_slots(outs[e::2], swap)):
                    for slot, value in enumerate(values):
                        out_refs[4 * index + array][slot, row : row + 16, :] = value.astype(jnp.bfloat16)


def join_parts(value, chans):
    return value + pltpu.roll(value, HAD - chans, 1)


def split_parts(value, chans):
    high = value.astype(jnp.bfloat16).astype(jnp.float32)
    lane = lax.broadcasted_iota(jnp.int32, value.shape, 1)
    both = jnp.where(lane < chans, high, pltpu.roll(value - high, chans, 1))
    return jnp.where(lane < 2 * chans, both, 0.0).astype(jnp.bfloat16)


def cross_turn_kernel(heads, chans, *refs):
    in_refs, out_refs = refs[:5], refs[5:]
    group = lax.axis_index("fsdp")
    swap = group & 1 != 0
    flips_in = [sign_of(group, s) for s in range(8)]
    flips_out = [flip * sign_of(group, group) for flip in flips_in]
    row_id = lax.broadcasted_iota(jnp.int32, (TAIL, HAD), 0)
    tail = jnp.zeros((TAIL, HAD), jnp.float32)
    for head in range(heads):
        columns = []
        for low in range(0, chans, 16):
            largest = None
            for e in range(2):
                rows = slice((head * 2 + e) * chans + low, (head * 2 + e) * chans + low + 16)
                got = [in_ref[0, rows, :] for in_ref in in_refs[:4]] + [in_refs[4][i, rows, :] for i in range(4)]
                got = from_origins([value.astype(jnp.float32) for value in got], swap)
                outs = butterfly([got[s] * flips_in[s] for s in range(8)])
                for s in range(8):
                    magnitude = jnp.abs(outs[s])
                    largest = magnitude if largest is None else jnp.maximum(largest, magnitude)
                outs = [outs[s] * flips_out[s] for s in range(8)]
                for array, values in enumerate(to_slots(outs, swap)):
                    for slot, value in enumerate(values):
                        out_refs[array][slot, rows, :] = value.astype(jnp.bfloat16)
            columns.append(largest)
        columns.append(jnp.zeros((HAD - chans, HAD), jnp.float32))
        peak = jnp.max(jnp.concatenate(columns, axis=0).T, axis=0, keepdims=True)
        tail = jnp.where(row_id == head, peak, tail)
    tail = split_parts(tail, chans)
    for out_ref in out_refs:
        for slot in range(2):
            out_ref[slot, heads * 2 * chans :, :] = tail


def pairing_offset(core, which, index):
    factor = (index & 1) + 4 * (index >> 1)
    return factor * jnp.where(core == 0, PAIRINGS[0][which], PAIRINGS[1][which])


def spread_kernel(heads, chans, placement_ref, *refs):
    in_refs, out_refs = refs[:5], refs[5:]
    me, core = lax.axis_index("tp"), lax.axis_index("fsdp") & 1
    mine = [placement_ref[me * heads + head] for head in range(heads)]
    blocks = [(in_ref, 0) for in_ref in in_refs[:4]] + [(in_refs[4], index) for index in range(4)]
    peaks = None
    for in_ref, index in blocks:
        part = join_parts(in_ref[index, heads * 2 * chans :, :].astype(jnp.float32), chans)
        peaks = part if peaks is None else jnp.maximum(peaks, part)
    row_id = lax.broadcasted_iota(jnp.int32, (TAIL, HAD), 0)
    span = 2 * chans
    for i, out_ref in enumerate(out_refs):
        for j in range(4):
            owner = me ^ pairing_offset(core, 0, i) ^ pairing_offset(core, 1, j)
            head = 0
            for index in range(1, heads):
                head = jnp.where(mine[index] == owner, index, head)
            rows = pl.ds(pl.multiple_of(head * span, 16), span)
            for s, (in_ref, index) in enumerate(blocks):
                out_ref[j, s * span : (s + 1) * span, :] = in_ref[index, rows, :]
            peak = jnp.sum(jnp.where(row_id == head, peaks, 0.0), axis=0, keepdims=True)
            out_ref[j, 8 * span :, :] = split_parts(jnp.broadcast_to(peak, (TAIL, HAD)), chans)


def pack_kernel(owners, heads, chunk, has_past, placement_ref, *refs):
    first, chans = chunk
    peak_ref, out_ref, buffer, sems, live_ref, slot_ref = refs[-6:]
    past_ref = refs[-8] if has_past else None
    in_refs = refs[: -8 if has_past else -6]
    me, group = lax.axis_index("tp"), lax.axis_index("fsdp")
    count = 0
    for source in range(owners):
        live = 0
        for head in range(heads):
            live = jnp.where(placement_ref[source * heads + head] == me, 1, live)
        live_ref[source] = live
        slot_ref[source] = count
        count = count + live
    lane = lax.broadcasted_iota(jnp.int32, (TAIL, HAD), 1)
    copies = []
    core = group & 1
    pair = jnp.where(core == 0, 2, 6)
    offsets = (0, 1, pair, pair ^ 1, pair ^ 4, pair ^ 5, 4, 5)
    blocks, rows = [], []
    for origin in range(owners):
        i, j = origin % 4, origin // 4
        in_ref, index = (in_refs[3 + j], i) if j else (in_refs[i], 0)
        source = me ^ pairing_offset(core, 0, i) ^ pairing_offset(core, 1, j)
        live = live_ref[source] != 0
        slot = jnp.where(live, slot_ref[source], count + source - slot_ref[source])
        tail = in_ref[index, 16 * chans :, :].astype(jnp.float32)
        row = jnp.where((lane < chans) & live, join_parts(tail, chans), 0.0)
        rows.append(jnp.where(live, 1.0 / (row[:1, :] + 1e-06), 0.0))
        row = (pltpu.roll(row, first, 1) if first else row)[:1, :]
        if has_past:
            row = row + past_ref[pl.ds(slot, 1), :]
        peak_ref[pl.ds(slot, 1), :] = row
        blocks.append((in_ref, index, slot))
    rows.append(jnp.zeros((HAD - owners, HAD), jnp.float32))
    scales = jnp.concatenate(rows, axis=0).T
    for origin, (in_ref, index, slot) in enumerate(blocks):
        scale = scales[:chans, origin : origin + 1]
        for s in range(8):
            for e in range(2):
                start = (s * 2 + e) * chans
                lanes = pl.ds(pl.multiple_of(((group ^ offsets[s]) * 2 + e) * HAD, HAD), HAD)
                block = in_ref[index, start : start + chans, :]
                buffer[origin, :, lanes] = (block.astype(jnp.float32) * scale).astype(jnp.bfloat16)
        rows = out_ref.at[0, slot, first : first + chans, :]
        copies.append(pltpu.make_async_copy(buffer.at[origin], rows, sems.at[origin]))
        copies[-1].start()
    for copy in copies:
        copy.wait()


def per_device(qkv_weight, placement):
    rows_local, cols_local = qkv_weight.shape
    heads = cols_local // HEAD_DIM
    owners = lax.axis_size("tp")
    rows_a = rows_local // HAD
    params = pltpu.CompilerParams(vmem_limit_bytes=VMEM_BYTES)
    any_spec = pl.BlockSpec(memory_space=pl.ANY)
    smem_spec = pl.BlockSpec(memory_space=pltpu.SMEM)
    vmem_spec = pl.BlockSpec(memory_space=pltpu.VMEM)

    def call(kernel, name, shapes, *arrays, table=False):
        return pl.pallas_call(
            kernel,
            in_specs=[smem_spec] * table + [vmem_spec] * (len(arrays) - table),
            out_specs=[vmem_spec] * len(shapes),
            out_shape=[jax.ShapeDtypeStruct(shape + (HAD,), jnp.bfloat16) for shape in shapes],
            compiler_params=params,
            name=name,
        )(*arrays)

    widths = [2 * chans for _, chans in CHUNKS for _ in range(4)]
    turned = pl.pallas_call(
        functools.partial(local_turn_kernel, rows_a),
        grid=(heads,),
        in_specs=[pl.BlockSpec((rows_local, HEAD_DIM), lambda h: (0, h))],
        out_specs=[pl.BlockSpec((2, width, HAD), lambda h: (0, h, 0)) for width in widths],
        out_shape=[jax.ShapeDtypeStruct((2, heads * width, HAD), jnp.bfloat16) for width in widths],
        scratch_shapes=[pltpu.VMEM((rows_local, HAD), jnp.float32)],
        compiler_params=params,
        name="local_turn",
    )(qkv_weight)

    state = [turned[4 * index : 4 * index + 4] for index in range(len(CHUNKS))]
    token = None
    past = []

    def tie(arrays):
        if token is None:
            return list(arrays)
        return list(lax.optimization_barrier((list(arrays), token))[0])

    for stage, index in ORDER:
        first, chans = chunk = CHUNKS[index]
        arrays = tie(state[index])
        if stage == "start":
            state[index] = y_first(arrays)
        elif stage == "y_regroup":
            (token,) = call(y_regroup_kernel, stage, [(4,) + arrays[0].shape[1:2]], *arrays)
            state[index] = arrays + [y_second(token)]
        elif stage == "cross":
            shapes = [(2, heads * 2 * chans + TAIL)] * 4
            outs = call(functools.partial(cross_turn_kernel, heads, chans), stage, shapes, *arrays)
            token = outs[0]
            state[index] = y_first(outs)
        elif stage == "spread":
            shapes = [(4, 16 * chans + TAIL)] * 4
            kernel = functools.partial(spread_kernel, heads, chans)
            outs = call(kernel, stage, shapes, placement, *arrays, table=True)
            token = outs[0]
            state[index] = [token] + owner_hops(outs[1:], 0)
        elif stage == "regroup":
            outs = call(regroup_kernel, stage, [arrays[0].shape[:2]] * 3, *arrays)
            token = outs[0]
            state[index] = arrays + owner_hops(outs, 1)
        else:
            past = pl.pallas_call(
                functools.partial(pack_kernel, owners, heads, chunk, bool(past)),
                in_specs=[smem_spec] + [vmem_spec] * len(arrays) + ([vmem_spec, any_spec] if past else []),
                out_specs=[vmem_spec, any_spec],
                out_shape=[
                    jax.ShapeDtypeStruct((owners, HEAD_DIM), jnp.float32),
                    jax.ShapeDtypeStruct((1, owners, HEAD_DIM, rows_local), jnp.bfloat16),
                ],
                scratch_shapes=[
                    pltpu.VMEM((owners, chans, rows_local), jnp.bfloat16),
                    pltpu.SemaphoreType.DMA((owners,)),
                    pltpu.SMEM((owners,), jnp.int32),
                    pltpu.SMEM((owners,), jnp.int32),
                ],
                input_output_aliases={2 + len(arrays): 1} if past else {},
                compiler_params=params,
                name="pack",
            )(placement, *arrays, *past)
            token = past[0]
    peaks, packed = past
    return packed, peaks[None]


def solution(mesh):
    in_specs = (P("fsdp", "tp"), P())
    out_specs = (P("tp", None, None, "fsdp"), P("tp", None, None))
    return jax.shard_map(
        per_device, mesh=mesh, in_specs=in_specs, out_specs=out_specs, check_vma=False
    )
```
